32 devices in a mesh: dp: 16 (over z, y, x), rep: 2 (over core).
Axes of the slice: x: 2, y: 2, z: 4, core: 2. Of those that a mesh axis runs over, the one named last changes fastest.
Arguments:
- language_in: bfloat16 [64, 128, 768], P(('dp', 'rep')), may hold values from -6 to 6
- vision_in: bfloat16 [64, 128, 768], P(('dp', 'rep')), may hold values from -6 to 6
- language_count: int32 [64], P(('dp', 'rep')), may hold values from 5 to 128, as said below
- vision_count: int32 [64], P(('dp', 'rep')), may hold values from 5 to 128, as said below
- cross_qkv: bfloat16 [2, 3, 768, 768], P(None, None, 'dp'), may hold values from -0.21875 to 0.21875
- cross_proj: bfloat16 [2, 768, 768], P(None, 'dp'), may hold values from -1.25 to 1.25
- cross_bias: bfloat16 [2, 3, 768], P(None, None, 'dp'), may hold values from -4 to 4
- norm_gain: bfloat16 [2, 3, 768], P(None, None, 'dp'), may hold values from 0.5 to 1.5
- norm_bias: bfloat16 [2, 3, 768], P(None, None, 'dp'), may hold values from -4 to 4
- self_qkv: bfloat16 [2, 3, 768, 768], P(None, None, 'dp'), may hold values from -0.21875 to 0.21875
- self_proj: bfloat16 [2, 768, 768], P(None, 'dp'), may hold values from -1.25 to 1.25
- self_bias: bfloat16 [2, 3, 768], P(None, None, 'dp'), may hold values from -4 to 4
- ffn_in: bfloat16 [2, 768, 3072], P(None, 'dp'), may hold values from -0.21875 to 0.21875
- ffn_in_bias: bfloat16 [2, 3072], P(None, 'dp'), may hold values from -4 to 4
- ffn_out: bfloat16 [2, 3072, 768], P(None, 'dp'), may hold values from -0.109375 to 0.109375
- ffn_out_bias: bfloat16 [2, 768], P(None, 'dp'), may hold values from -4 to 4
- gate_weight: bfloat16 [2, 768, 768], P(None, 'dp'), may hold values from -0.15625 to 0.15625
- gate_bias: bfloat16 [768], P('dp'), may hold values from -6 to 6
- cotangent: bfloat16 [64, 128, 768], P(('dp', 'rep')), may hold values from -6 to 6
Outputs:
- united: bfloat16 [64, 128, 768], P(('dp', 'rep'))
- grad_language: bfloat16 [64, 128, 768], P(('dp', 'rep'))
- grad_vision: bfloat16 [64, 128, 768], P(('dp', 'rep'))
- grad_cross_qkv: float32 [2, 3, 768, 768], P(None, None, 'dp')
- grad_cross_proj: float32 [2, 768, 768], P(None, 'dp')
- grad_cross_bias: float32 [2, 3, 768], P(None, None, 'dp')
- grad_norm_gain: float32 [2, 3, 768], P(None, None, 'dp')
- grad_norm_bias: float32 [2, 3, 768], P(None, None, 'dp')
- grad_self_qkv: float32 [2, 3, 768, 768], P(None, None, 'dp')
- grad_self_proj: float32 [2, 768, 768], P(None, 'dp')
- grad_self_bias: float32 [2, 3, 768], P(None, None, 'dp')
- grad_ffn_in: float32 [2, 768, 3072], P(None, 'dp')
- grad_ffn_in_bias: float32 [2, 3072], P(None, 'dp')
- grad_ffn_out: float32 [2, 3072, 768], P(None, 'dp')
- grad_ffn_out_bias: float32 [2, 768], P(None, 'dp')
- grad_gate_weight: float32 [2, 768, 768], P(None, 'dp')
- grad_gate_bias: float32 [768], P('dp')
The draws below stay inside these ranges and needn't reach their ends.
Inputs may be any that keep to these rules, and one draw needn't show every extreme that they name: The real language regions of a page are its first language_count slots. The real vision regions of a page are its first vision_count slots.
All inputs are finite; a program needn't handle non-finite values.
Results may differ from the reference program's by a relative error of at most 0.024.
Values may be sent and summed in bfloat16 or wider, within the bound.
No kernel may reach another device: no remote copies, remote signals or barrier semaphores. Data moves between devices by JAX's collectives and lax.ppermute only.
A program may use at most 256 MiB of HBM per device.

```python
import math
import jax
import jax.numpy as jnp
from jax import lax

D = 768
HEADS = 12
HEAD = 64
FF = 3072
SLOTS = 128
PAGES = 64


def count_draw(key):
    first_key, second_key = jax.random.split(key)
    counts = jax.random.randint(first_key, (PAGES,), 5, SLOTS + 1)
    chosen = jax.random.permutation(second_key, PAGES)
    counts = counts.at[chosen[0]].set(SLOTS)
    counts = counts.at[chosen[1]].set(5)
    return counts.astype(jnp.int32)


def draw_language_count(key, part):
    key = jax.random.fold_in(key, 1)
    return count_draw(key)


def draw_vision_count(key, part):
    key = jax.random.fold_in(key, 2)
    return count_draw(key)


def strengthened(result, rng, source, target, blocks, factor):
    owner, partner = [(jnp.arange(result.shape[dim]) // (result.shape[dim] // blocks)).reshape([-1 if axis == dim else 1 for axis in range(result.ndim)]) for dim in (source, target)]
    chosen = jax.random.permutation(rng, blocks)[partner]
    strong = (owner == chosen) | (owner == (partner + blocks // 2) % blocks)
    return jnp.where(strong, factor * result, result)


def levels(stream_key, shape, shards, low, top_value):
    factor_of = 1.0
    for axis_at, parts in shards:
        heights = jax.random.uniform(jax.random.fold_in(jax.random.fold_in(stream_key, 6), axis_at), (parts,), jnp.float32, low / len(shards), top_value / len(shards))
        factor_of = factor_of * jnp.repeat(jnp.exp(heights), shape[axis_at] // parts).reshape((-1,) + (1,) * (len(shape) - 1 - axis_at))
    return factor_of


def bell_draw(rng, extent, deviation, reach, cuts=(), dtype=jnp.bfloat16):
    array = deviation * jax.random.normal(rng, extent, jnp.float32)
    if cuts:
        array = array * levels(rng, extent, cuts, -0.22, 0.18)
    return jnp.clip(array, -reach, reach).astype(dtype)


def heavy_noise(stream_key, shape, spread, most, shards, heavy, held_as=jnp.bfloat16):
    values = spread * jax.random.normal(stream_key, shape, jnp.float32)
    if shards:
        values = values * levels(stream_key, shape, shards, -0.22, 0.18)
    return jnp.clip(strengthened(values, jax.random.fold_in(stream_key, 3), *heavy), -most, most).astype(held_as)


def setup_inputs(seed: int = 0) -> dict:
    key_list = jax.random.split(jax.random.key(seed), 20)
    language_in = heavy_noise(key_list[0], (PAGES, SLOTS, D), 1.0, 6.0, ((0, 32),), (0, 2, 32, 2.75))
    vision_in = heavy_noise(key_list[1], (PAGES, SLOTS, D), 1.0, 6.0, ((0, 32),), (0, 2, 32, 2.75))
    language_count = draw_language_count(jax.random.fold_in(key_list[19], 71), 0)
    vision_count = draw_vision_count(jax.random.fold_in(key_list[19], 71), 0)
    cross_qkv = bell_draw(key_list[4], (2, 3, D, D), D ** -0.5, 0.21875, ((2, 16),))
    cross_proj = bell_draw(key_list[5], (2, D, D), (D // 32) ** -0.5, 1.25, ((1, 16),))
    cross_bias = bell_draw(key_list[6], (2, 3, D), 0.3, 4.0, ((2, 16),))
    norm_gain = jnp.clip(1.0 + 0.1 * jax.random.normal(key_list[7], (2, 3, D), jnp.float32), 0.5, 1.5).astype(jnp.bfloat16)
    norm_bias = bell_draw(key_list[8], (2, 3, D), 0.3, 4.0, ((2, 16),))
    self_qkv = bell_draw(key_list[9], (2, 3, D, D), D ** -0.5, 0.21875, ((2, 16),))
    self_proj = bell_draw(key_list[10], (2, D, D), (D // 32) ** -0.5, 1.25, ((1, 16),))
    self_bias = bell_draw(key_list[11], (2, 3, D), 0.3, 4.0, ((2, 16),))
    ffn_in = bell_draw(key_list[12], (2, D, FF), D ** -0.5, 0.21875, ((1, 16),))
    ffn_in_bias = bell_draw(key_list[13], (2, FF), 0.3, 4.0, ((1, 16),))
    ffn_out = bell_draw(key_list[14], (2, FF, D), FF ** -0.5, 0.109375, ((1, 16),))
    ffn_out_bias = bell_draw(key_list[15], (2, D), 0.3, 4.0, ((1, 16),))
    gate_weight = bell_draw(key_list[16], (2, D, D), (2 * D) ** -0.5, 0.15625, ((1, 16),))
    gate_bias = bell_draw(key_list[17], (D,), 0.5, 6.0, ((0, 16),))
    cotangent = heavy_noise(key_list[18], (PAGES, SLOTS, D), 1.0, 6.0, ((0, 32),), (0, 2, 32, 2.75))
    return dict(language_in=language_in, vision_in=vision_in, language_count=language_count, vision_count=vision_count, cross_qkv=cross_qkv, cross_proj=cross_proj, cross_bias=cross_bias, norm_gain=norm_gain, norm_bias=norm_bias, self_qkv=self_qkv, self_proj=self_proj, self_bias=self_bias, ffn_in=ffn_in, ffn_in_bias=ffn_in_bias, ffn_out=ffn_out, ffn_out_bias=ffn_out_bias, gate_weight=gate_weight, gate_bias=gate_bias, cotangent=cotangent)


exact_mode = lax.Precision.HIGHEST
norm_epsilon = 1e-05

@jax.custom_vjp
def low(v):
    return lax.optimization_barrier(v.astype(jnp.bfloat16)).astype(jnp.float32)

@jax.custom_vjp
def low_back(v):
    return v

def low_keep(v):
    return (low(v), None)

def low_pass(kept, grad):
    return (grad,)

def back_keep(v):
    return (v, None)

def back_low(kept, grad):
    return (low(grad),)
low.defvjp(low_keep, low_pass)
low_back.defvjp(back_keep, back_low)

def project(values, weight):
    return jnp.einsum('sgnd,sde->sgne', values, weight, precision=exact_mode)

def rounded(values):
    return low_back(low(values))

def widened(bias):
    return bias[:, None, None, :]

def layer_norm(values, scale_row, shift_row):
    mean_row = lax.optimization_barrier(jnp.mean(values, axis=-1, keepdims=True))
    centred = values - mean_row
    variance = lax.optimization_barrier(jnp.mean(centred * centred, axis=-1, keepdims=True))
    return centred * lax.rsqrt(variance + norm_epsilon) * widened(scale_row) + widened(shift_row)

def gelu_tanh(values):
    return 0.5 * values * (1.0 + jnp.tanh(0.7978845608028654 * (values + 0.044715 * values * values * values)))

def attention(queries, keys, values, counts):
    layout = queries.shape
    split_q = queries.reshape(layout[:3] + (HEADS, HEAD))
    split_k = keys.reshape(layout[:3] + (HEADS, HEAD))
    split_v = values.reshape(layout[:3] + (HEADS, HEAD))
    scores = low_back(jnp.einsum('sgnhk,sgmhk->sghnm', split_q, split_k, precision=exact_mode) * HEAD ** (-0.5))
    valid_keys = jnp.arange(layout[2])[None, None, None, None, :] < counts[:, :, None, None, None]
    scores = jnp.where(valid_keys, scores, -1000000000.0)
    peak_score = lax.optimization_barrier(jnp.max(scores, axis=-1, keepdims=True))
    exponent = jnp.exp(scores - peak_score)
    soft_weights = low(exponent / lax.optimization_barrier(jnp.sum(exponent, axis=-1, keepdims=True)))
    mixed_heads = jnp.einsum('sghnm,sgmhk->sgnhk', soft_weights, split_v, precision=exact_mode)
    return rounded(mixed_heads.reshape(layout))

def attention_block(source, others, counts, weights, biases, projection):
    queries = rounded(project(source, weights[:, 0]) + widened(biases[:, 0]))
    keys = rounded(project(others, weights[:, 1]))
    values = rounded(project(others, weights[:, 2]) + widened(biases[:, 1]))
    mixed = attention(queries, keys, values, counts)
    return low_back(project(mixed, projection) + widened(biases[:, 2]))

def group_forward(params, language, vision, language_counts, vision_counts):
    cross_qkv, cross_proj, cross_bias, norm_gain, norm_bias, self_qkv, self_proj, self_bias, ffn_in, ffn_in_bias, ffn_out, ffn_out_bias, gate_weight, gate_bias = params
    inputs = jnp.stack([language, vision])
    counts = jnp.stack([language_counts, vision_counts])
    cross_out = attention_block(inputs, inputs[::-1], counts[::-1], cross_qkv, cross_bias, cross_proj)
    first_norm = layer_norm(inputs + cross_out, norm_gain[:, 0], norm_bias[:, 0])
    first_low = low(first_norm)
    inner_out = attention_block(first_low, first_low, counts, self_qkv, self_bias, self_proj)
    second = layer_norm(first_norm + inner_out, norm_gain[:, 1], norm_bias[:, 1])
    hidden = low_back(project(low(second), ffn_in) + widened(ffn_in_bias))
    active = gelu_tanh(hidden)
    branch = low_back(project(low(active), ffn_out) + widened(ffn_out_bias))
    third_norm = layer_norm(second + branch, norm_gain[:, 2], norm_bias[:, 2])
    logits = low_back(jnp.einsum('sgnd,sde->gne', low(third_norm), gate_weight, precision=exact_mode) + gate_bias)
    mixing = 1.0 / (1.0 + jnp.exp(-logits))
    return mixing * third_norm[0] + (1.0 - mixing) * third_norm[1]

def reference(language_in, vision_in, language_count, vision_count, cross_qkv, cross_proj, cross_bias, norm_gain, norm_bias, self_qkv, self_proj, self_bias, ffn_in, ffn_in_bias, ffn_out, ffn_out_bias, gate_weight, gate_bias, cotangent):
    params = tuple((weight.astype(jnp.float32) for weight in (cross_qkv, cross_proj, cross_bias, norm_gain, norm_bias, self_qkv, self_proj, self_bias, ffn_in, ffn_in_bias, ffn_out, ffn_out_bias, gate_weight, gate_bias)))
    group_size = math.gcd(PAGES, 16)
    groups = PAGES // group_size

    def grouped(values):
        return values.reshape((groups, group_size) + values.shape[1:])

    def ungrouped(values):
        return values.reshape((PAGES,) + values.shape[2:])
    language_counts = grouped(language_count)
    vision_counts = grouped(vision_count)

    def whole_layer(weights, language, vision):

        def one_group(pieces):
            return jax.checkpoint(group_forward)(weights, pieces[0], pieces[1], pieces[2], pieces[3])
        return lax.map(one_group, (language, vision, language_counts, vision_counts))
    united_out, pullback = jax.vjp(whole_layer, params, grouped(language_in.astype(jnp.float32)), grouped(vision_in.astype(jnp.float32)))
    weight_grads, grad_language, grad_vision = pullback(grouped(cotangent.astype(jnp.float32)))
    return (ungrouped(united_out).astype(jnp.bfloat16), ungrouped(grad_language).astype(jnp.bfloat16), ungrouped(grad_vision).astype(jnp.bfloat16), weight_grads[0], weight_grads[1], weight_grads[2], weight_grads[3], weight_grads[4], weight_grads[5], weight_grads[6], weight_grads[7], weight_grads[8], weight_grads[9], weight_grads[10], weight_grads[11], weight_grads[12], weight_grads[13])
```

```python
import functools

import jax
import jax.numpy as jnp
from jax import lax
from jax.experimental import pallas as pl
from jax.experimental.pallas import tpu as pltpu
from jax.sharding import PartitionSpec as P

HEADS = 12
HEAD = 64
norm_epsilon = 1e-05
bf16 = jnp.bfloat16
f32 = jnp.float32
AXES = ("dp", "rep")
TILE = 256
VMEM_LIMIT = 56 << 20
ANY = pl.BlockSpec(memory_space=pl.ANY)
VMEM = pl.BlockSpec(memory_space=pltpu.VMEM)
SMEM = pl.BlockSpec(memory_space=pltpu.SMEM)


class Grid:
    def __init__(self, mesh):
        self.n = mesh.shape["dp"]
        self.r = mesh.shape["rep"]
        self.high = self.n >> 1
        self.partner = self.n >> 2
        self.groups = [0, self.partner, self.high, self.high | self.partner]
        low = []
        bit = 1
        while bit < self.partner:
            low.append(bit)
            bit *= 2
        self.orders = [low, low[::-1]]

    def across(self, values, mask):
        pairs = [
            (d * self.r + c, (d ^ mask) * self.r + c) for d in range(self.n) for c in range(self.r)
        ]
        return lax.ppermute(values, AXES, pairs)

    def swap_cores(self, values):
        pairs = [
            (d * self.r + c, d * self.r + (c ^ 1)) for d in range(self.n) for c in range(self.r)
        ]
        return lax.ppermute(values, AXES, pairs)

    def piece_masks(self, stream):
        masks = [0]
        for bit in self.orders[stream]:
            masks = masks + [m ^ bit for m in masks]
        return masks


def call(kernel, outs, ins, specs, out_specs, scratch=(), flops=0, moved=0):
    return pl.pallas_call(
        kernel,
        out_shape=[jax.ShapeDtypeStruct(shape, dtype) for shape, dtype in outs],
        in_specs=specs,
        out_specs=out_specs,
        scratch_shapes=list(scratch),
        compiler_params=pltpu.CompilerParams(vmem_limit_bytes=VMEM_LIMIT),
        cost_estimate=pl.CostEstimate(flops=flops, bytes_accessed=moved, transcendentals=0),
    )(*ins)


def regroup_kernel(*refs):
    sources, outs = refs[:4], refs[4:]
    for k, source in enumerate(sources):
        for j, out in enumerate(outs):
            out[k] = source[j]


def regroup(sources):
    shape = sources[0].shape
    if shape[1] % 16:
        stacked = jnp.stack(sources, 1)
        return [stacked[0], stacked[1]]
    return call(
        regroup_kernel,
        [((4,) + shape[1:], bf16)] * 2,
        sources,
        [VMEM] * 4,
        [VMEM] * 2,
        moved=16 * shape[1] * shape[2] * 2,
    )


def place_kernel(grid, info_ref, *refs):
    sources, out_ref, sem = refs[:-2], refs[-2], refs[-1]
    count = len(sources) // 2
    me = info_ref[2]
    for j in range(2):
        masks = grid.piece_masks(j)
        for q in range(count):
            for g, group in enumerate(grid.groups):
                target = jnp.bitwise_xor(me, masks[q] ^ group)
                pltpu.make_async_copy(
                    sources[j * count + q].at[g], out_ref.at[j, target], sem
                ).start()
    pltpu.make_async_copy(out_ref, out_ref, sem).wait()


def place(grid, info, pieces):
    rows, width = pieces[0][0].shape[1:]
    if rows % 16:
        result = []
        for j in range(2):
            masks = [m ^ g for m in grid.piece_masks(j) for g in grid.groups]
            at = [masks.index(i) for i in range(grid.n)]
            order = jnp.take(jnp.array(at), jnp.arange(grid.n) ^ info[2])
            result.append(jnp.take(jnp.concatenate(pieces[j], 0), order, axis=0))
        return jnp.stack(result)
    sources = pieces[0] + pieces[1]
    return call(
        functools.partial(place_kernel, grid),
        [((2, grid.n, rows, width), bf16)],
        [info] + sources,
        [SMEM] + [ANY] * len(sources),
        [VMEM],
        [pltpu.SemaphoreType.DMA],
        moved=4 * grid.n * rows * width * 2,
    )[0]


def gather_round(grid, info, mine, theirs):
    bufs = regroup(
        [
            mine,
            grid.across(theirs, grid.groups[1]),
            grid.across(theirs, grid.groups[2]),
            grid.across(mine, grid.groups[3]),
        ]
    )
    pieces = []
    for j in range(2):
        held = [bufs[j]]
        for bit in grid.orders[j]:
            held = held + [grid.across(piece, bit) for piece in held]
            if len(grid.orders[j]) > 2:
                held = [jnp.concatenate(held, 0)]
        if len(grid.orders[j]) > 2:
            held = [held[0][4 * q : 4 * q + 4] for q in range(grid.n // 4)]
        pieces.append(held)
    own = place(grid, info, pieces)
    return own, grid.swap_cores(own)


def split_kernel(grid, info_ref, keep, received, *outs):
    count = len(outs) // 2
    me = info_ref[2]
    for j in range(2):
        masks = grid.piece_masks(j)
        for q in range(count):
            for g, group in enumerate(grid.groups):
                source = jnp.bitwise_xor(me, masks[q] ^ group)
                total = keep[j, source].astype(f32) + received[j, source].astype(f32)
                outs[j * count + q][g] = total.astype(bf16)


def split(grid, info, keep, received):
    n, rows, width = keep.shape[1:]
    count = n // 4
    if rows % 16:
        total = (keep.astype(f32) + received.astype(f32)).astype(bf16)
        pieces = []
        for j in range(2):
            masks = jnp.array([m ^ g for m in grid.piece_masks(j) for g in grid.groups])
            by_slot = jnp.take(total[j], masks ^ info[2], axis=0)
            pieces.append([by_slot[4 * q : 4 * q + 4] for q in range(count)])
        return pieces
    outs = call(
        functools.partial(split_kernel, grid),
        [((4, rows, width), bf16)] * (2 * count),
        [info, keep, received],
        [SMEM, VMEM, VMEM],
        [VMEM] * (2 * count),
        moved=6 * n * rows * width * 2,
    )
    return [outs[:count], outs[count:]]


def added(a, b):
    return (a.astype(f32) + b.astype(f32)).astype(bf16)


def scatter_round(grid, info, keep, send):
    pieces = split(grid, info, keep, grid.swap_cores(send))
    owned = []
    for j in range(2):
        held = pieces[j]
        for bit in reversed(grid.orders[j]):
            half = len(held) // 2
            if len(grid.orders[j]) > 2:
                received = grid.across(jnp.concatenate(held[half:], 0), bit)
                received = [received[4 * q : 4 * q + 4] for q in range(half)]
            else:
                received = [grid.across(piece, bit) for piece in held[half:]]
            held = [added(a, b) for a, b in zip(held[:half], received, strict=True)]
        owned.append(held[0])
    stacked = jnp.stack(owned)
    near = stacked[:, 0].astype(f32) + grid.across(stacked[:, 3], grid.groups[3]).astype(f32)
    far = grid.across(stacked[:, 1], grid.groups[1]).astype(f32) + grid.across(
        stacked[:, 2], grid.groups[2]
    ).astype(f32)
    return near, far


def nn(a, b):
    return lax.dot_general(a, b, (((1,), (0,)), ((), ())), preferred_element_type=f32)


def nt(a, b):
    return lax.dot_general(a, b, (((1,), (1,)), ((), ())), preferred_element_type=f32)


def tn(a, b):
    return lax.dot_general(a, b, (((0,), (0,)), ((), ())), preferred_element_type=f32)


def tiles(extent, body, size=TILE):
    def step(i, carry):
        body(pl.ds(pl.multiple_of(i * size, size), size))
        return carry

    lax.fori_loop(0, extent // size, step, 0)


def load_blocks(core, own, swapped, blocks, sem):
    count = own.shape[0]
    copies = []
    for j in range(count):
        copies.append(pltpu.make_async_copy(own.at[j], blocks.at[core * count + j], sem.at[j]))
        copies.append(
            pltpu.make_async_copy(
                swapped.at[j], blocks.at[(1 - core) * count + j], sem.at[count + j]
            )
        )
    for copy in copies:
        copy.start()

    def wait():
        for copy in copies:
            copy.wait()

    return wait


def store_blocks(core, blocks, keep, send, sem):
    count = keep.shape[0]
    copies = []
    for j in range(count):
        copies.append(pltpu.make_async_copy(blocks.at[core * count + j], keep.at[j], sem.at[j]))
        copies.append(
            pltpu.make_async_copy(
                blocks.at[(1 - core) * count + j], send.at[j], sem.at[count + j]
            )
        )
    for copy in copies:
        copy.start()
    for copy in copies:
        copy.wait()


def normalised(values):
    mean_row = jnp.mean(values, axis=-1, keepdims=True)
    centred = values - mean_row
    variance = jnp.mean(centred * centred, axis=-1, keepdims=True)
    scale = lax.rsqrt(variance + norm_epsilon)
    return centred * scale, scale


def norm_back(values, grads, gain):
    unit, scale = normalised(values)
    scaled = grads * gain
    first = jnp.mean(scaled, axis=-1, keepdims=True)
    second = jnp.mean(scaled * unit, axis=-1, keepdims=True)
    return (scaled - first - unit * second) * scale, grads * unit


def lane_masks():
    lanes = lax.broadcasted_iota(jnp.int32, (128, 2 * HEAD), 1)
    left = (lanes < HEAD).astype(f32).astype(bf16)
    right = (lanes >= HEAD).astype(f32).astype(bf16)
    return lanes < HEAD, left, right


def two_heads(values, left, right):
    return jnp.concatenate([values * left, values * right], 0)


def softened(queries, keys_both, count):
    scores = nt(queries, keys_both) * HEAD ** (-0.5)
    slots = queries.shape[0]
    valid = lax.broadcasted_iota(jnp.int32, (slots, slots), 1) < count
    halves = []
    for half in (scores[:, :slots], scores[:, slots:]):
        half = jnp.where(valid, half, -1000000000.0)
        weights = jnp.exp(half - jnp.max(half, axis=-1, keepdims=True))
        halves.append(weights / jnp.sum(weights, axis=-1, keepdims=True))
    return jnp.concatenate(halves, 1)


def attend_kernel(
    cross,
    slots,
    info_ref,
    counts_ref,
    vec_ref,
    *refs,
):
    if cross:
        lang, vis, lang_far, vis_far, own_w, swapped_w = refs[:6]
        refs = refs[6:]
    else:
        residual_ref, low_ref, own_w, swapped_w = refs[:4]
        refs = refs[4:]
    q_ref, k_ref, v_ref, o_ref, sum_ref, norm_ref, norm_low_ref = refs[:7]
    blocks, sem = refs[7:9]
    core = info_ref[1]
    rows = q_ref.shape[0]
    half = rows // 2
    wait_blocks = load_blocks(core, own_w, swapped_w, blocks, sem)
    if cross:
        src_ref, oth_ref, in_sem = refs[9:12]

        def copies(mine, mine_far, other, other_far):
            return [
                pltpu.make_async_copy(mine, src_ref.at[pl.ds(0, half)], in_sem.at[0]),
                pltpu.make_async_copy(mine_far, src_ref.at[pl.ds(half, half)], in_sem.at[1]),
                pltpu.make_async_copy(other, oth_ref.at[pl.ds(0, half)], in_sem.at[2]),
                pltpu.make_async_copy(other_far, oth_ref.at[pl.ds(half, half)], in_sem.at[3]),
            ]

        @pl.when(info_ref[0] == 0)
        def _():
            for copy in copies(lang, lang_far, vis, vis_far):
                copy.start()

        @pl.when(info_ref[0] != 0)
        def _():
            for copy in copies(vis, vis_far, lang, lang_far):
                copy.start()

        for copy in copies(lang, lang_far, vis, vis_far):
            copy.wait()
    else:
        src_ref = oth_ref = low_ref
    wait_blocks()
    width = q_ref.shape[1]

    def project_tile(at):
        q_ref[:, at] = (nn(src_ref[...], blocks[0, :, at]) + vec_ref[0:1, at]).astype(bf16)
        k_ref[:, at] = nn(oth_ref[...], blocks[1, :, at]).astype(bf16)
        v_ref[:, at] = (nn(oth_ref[...], blocks[2, :, at]) + vec_ref[1:2, at]).astype(bf16)

    tiles(width, project_tile)
    unused, left, right = lane_masks()

    def one_page(page, carry):
        at_rows = pl.ds(pl.multiple_of(page * slots, slots), slots)
        count = counts_ref[page]
        for pair in range(width // 128):
            lanes = slice(pair * 128, pair * 128 + 128)
            soft = softened(
                q_ref[at_rows, lanes], two_heads(k_ref[at_rows, lanes], left, right), count
            ).astype(bf16)
            mixed = nn(soft, two_heads(v_ref[at_rows, lanes], left, right))
            o_ref[at_rows, lanes] = mixed.astype(bf16)
        return carry

    lax.fori_loop(0, rows // slots, one_page, 0)

    def out_tile(at):
        out = nn(o_ref[...], blocks[3, :, at]) + vec_ref[2:3, at]
        if cross:
            sum_ref[:, at] = src_ref[:, at].astype(f32) + out
        else:
            sum_ref[:, at] = residual_ref[:, at] + out

    tiles(width, out_tile)

    def norm_rows(at):
        result = normalised(sum_ref[at, :])[0] * vec_ref[3:4, :] + vec_ref[4:5, :]
        norm_ref[at, :] = result
        norm_low_ref[at, :] = result.astype(bf16)

    tiles(rows, norm_rows, 128)


def attend(cross, slots, info, counts, vectors, inputs, weights):
    width = weights[0].shape[-1]
    rows = counts.shape[0] * slots
    blocks = (4, width, width)
    scratch = [pltpu.VMEM(blocks, bf16), pltpu.SemaphoreType.DMA((4,))]
    if cross:
        scratch += [pltpu.VMEM((rows, width), bf16)] * 2 + [pltpu.SemaphoreType.DMA((4,))]
    return call(
        functools.partial(attend_kernel, cross, slots),
        [((rows, width), bf16)] * 4 + [((rows, width), f32)] * 2 + [((rows, width), bf16)],
        [info, counts, vectors] + list(inputs) + list(weights),
        [SMEM, SMEM, VMEM] + ([ANY] * 4 if cross else [VMEM] * 2) + [ANY] * 2,
        [VMEM] * 7,
        scratch,
        flops=8 * rows * width * width + 8 * rows * slots * width,
        moved=4 * width * width * 2 + rows * width * 20,
    )


def hidden_kernel(info_ref, shift_ref, low_ref, own_w, swapped_w, active_ref, slope_ref, blocks, sem):
    wait_blocks = load_blocks(info_ref[1], own_w, swapped_w, blocks, sem)
    wait_blocks()
    width = low_ref.shape[1]
    for b in range(4):

        def tile(at, b=b):
            wide = pl.ds(pl.multiple_of(at.start + b * width, TILE), TILE)
            hidden = nn(low_ref[...], blocks[b, :, at]) + shift_ref[0:1, wide]
            square = hidden * hidden
            bent = jnp.tanh(0.7978845608028654 * (hidden + 0.044715 * square * hidden))
            active_ref[:, wide] = (0.5 * hidden * (1.0 + bent)).astype(bf16)
            slope = 0.5 * (1.0 + bent) + 0.5 * hidden * (1.0 - bent * bent) * (
                0.7978845608028654 * (1.0 + 3.0 * 0.044715 * square)
            )
            slope_ref[:, wide] = slope.astype(bf16)

        tiles(width, tile)


def hidden_layer(info, shift, low, weights):
    rows, width = low.shape
    return call(
        hidden_kernel,
        [((rows, 4 * width), bf16)] * 2,
        [info, shift, low] + list(weights),
        [SMEM, VMEM, VMEM, ANY, ANY],
        [VMEM, VMEM],
        [pltpu.VMEM((4, width, width), bf16), pltpu.SemaphoreType.DMA((4,))],
        flops=8 * rows * width * width,
        moved=8 * width * width + rows * width * 18,
    )


def load_wide(core, own, swapped, wide, sem):
    n, rows = own.shape[1:3]
    for j in range(2):
        for which, source in ((core, own), (1 - core, swapped)):

            def body(p, carry, j=j, which=which, source=source):
                at = pl.multiple_of((4 * p + 2 * which + j) * rows, 16)
                pltpu.make_async_copy(source.at[j, p], wide.at[pl.ds(at, rows)], sem).start()
                return carry

            lax.fori_loop(0, n, body, 0)


def store_wide(core, wide, keep, send, sem):
    n, rows = keep.shape[1:3]
    for j in range(2):
        for which, target in ((core, keep), (1 - core, send)):

            def body(p, carry, j=j, which=which, target=target):
                at = pl.multiple_of((4 * p + 2 * which + j) * rows, 16)
                pltpu.make_async_copy(wide.at[pl.ds(at, rows)], target.at[j, p], sem).start()
                return carry

            lax.fori_loop(0, n, body, 0)
    pltpu.make_async_copy(wide, wide, sem).wait()


def branch_kernel(
    wide_in,
    info_ref,
    vec_ref,
    active_ref,
    residual_ref,
    *refs,
):
    if wide_in:
        own_w, swapped_w, sum_ref, norm_ref, far_ref, wide, sem = refs
        load_wide(info_ref[1], own_w, swapped_w, wide, sem)
        pltpu.make_async_copy(wide, wide, sem).wait()
    else:
        whole_w, sum_ref, norm_ref, far_ref, wide, sem = refs
        copy = pltpu.make_async_copy(whole_w, wide, sem)
        copy.start()
        copy.wait()
    rows, width = residual_ref.shape
    half = rows // 2

    def tile(at):
        out = nn(active_ref[...], wide[:, at]) + vec_ref[0:1, at]
        sum_ref[:, at] = residual_ref[:, at] + out

    tiles(width, tile)

    def norm_rows(at):
        result = normalised(sum_ref[at, :])[0] * vec_ref[1:2, :] + vec_ref[2:3, :]
        norm_ref[at, :] = result

    tiles(half, norm_rows, 128)

    def norm_far(at):
        below = pl.ds(pl.multiple_of(at.start + half, 128), 128)
        result = normalised(sum_ref[below, :])[0] * vec_ref[1:2, :] + vec_ref[2:3, :]
        far_ref[at, :] = result.astype(bf16)

    tiles(half, norm_far, 128)


def branch_layer(info, vectors, active, residual, weights):
    rows, width = residual.shape
    wide_in = len(weights) == 2
    return call(
        functools.partial(branch_kernel, wide_in),
        [((rows, width), f32), ((rows // 2, width), f32), ((rows // 2, width), bf16)],
        [info, vectors, active, residual] + list(weights),
        [SMEM, VMEM, VMEM, VMEM] + [ANY] * len(weights),
        [VMEM] * 3,
        [pltpu.VMEM((4 * width, width), bf16), pltpu.SemaphoreType.DMA],
        flops=8 * rows * width * width,
        moved=8 * width * width + rows * width * 20,
    )


def gate_kernel(
    info_ref,
    shift_ref,
    third_ref,
    far_ref,
    cotangent_ref,
    own_w,
    swapped_w,
    united_ref,
    grad_own_ref,
    grad_far_ref,
    grad_shift_ref,
    keep_ref,
    send_ref,
    blocks,
    sem,
    grads,
    mix_ref,
    low_ref,
):
    core = info_ref[1]
    side = info_ref[0]
    load_blocks(core, own_w, swapped_w, blocks, sem)()
    rows, width = third_ref.shape
    part = width // 2
    low_ref[...] = third_ref[...].astype(bf16)
    for h in range(2):
        at = slice(h * part, (h + 1) * part)
        logits = nn(low_ref[...], blocks[h]) + nn(far_ref[...], blocks[2 + h]) + shift_ref[0:1, at]
        mixing = 1.0 / (1.0 + jnp.exp(-logits))
        first = side == 0
        share = jnp.where(first, mixing, 1.0 - mixing)
        mine, other = third_ref[:, at], far_ref[:, at].astype(f32)
        united_ref[:, at] = (share * mine + (1.0 - share) * other).astype(bf16)
        cotangent = cotangent_ref[:, at].astype(f32)
        gap = jnp.where(first, mine - other, other - mine)
        grad = (cotangent * gap * mixing * (1.0 - mixing)).astype(bf16)
        mix_ref[:, at] = grad
        grad_own_ref[:, at] = cotangent * share
        grad_shift_ref[0:1, at] = jnp.sum(grad.astype(f32), axis=0, keepdims=True)
        grads[h] = tn(low_ref[...], grad).astype(bf16)
        grads[2 + h] = tn(far_ref[...], grad).astype(bf16)
    left, right = mix_ref[:, :part], mix_ref[:, part:]
    for t in range(width // TILE):
        at = slice(t * TILE, (t + 1) * TILE)
        cotangent = cotangent_ref[:, at].astype(f32)
        direct = grad_own_ref[:, at]
        back = nt(left, blocks[0, at]) + nt(right, blocks[1, at])
        back_far = nt(left, blocks[2, at]) + nt(right, blocks[3, at])
        grad_own_ref[:, at] = direct + back
        grad_far_ref[:, at] = (cotangent - direct + back_far).astype(bf16)
    store_blocks(core, grads, keep_ref, send_ref, sem)


def gate_layer(info, shift, third, far, cotangent, weights):
    rows, width = third.shape
    blocks = (4, width, width // 2)
    return call(
        gate_kernel,
        [
            ((rows, width), bf16),
            ((rows, width), f32),
            ((rows, width), bf16),
            ((8, width), f32),
            ((2,) + blocks[1:], bf16),
            ((2,) + blocks[1:], bf16),
        ],
        [info, shift, third, far, cotangent] + list(weights),
        [SMEM] + [VMEM] * 4 + [ANY] * 2,
        [VMEM] * 4 + [ANY] * 2,
        [
            pltpu.VMEM(blocks, bf16),
            pltpu.SemaphoreType.DMA((4,)),
            pltpu.VMEM(blocks, bf16),
            pltpu.VMEM((rows, width), bf16),
            pltpu.VMEM((rows, width), bf16),
        ],
        flops=12 * rows * width * width,
        moved=8 * width * width + rows * width * 14,
    )


def branch_back_kernel(
    wide_out,
    info_ref,
    gain_ref,
    sum_ref,
    grad_own_ref,
    grad_far_ref,
    active_ref,
    grad_sum_ref,
    grad_low_ref,
    vec_ref,
    *refs,
):
    rows, width = sum_ref.shape
    half = rows // 2
    vec_ref[...] = jnp.zeros_like(vec_ref)

    def norm_rows(at, offset, grads):
        below = pl.ds(pl.multiple_of(at.start + offset, 128), 128)
        back, gain_rows = norm_back(sum_ref[below, :], grads, gain_ref[0:1, :])
        low = back.astype(bf16)
        grad_sum_ref[below, :] = back
        grad_low_ref[below, :] = low
        vec_ref[0:1, :] += jnp.sum(gain_rows, axis=0, keepdims=True)
        vec_ref[1:2, :] += jnp.sum(grads, axis=0, keepdims=True)
        vec_ref[2:3, :] += jnp.sum(low.astype(f32), axis=0, keepdims=True)

    tiles(half, lambda at: norm_rows(at, 0, grad_own_ref[at, :]), 128)
    tiles(half, lambda at: norm_rows(at, half, grad_far_ref[at, :].astype(f32)), 128)
    wide, sem = refs[-2:]

    def tile(at):
        wide[at, :] = tn(active_ref[:, at], grad_low_ref[...]).astype(bf16)

    tiles(4 * width, tile)
    if wide_out:
        store_wide(info_ref[1], wide, refs[0], refs[1], sem)
    else:
        copy = pltpu.make_async_copy(wide, refs[0], sem)
        copy.start()
        copy.wait()


def branch_back(grid, info, gain, sums, grad_own, grad_far, active, piece):
    rows, width = sums.shape
    wide_out = piece % 16 == 0
    target = (2, grid.n, piece, width) if wide_out else (4 * width, width)
    outs = [(target, bf16)] * (2 if wide_out else 1)
    return call(
        functools.partial(branch_back_kernel, wide_out),
        [((rows, width), f32), ((rows, width), bf16), ((8, width), f32)] + outs,
        [info, gain, sums, grad_own, grad_far, active],
        [SMEM] + [VMEM] * 5,
        [VMEM] * 3 + [ANY] * len(outs),
        [pltpu.VMEM((4 * width, width), bf16), pltpu.SemaphoreType.DMA],
        flops=8 * rows * width * width,
        moved=8 * width * width + rows * width * 24,
    )


def hidden_back_kernel(
    wide_in,
    info_ref,
    grad_low_ref,
    slope_ref,
    low_ref,
    *refs,
):
    core = info_ref[1]
    grad_hidden_ref, vec_ref, keep_ref, send_ref, wide, sem, grads, out_sem = refs[-8:]
    if wide_in:
        load_wide(core, refs[0], refs[1], wide, sem)
        pltpu.make_async_copy(wide, wide, sem).wait()
    else:
        copy = pltpu.make_async_copy(refs[0], wide, sem)
        copy.start()
        copy.wait()
    width = low_ref.shape[1]
    for b in range(4):

        def tile(at, b=b):
            cols = pl.ds(pl.multiple_of(at.start + b * width, TILE), TILE)
            back = nt(grad_low_ref[...], wide[cols, :]) * slope_ref[:, cols].astype(f32)
            low = back.astype(bf16)
            grad_hidden_ref[:, cols] = low
            vec_ref[0:1, cols] = jnp.sum(low.astype(f32), axis=0, keepdims=True)
            grads[b, :, at] = tn(low_ref[...], low).astype(bf16)

        tiles(width, tile)
    store_blocks(core, grads, keep_ref, send_ref, out_sem)


def hidden_back(info, grad_low, slope, low, weights):
    rows, width = low.shape
    blocks = (4, width, width)
    return call(
        functools.partial(hidden_back_kernel, len(weights) == 2),
        [((rows, 4 * width), bf16), ((8, 4 * width), f32)] + [((2,) + blocks[1:], bf16)] * 2,
        [info, grad_low, slope, low] + list(weights),
        [SMEM] + [VMEM] * 3 + [ANY] * len(weights),
        [VMEM] * 2 + [ANY] * 2,
        [
            pltpu.VMEM((4 * width, width), bf16),
            pltpu.SemaphoreType.DMA,
            pltpu.VMEM(blocks, bf16),
            pltpu.SemaphoreType.DMA((4,)),
        ],
        flops=16 * rows * width * width,
        moved=16 * width * width + rows * width * 30,
    )


def second_back_kernel(
    info_ref,
    gain_ref,
    sum_ref,
    grad_ref,
    grad_hidden_ref,
    own_w,
    swapped_w,
    grad_sum_ref,
    vec_ref,
    blocks,
    sem,
):
    load_blocks(info_ref[1], own_w, swapped_w, blocks, sem)()
    rows, width = sum_ref.shape

    def tile(at):
        total = grad_ref[:, at]
        for b in range(4):
            total += nt(grad_hidden_ref[:, b * width : (b + 1) * width], blocks[b, at, :])
        grad_sum_ref[:, at] = total

    tiles(width, tile)
    norm_back_rows(sum_ref, grad_sum_ref, gain_ref, vec_ref, rows)


def norm_back_rows(sum_ref, grad_ref, gain_ref, vec_ref, rows):
    vec_ref[0:2, :] = jnp.zeros_like(vec_ref[0:2, :])

    def norm_rows(at):
        grads = grad_ref[at, :]
        back, gain_rows = norm_back(sum_ref[at, :], grads, gain_ref[0:1, :])
        grad_ref[at, :] = back
        vec_ref[0:1, :] += jnp.sum(gain_rows, axis=0, keepdims=True)
        vec_ref[1:2, :] += jnp.sum(grads, axis=0, keepdims=True)

    tiles(rows, norm_rows, 128)


def second_back(info, gain, sums, grads, grad_hidden, weights):
    rows, width = sums.shape
    return call(
        second_back_kernel,
        [((rows, width), f32), ((8, width), f32)],
        [info, gain, sums, grads, grad_hidden] + list(weights),
        [SMEM] + [VMEM] * 4 + [ANY] * 2,
        [VMEM] * 2,
        [pltpu.VMEM((4, width, width), bf16), pltpu.SemaphoreType.DMA((4,))],
        flops=8 * rows * width * width,
        moved=8 * width * width + rows * width * 20,
    )


def attend_back_kernel(cross, slots, info_ref, counts_ref, gain_ref, grad_ref, *refs):
    q_ref, k_ref, v_ref, o_ref = refs[:4]
    refs = refs[4:]
    if cross:
        lang, vis, lang_far, vis_far, own_w, swapped_w = refs[:6]
        own_ref, own_far_ref, oth_ref_out, oth_far_ref, vec_ref, keep_ref, send_ref = refs[6:13]
        refs = refs[13:]
    else:
        low_ref, sum_ref, own_w, swapped_w = refs[:4]
        out_ref, vec_ref, keep_ref, send_ref = refs[4:8]
        refs = refs[8:]
    blocks, sem, grads, low_grad, grad_o, dq_ref, dk_ref, dv_ref = refs[:8]
    core = info_ref[1]
    rows, width = q_ref.shape
    half = rows // 2
    wait_blocks = load_blocks(core, own_w, swapped_w, blocks, sem)
    if cross:
        src_ref, oth_ref, in_sem = refs[8:11]

        def copies(mine, mine_far, other, other_far):
            return [
                pltpu.make_async_copy(mine, src_ref.at[pl.ds(0, half)], in_sem.at[0]),
                pltpu.make_async_copy(mine_far, src_ref.at[pl.ds(half, half)], in_sem.at[1]),
                pltpu.make_async_copy(other, oth_ref.at[pl.ds(0, half)], in_sem.at[2]),
                pltpu.make_async_copy(other_far, oth_ref.at[pl.ds(half, half)], in_sem.at[3]),
            ]

        @pl.when(info_ref[0] == 0)
        def _():
            for copy in copies(lang, lang_far, vis, vis_far):
                copy.start()

        @pl.when(info_ref[0] != 0)
        def _():
            for copy in copies(vis, vis_far, lang, lang_far):
                copy.start()

    else:
        src_ref = oth_ref = low_ref
    vec_ref[...] = jnp.zeros_like(vec_ref)

    def lower(at):
        low = grad_ref[at, :].astype(bf16)
        low_grad[at, :] = low
        vec_ref[4:5, :] += jnp.sum(low.astype(f32), axis=0, keepdims=True)

    tiles(rows, lower, 128)
    wait_blocks()

    def project_tile(at):
        grad_o[:, at] = nt(low_grad[...], blocks[3, at, :]).astype(bf16)
        grads[3, at, :] = tn(o_ref[:, at], low_grad[...]).astype(bf16)

    tiles(width, project_tile)
    left_lanes, left, right = lane_masks()

    def one_page(page, carry):
        at_rows = pl.ds(pl.multiple_of(page * slots, slots), slots)
        count = counts_ref[page]
        for pair in range(width // 128):
            lanes = slice(pair * 128, pair * 128 + 128)
            queries = q_ref[at_rows, lanes]
            keys = two_heads(k_ref[at_rows, lanes], left, right)
            values = two_heads(v_ref[at_rows, lanes], left, right)
            grad_pair = grad_o[at_rows, lanes]
            soft = softened(queries, keys, count)
            grad_soft = nt(grad_pair, values)
            dv = tn(soft.astype(bf16), grad_pair)
            dv_ref[at_rows, lanes] = jnp.where(left_lanes, dv[:slots], dv[slots:]).astype(bf16)
            weighted = soft * grad_soft
            parts = []
            for h in range(2):
                cut = slice(h * slots, (h + 1) * slots)
                row_sum = jnp.sum(weighted[:, cut], axis=-1, keepdims=True)
                parts.append(weighted[:, cut] - soft[:, cut] * row_sum)
            grad_scores = jnp.concatenate(parts, 1).astype(bf16)
            dq = nn(grad_scores, keys) * HEAD ** (-0.5)
            dq_ref[at_rows, lanes] = dq.astype(bf16)
            dk = tn(grad_scores, queries) * HEAD ** (-0.5)
            dk_ref[at_rows, lanes] = jnp.where(left_lanes, dk[:slots], dk[slots:]).astype(bf16)
        return carry

    lax.fori_loop(0, rows // slots, one_page, 0)

    def sum_rows(at):
        vec_ref[2:3, :] += jnp.sum(dq_ref[at, :].astype(f32), axis=0, keepdims=True)
        vec_ref[3:4, :] += jnp.sum(dv_ref[at, :].astype(f32), axis=0, keepdims=True)

    tiles(rows, sum_rows, 128)
    if cross:
        for copy in copies(lang, lang_far, vis, vis_far):
            copy.wait()

    def weight_tile(at):
        grads[0, at, :] = tn(src_ref[:, at], dq_ref[...]).astype(bf16)
        grads[1, at, :] = tn(oth_ref[:, at], dk_ref[...]).astype(bf16)
        grads[2, at, :] = tn(oth_ref[:, at], dv_ref[...]).astype(bf16)

    tiles(width, weight_tile)

    def input_tile(at):
        mine = grad_ref[:, at] + nt(dq_ref[...], blocks[0, at, :])
        other = nt(dk_ref[...], blocks[1, at, :]) + nt(dv_ref[...], blocks[2, at, :])
        if cross:
            own_ref[:, at] = mine[:half]
            own_far_ref[:, at] = mine[half:].astype(bf16)
            oth_ref_out[:, at] = other[:half]
            oth_far_ref[:, at] = other[half:].astype(bf16)
        else:
            out_ref[:, at] = mine + other

    tiles(width, input_tile)
    if not cross:
        norm_back_rows(sum_ref, out_ref, gain_ref, vec_ref, rows)
    store_blocks(core, grads, keep_ref, send_ref, sem)


def attend_back(cross, slots, info, counts, gain, grad, saved, inputs, weights):
    rows, width = grad.shape
    blocks = (4, width, width)
    whole = pltpu.VMEM((rows, width), bf16)
    scratch = [
        pltpu.VMEM(blocks, bf16),
        pltpu.SemaphoreType.DMA((4,)),
        pltpu.VMEM(blocks, bf16),
    ] + [whole] * 5
    half = (rows // 2, width)
    if cross:
        scratch += [whole, whole, pltpu.SemaphoreType.DMA((4,))]
        outs = [(half, f32), (half, bf16), (half, f32), (half, bf16)]
    else:
        outs = [((rows, width), f32)]
    return call(
        functools.partial(attend_back_kernel, cross, slots),
        outs + [((8, width), f32)] + [((2,) + blocks[1:], bf16)] * 2,
        [info, counts, gain, grad] + list(saved) + list(inputs) + list(weights),
        [SMEM, SMEM] + [VMEM] * 6 + ([ANY] * 4 if cross else [VMEM] * 2) + [ANY] * 2,
        [VMEM] * (len(outs) + 1) + [ANY] * 2,
        scratch,
        flops=16 * rows * width * width + 24 * rows * slots * width,
        moved=16 * width * width + rows * width * 26,
    )


def reorder(values, hits):
    hits = hits.reshape(hits.shape + (1,) * (values.ndim - 1))
    return jnp.sum(jnp.where(hits, values.astype(f32)[None], 0.0), axis=1)


def on_device(
    grid,
    language_in,
    vision_in,
    language_count,
    vision_count,
    cross_qkv,
    cross_proj,
    cross_bias,
    norm_gain,
    norm_bias,
    self_qkv,
    self_proj,
    self_bias,
    ffn_in,
    ffn_in_bias,
    ffn_out,
    ffn_out_bias,
    gate_weight,
    gate_bias,
    cotangent,
):
    n = grid.n
    me = lax.axis_index("dp")
    core = lax.axis_index("rep")
    side = ((me // grid.high) ^ (me // grid.partner)) & 1
    first = side == 0
    info = jnp.stack([side, core, me]).astype(jnp.int32)
    rows, width = cross_proj.shape[1:]
    dim = n * rows
    pages, slots = language_in.shape[:2]
    wide_ok = rows % 16 == 0

    def own(pair):
        return lax.dynamic_index_in_dim(pair, side, 0, keepdims=False)

    def other(pair):
        return lax.dynamic_index_in_dim(pair, 1 - side, 0, keepdims=False)

    def gathered(blocks):
        stacked = jnp.stack(blocks, 1)
        stacked = stacked.reshape((2, 2, 2) + stacked.shape[2:])
        stacked = lax.dynamic_index_in_dim(stacked, core, 1, keepdims=False)
        return gather_round(grid, info, own(stacked), other(stacked))

    def natural(pair):
        return [w.reshape(2, dim, w.shape[-1]) for w in pair]

    cross_w = natural(gathered([cross_qkv[:, 0], cross_qkv[:, 1], cross_qkv[:, 2], cross_proj]))
    language = language_in.reshape(pages * slots, width)
    vision = vision_in.reshape(pages * slots, width)
    language_far = grid.across(language, grid.partner)
    vision_far = grid.across(vision, grid.partner)
    counts_mine = jnp.stack([language_count, vision_count])
    counts_far = grid.across(counts_mine, grid.partner)
    counts = jnp.concatenate([own(counts_mine), own(counts_far)])
    other_counts = jnp.concatenate([other(counts_mine), other(counts_far)])

    vectors = jnp.concatenate(
        [
            cross_bias,
            self_bias,
            norm_gain,
            norm_bias,
            ffn_in_bias.reshape(2, 4, rows),
            ffn_out_bias[:, None],
            jnp.broadcast_to(gate_bias[None, None], (2, 1, rows)),
        ],
        1,
    ).reshape(2, 18 * rows)
    pad = -(18 * rows) % 1024
    vectors = jnp.pad(vectors, ((0, 0), (0, pad))).reshape(2, 1, -1, 128)
    vec_mine, vec_theirs = own(vectors), other(vectors)
    held = jnp.concatenate(
        [
            vec_mine,
            grid.across(vec_theirs, grid.groups[1]),
            grid.across(vec_theirs, grid.groups[2]),
            grid.across(vec_mine, grid.groups[3]),
        ],
        0,
    )
    for bit in grid.orders[0]:
        held = jnp.concatenate([held, grid.across(held, bit)], 0)
    masks = jnp.array([m ^ g for m in grid.piece_masks(0) for g in grid.groups], jnp.int32)
    hits = (masks ^ me)[None, :] == jnp.arange(n)[:, None]
    vec_full = reorder(held, hits).reshape(n, -1)[:, : 18 * rows].reshape(n, 18, rows)
    vec_rows = vec_full.transpose(1, 0, 2).reshape(18, dim)
    ffn_in_shift = vec_full[:, 12:16].reshape(1, 4 * dim)

    def rows_of(*indices):
        return jnp.stack([vec_rows[i] for i in indices])

    self_w = natural(gathered([self_qkv[:, 0], self_qkv[:, 1], self_qkv[:, 2], self_proj]))
    in_w = natural(gathered([ffn_in[:, :, i * width : (i + 1) * width] for i in range(4)]))
    out_w = gathered([ffn_out[:, i * rows : (i + 1) * rows] for i in range(4)])
    if not wide_ok:
        both = jnp.where(core == 0, jnp.stack(out_w), jnp.stack(out_w[::-1]))
        out_w = [both.reshape(4, n, rows, width).transpose(1, 0, 2, 3).reshape(4 * dim, width)]
    part = width // 2
    turned = gate_weight[::-1]
    gate_w = natural(
        gathered(
            [gate_weight[:, :, :part], gate_weight[:, :, part:], turned[:, :, :part], turned[:, :, part:]]
        )
    )

    inputs = [language, vision, language_far, vision_far]
    cq, ck, cv, co, first_sum, first_norm, first_low = attend(
        True, slots, info, other_counts, rows_of(0, 1, 2, 6, 9), inputs, cross_w
    )
    sq, sk, sv, so, second_sum, second_norm, second_low = attend(
        False, slots, info, counts, rows_of(3, 4, 5, 7, 10), [first_norm, first_low], self_w
    )
    active, slope = hidden_layer(info, ffn_in_shift, second_low, in_w)
    third_sum, third_own, third_send = branch_layer(
        info, rows_of(16, 8, 11), active, second_norm, out_w
    )
    third_far = grid.across(third_send, grid.partner)
    united, grad_third_own, grad_third_send, grad_gate_shift, gate_keep, gate_send = gate_layer(
        info, rows_of(17), third_own, third_far, cotangent.reshape(pages * slots, width), gate_w
    )
    grad_third_far = grid.across(grad_third_send, grid.partner)

    def by_piece(pair):
        return [g.reshape(2, n, rows, g.shape[-1]) for g in pair]

    gate_done = scatter_round(grid, info, *by_piece([gate_keep, gate_send]))
    grad_third_sum, grad_branch_low, vec_third, *out_grads = branch_back(
        grid, info, rows_of(8), third_sum, grad_third_own, grad_third_far, active, rows
    )
    if not wide_ok:
        by_core = out_grads[0].reshape(n, 2, 2, rows, width).transpose(1, 2, 0, 3, 4)
        out_grads = [
            lax.dynamic_index_in_dim(by_core, c, 0, keepdims=False) for c in (core, 1 - core)
        ]
    out_done = scatter_round(grid, info, *out_grads)
    grad_hidden, vec_hidden, in_keep, in_send = hidden_back(
        info, grad_branch_low, slope, second_low, out_w
    )
    in_done = scatter_round(grid, info, *by_piece([in_keep, in_send]))
    grad_second_sum, vec_second = second_back(
        info, rows_of(7), second_sum, grad_third_sum, grad_hidden, in_w
    )
    grad_first_sum, vec_self, self_keep, self_send = attend_back(
        False,
        slots,
        info,
        counts,
        rows_of(6),
        grad_second_sum,
        [sq, sk, sv, so],
        [first_low, first_sum],
        self_w,
    )
    self_done = scatter_round(grid, info, *by_piece([self_keep, self_send]))
    grad_own, grad_own_far, grad_oth, grad_oth_far, vec_cross, cross_keep, cross_send = attend_back(
        True,
        slots,
        info,
        other_counts,
        rows_of(6),
        grad_first_sum,
        [cq, ck, cv, co],
        inputs,
        cross_w,
    )
    grad_mine = grad_own + grid.across(grad_oth_far, grid.partner).astype(f32)
    grad_theirs = grad_oth + grid.across(grad_own_far, grid.partner).astype(f32)
    cross_done = scatter_round(grid, info, *by_piece([cross_keep, cross_send]))
    page_shape = language_in.shape
    grad_language = jnp.where(first, grad_mine, grad_theirs).astype(bf16).reshape(page_shape)
    grad_vision = jnp.where(first, grad_theirs, grad_mine).astype(bf16).reshape(page_shape)

    grad_rows = jnp.stack(
        [vec_cross[2], vec_cross[3], vec_cross[4]]
        + [vec_self[2], vec_self[3], vec_self[4]]
        + [vec_self[0], vec_second[0], vec_third[0]]
        + [vec_self[1], vec_second[1], vec_third[1]]
    ).reshape(12, n, rows)
    grad_tail = jnp.stack([vec_third[2], grad_gate_shift[0]]).reshape(2, n, rows)
    grad_vec = jnp.concatenate(
        [
            grad_rows.transpose(1, 0, 2),
            vec_hidden[0].reshape(n, 4, rows),
            grad_tail.transpose(1, 0, 2),
        ],
        1,
    ).reshape(n, 18 * rows)
    grad_vec = jnp.pad(grad_vec, ((0, 0), (0, pad))).reshape(n, -1, 128)
    grad_vec = reorder(grad_vec, hits.T)
    grad_vec = grad_vec + grid.swap_cores(grad_vec)
    for bit in reversed(grid.orders[0]):
        half = grad_vec.shape[0] // 2
        grad_vec = grad_vec[:half] + grid.across(grad_vec[half:], bit)
    vec_near = grad_vec[0] + grid.across(grad_vec[3], grid.groups[3])
    vec_far = grid.across(grad_vec[1], grid.groups[1]) + grid.across(grad_vec[2], grid.groups[2])
    vec_near = vec_near.reshape(-1)[: 18 * rows].reshape(18, rows)
    vec_far = vec_far.reshape(-1)[: 18 * rows].reshape(18, rows)

    def sides(near, far):
        return jnp.where(first, jnp.stack([near, far]), jnp.stack([far, near]))

    vec_both = sides(vec_near, vec_far)

    def finished(done):
        mine = jnp.stack(done).astype(bf16)
        far = grid.swap_cores(mine)
        whole = jnp.where(core == 0, jnp.stack([mine, far], 1), jnp.stack([far, mine], 1))
        return whole.reshape((2, 4) + whole.shape[3:]).astype(f32)

    def by_side(done):
        whole = finished(done)
        return jnp.where(first, whole, whole[::-1])

    cross_all = by_side(cross_done)
    self_all = by_side(self_done)
    in_all = by_side(in_done)
    out_all = by_side(out_done)
    gate_all = finished(gate_done)
    gate_near = gate_all[0, :2] + gate_all[1, 2:]
    gate_far = gate_all[0, 2:] + gate_all[1, :2]
    gate_both = sides(
        jnp.concatenate([gate_near[0], gate_near[1]], -1),
        jnp.concatenate([gate_far[0], gate_far[1]], -1),
    )
    return (
        united.reshape(page_shape),
        grad_language,
        grad_vision,
        cross_all[:, 0:3],
        cross_all[:, 3],
        vec_both[:, 0:3],
        vec_both[:, 6:9],
        vec_both[:, 9:12],
        self_all[:, 0:3],
        self_all[:, 3],
        vec_both[:, 3:6],
        in_all.transpose(0, 2, 1, 3).reshape(2, rows, 4 * width),
        vec_both[:, 12:16].reshape(2, 4 * rows),
        out_all.reshape(2, 4 * rows, width),
        vec_both[:, 16],
        gate_both,
        vec_near[17] + vec_far[17],
    )


def solution(mesh):
    whole = P(("dp", "rep"), None, None)
    weights = (
        P(None, None, "dp", None),
        P(None, "dp", None),
        P(None, None, "dp"),
        P(None, None, "dp"),
        P(None, None, "dp"),
        P(None, None, "dp", None),
        P(None, "dp", None),
        P(None, None, "dp"),
        P(None, "dp", None),
        P(None, "dp"),
        P(None, "dp", None),
        P(None, "dp"),
        P(None, "dp", None),
        P("dp"),
    )
    return jax.shard_map(
        functools.partial(on_device, Grid(mesh)),
        mesh=mesh,
        in_specs=(whole, whole, P(("dp", "rep")), P(("dp", "rep"))) + weights + (whole,),
        out_specs=(whole, whole, whole) + weights,
        check_vma=False,
    )
```

```python
import functools

import jax
import jax.numpy as jnp
from jax import lax
from jax.experimental import pallas as pl
from jax.experimental.pallas import tpu as pltpu
from jax.sharding import PartitionSpec as P

HEADS = 12
HEAD = 64
norm_epsilon = 1e-05
bf16 = jnp.bfloat16
f32 = jnp.float32
AXES = ("dp", "rep")
VMEM_LIMIT = 56 << 20
GLUE_LIMIT = 20 << 20
HBM = pl.BlockSpec(memory_space=pltpu.HBM)
VMEM = pl.BlockSpec(memory_space=pltpu.VMEM)
SMEM = pl.BlockSpec(memory_space=pltpu.SMEM)


class Grid:
    def __init__(self, mesh):
        self.n = mesh.shape["dp"]
        self.r = mesh.shape["rep"]
        self.high = self.n >> 1
        self.partner = self.n >> 2
        self.groups = [0, self.partner, self.high, self.high | self.partner]
        low = []
        bit = 1
        while bit < self.partner:
            low.append(bit)
            bit *= 2
        self.orders = [low, low[::-1]]
        self.high_bit = len(low) + 1

    def across(self, values, mask):
        pairs = [
            (d * self.r + c, (d ^ mask) * self.r + c) for d in range(self.n) for c in range(self.r)
        ]
        return lax.ppermute(values, AXES, pairs)

    def swap_cores(self, values):
        pairs = [
            (d * self.r + c, d * self.r + (c ^ 1)) for d in range(self.n) for c in range(self.r)
        ]
        return lax.ppermute(values, AXES, pairs)

    def hop(self, values, step):
        pairs = []
        for d in range(self.n):
            for c in range(self.r):
                mask = self.orders[c % 2][step]
                pairs.append((d * self.r + c, (d ^ mask) * self.r + c))
        return lax.ppermute(values, AXES, pairs)

    def place(self, info):
        core, me = info[1], info[2]
        first = jnp.right_shift(me, core) & 1
        second = jnp.right_shift(me, 1 - core) & 1
        return jnp.right_shift(me, 2), first, second, 1 + core, 2 - core

    def masks(self, core):
        found = [0]
        for low, high in zip(*self.orders, strict=True):
            bit = low + core * (high - low)
            found = found + [m ^ bit for m in found]
        return found


def call(kernel, outs, ins, specs, out_specs, scratch=(), flops=0, moved=0, room=VMEM_LIMIT):
    results = pl.pallas_call(
        kernel,
        out_shape=[jax.ShapeDtypeStruct(shape, dtype) for shape, dtype in outs],
        in_specs=specs,
        out_specs=out_specs,
        scratch_shapes=list(scratch),
        compiler_params=pltpu.CompilerParams(vmem_limit_bytes=room),
        cost_estimate=pl.CostEstimate(flops=flops, bytes_accessed=moved, transcendentals=0),
    )(*ins)
    return list(results)


def pair_kernel(bit_of, info_ref, *refs):
    mine, other = refs[:2]
    bit = jnp.right_shift(info_ref[2], bit_of) & 1
    start = 0
    for out in refs[2:]:
        end = start + out.shape[-2]
        out[bit] = mine[..., start:end, :]
        out[1 - bit] = other[..., start:end, :]
        start = end


def pair(info, bit_of, mine, other, parts=None):
    shape = mine.shape
    parts = [shape[-2]] if parts is None else parts
    if shape[-2] % 16:
        bit = jnp.right_shift(info[2], bit_of) & 1
        both = jnp.where(bit == 0, jnp.stack([mine, other]), jnp.stack([other, mine]))
        starts = [sum(parts[:i]) for i in range(len(parts))]
        return [both[..., s : s + p, :] for s, p in zip(starts, parts, strict=True)]
    return call(
        functools.partial(pair_kernel, bit_of),
        [((2,) + shape[:-2] + (part, shape[-1]), bf16) for part in parts],
        [info, mine, other],
        [SMEM, VMEM, VMEM],
        [VMEM] * len(parts),
        room=GLUE_LIMIT,
    )


def join_kernel(grid, info_ref, mine, other, out):
    bit = grid.place(info_ref)[1]
    for g in range(4):
        out[g, bit] = mine[g]
        out[g, 1 - bit] = other[g]


def join_pair(grid, info, pieces):
    shape = pieces[0].shape
    return call(
        functools.partial(join_kernel, grid),
        [((4, 2) + shape[1:], bf16)],
        [info] + pieces,
        [SMEM] + [VMEM] * 2,
        [VMEM],
        room=GLUE_LIMIT,
    )[0]


def tie(*values):
    flat, tree = jax.tree.flatten(values)
    return jax.tree.unflatten(tree, lax.optimization_barrier(flat))


def meet(grid, info, held):
    rows, width = held.shape[1:]
    received = grid.across(held, grid.groups[3])

    def place():
        return pair(info, grid.high_bit, held, received)[0].reshape(4, rows, width)

    return received, place


def second_hops(grid, held):
    if len(grid.orders[0]) == 2:
        return [held, grid.hop(held, 0)]
    for step in range(len(grid.orders[0])):
        held = jnp.concatenate([held, grid.hop(held, step)], 0)
    return [held]


def third_hops(grid, info, pieces):
    if len(pieces) == 1:
        return pieces
    held = join_pair(grid, info, pieces)
    return [held, grid.hop(held, 1), grid.swap_cores(held)]


def extra_rows(grid, info, pieces, start, keep):
    held = pieces[0][:, start : start + keep]
    return jnp.take(held, jnp.argsort(slots_of(grid, info)), axis=0)


def slots_of(grid, info):
    masks = jnp.stack(grid.masks(info[1])).astype(jnp.int32)[:, None]
    groups = jnp.arange(4, dtype=jnp.int32)[None, :] * grid.partner
    return ((masks ^ (info[2] & (grid.partner - 1))) | groups).reshape(-1)


def whole(grid, info, pieces, rows, count):
    if len(pieces) == 3:
        return [pieces[0], pieces[1], pieces[2], grid.swap_cores(pieces[1])]
    held = pieces[0][:, : count * rows]
    held = jnp.take(held, jnp.argsort(slots_of(grid, info)), axis=0).reshape(grid.n, count, rows, -1).transpose(1, 0, 2, 3)
    held = held.reshape(count, grid.n * rows, -1)
    return [held, grid.swap_cores(held)]


def split_kernel(grid, extra, info_ref, keep, received, *refs):
    outs = refs[-2:]
    count, rows = keep.shape[0], keep.shape[2]
    unused, unused, second, first_step, second_step = grid.place(info_ref)
    for g in range(4):
        for a in range(2):
            for b, out in ((second, outs[0]), (1 - second, outs[1])):
                source = 4 * g + a * first_step + b * second_step
                for j in range(count):
                    total = keep[j, source].astype(f32) + received[j, source].astype(f32)
                    out[g, a, j * rows : (j + 1) * rows] = total.astype(bf16)
                if extra:
                    out[g, a, count * rows :] = refs[0][source]


def added(a, b):
    return (a.astype(f32) + b.astype(f32)).astype(bf16)


def first_returns(grid, info, keep, received, more=None):
    blocks, n, rows, width = keep.shape
    depth = blocks * rows + (0 if more is None else more.shape[1])
    extra = [] if more is None else [more]
    if len(grid.orders[0]) != 2:
        total = added(keep, received).transpose(1, 0, 2, 3).reshape(n, blocks * rows, width)
        total = jnp.concatenate([total] + extra, 1)
        held = jnp.take(total, slots_of(grid, info), axis=0)
        for step in reversed(range(len(grid.orders[0]))):
            half = held.shape[0] // 2
            held = added(held[:half], grid.hop(held[half:], step))
        return [held]
    held, sent = call(
        functools.partial(split_kernel, grid, len(extra)),
        [((4, 2, depth, width), bf16)] * 2,
        [info, keep, received] + extra,
        [SMEM, VMEM, VMEM] + [VMEM] * len(extra),
        [VMEM] * 2,
        room=GLUE_LIMIT,
    )
    return [held, grid.hop(sent, 1)]


def merge_kernel(grid, info_ref, *refs):
    near, far = refs[-2:]
    bit = grid.place(info_ref)[1]
    start = 0
    for held, received in zip(refs[:-2:2], refs[1:-2:2], strict=True):
        at = slice(start, start + held.shape[2])
        for g in range(4):
            for which, out in ((bit, near), (1 - bit, far)):
                out[g, at] = added(held[g, which], received[g, which])
        start += held.shape[2]


def second_returns(grid, info, *parts):
    if len(parts[0]) == 1:
        return [jnp.concatenate([part[0] for part in parts], 1)]
    depth = sum(part[0].shape[2] for part in parts)
    near, far = call(
        functools.partial(merge_kernel, grid),
        [((4, depth, parts[0][0].shape[3]), bf16)] * 2,
        [info] + [array for part in parts for array in part],
        [SMEM] + [VMEM] * (2 * len(parts)),
        [VMEM] * 2,
        room=GLUE_LIMIT,
    )
    return [near, grid.hop(far, 0)]


def collect_kernel(grid, info_ref, held, received, *outs):
    group = grid.place(info_ref)[0]
    for k, out in enumerate(outs):
        at = jnp.bitwise_xor(group, k)
        out[...] = added(held[at], received[at])


def third_returns(grid, info, pieces):
    if len(pieces) == 1:
        group = jnp.right_shift(info[2], grid.high_bit - 1)
        totals = [
            lax.dynamic_index_in_dim(pieces[0], group ^ g, 0, keepdims=False) for g in range(4)
        ]
    else:
        totals = call(
            functools.partial(collect_kernel, grid),
            [(pieces[0].shape[1:], bf16)] * 4,
            [info] + pieces,
            [SMEM] + [VMEM] * 2,
            [VMEM] * 4,
            room=GLUE_LIMIT,
        )
    return [totals[0]] + [grid.across(totals[g], grid.groups[g]) for g in (3, 1, 2)]


def last_kernel(near_a, near_b, far_a, far_b, out):
    out[0] = (near_a[...].astype(f32) + near_b[...].astype(f32)).astype(bf16)
    out[1] = (far_a[...].astype(f32) + far_b[...].astype(f32)).astype(bf16)


def last_swap(grid, terms):
    mine = call(
        last_kernel,
        [((2,) + terms[0].shape, bf16)],
        terms,
        [VMEM] * 4,
        [VMEM],
        room=GLUE_LIMIT,
    )[0]
    return mine, grid.swap_cores(mine)


def nn(a, b):
    return lax.dot_general(a, b, (((1,), (0,)), ((), ())), preferred_element_type=f32)


def nt(a, b):
    return lax.dot_general(a, b, (((1,), (1,)), ((), ())), preferred_element_type=f32)


def tn(a, b):
    return lax.dot_general(a, b, (((0,), (0,)), ((), ())), preferred_element_type=f32)


def block_shapes(grid, count, rows, width, mixed=False):
    if rows % 16 or len(grid.orders[0]) != 2:
        return (4 * grid.n * rows, width) if mixed else (count, grid.n * rows, width)
    inner = (4, rows, width) if mixed else (rows, width)
    return ((4, 2, 2) if mixed else (count, 4, 2, 2)) + inner


def load_blocks(grid, info_ref, sources, blocks, sem, start=0, only=None, mixed=False):
    core = info_ref[1]
    middle = len(sources) // 2

    def load(which, refs):
        count = 1 if only is not None else 2 if mixed else blocks.shape[0] // 2
        first = 0 if only is not None else which * count
        if len(refs) == 1:
            for j in range(count):
                pltpu.make_async_copy(refs[0].at[start + j], blocks.at[first + j], sem).start()
            return
        rows = blocks.shape[-2]
        bit = jnp.right_shift(info_ref[2], 1 - which) & 1
        for j in range(count):
            for ref, b in ((refs[0], bit), (refs[1], 1 - bit)):
                source = ref.at[:, :, pl.ds((start + j) * rows, rows)]

                def low_first(b=b, j=j, source=source):
                    target = blocks.at[:, b, :, first + j] if mixed else blocks.at[first + j, :, b]
                    pltpu.make_async_copy(source, target, sem).start()

                def high_first(b=b, j=j, source=source):
                    target = (
                        blocks.at[:, :, b, first + j] if mixed else blocks.at[first + j, :, :, b]
                    )
                    pltpu.make_async_copy(source, target, sem).start()

                pl.when(which == 0)(low_first)
                pl.when(which != 0)(high_first)

    if len(sources) == 1:
        pltpu.make_async_copy(sources[0], blocks, sem).start()
    elif only is None:
        load(core, sources[:middle])
        load(1 - core, sources[middle:])
    else:
        pl.when(core == only)(lambda: load(only, sources[:middle]))
        pl.when(core != only)(lambda: load(only, sources[middle:]))
    return pltpu.make_async_copy(blocks, blocks, sem).wait


def matrix(values):
    return values.reshape(-1, values.shape[-1])


def load_inputs(info_ref, language, vision, language_far, vision_far, src_ref, oth_ref, sem):
    half = language.shape[0]

    def copies(mine, mine_far, other, other_far):
        return [
            pltpu.make_async_copy(mine, src_ref.at[pl.ds(0, half)], sem.at[0]),
            pltpu.make_async_copy(
                mine_far.at[pl.ds(0, half)], src_ref.at[pl.ds(half, half)], sem.at[1]
            ),
            pltpu.make_async_copy(other, oth_ref.at[pl.ds(0, half)], sem.at[2]),
            pltpu.make_async_copy(
                other_far.at[pl.ds(0, half)], oth_ref.at[pl.ds(half, half)], sem.at[3]
            ),
        ]

    @pl.when(info_ref[0] == 0)
    def _():
        for copy in copies(language, language_far, vision, vision_far):
            copy.start()

    @pl.when(info_ref[0] != 0)
    def _():
        for copy in copies(vision, vision_far, language, language_far):
            copy.start()

    def wait():
        for copy in copies(language, language_far, vision, vision_far):
            copy.wait()

    return wait


def store_blocks(core, blocks, keep, send, sem):
    count = keep.shape[0]
    copies = []
    for j in range(count):
        copies.append(pltpu.make_async_copy(blocks.at[core * count + j], keep.at[j], sem.at[j]))
        copies.append(
            pltpu.make_async_copy(
                blocks.at[(1 - core) * count + j], send.at[j], sem.at[count + j]
            )
        )
    for copy in copies:
        copy.start()

    def wait():
        for copy in copies:
            copy.wait()

    return wait


def normalised(values):
    mean_row = jnp.mean(values, axis=-1, keepdims=True)
    centred = values - mean_row
    variance = jnp.mean(centred * centred, axis=-1, keepdims=True)
    scale = lax.rsqrt(variance + norm_epsilon)
    return centred * scale, scale


def norm_back(values, grads, gain):
    unit, scale = normalised(values)
    scaled = grads * gain
    first = jnp.mean(scaled, axis=-1, keepdims=True)
    second = jnp.mean(scaled * unit, axis=-1, keepdims=True)
    return (scaled - first - unit * second) * scale, grads * unit


def lane_masks():
    lanes = lax.broadcasted_iota(jnp.int32, (128, 2 * HEAD), 1)
    left = (lanes < HEAD).astype(f32).astype(bf16)
    right = (lanes >= HEAD).astype(f32).astype(bf16)
    return lanes < HEAD, left, right


def two_heads(values, left, right):
    return jnp.concatenate([values * left, values * right], 0)


def softened(queries, keys_both, barred):
    scores = []
    for pair, keys in zip(queries, keys_both, strict=True):
        both = nt(pair, keys) * HEAD ** (-0.5)
        slots = both.shape[0]
        scores += [both[:, :slots], both[:, slots:]]
    scores = [jnp.where(barred, -1000000000.0, part) for part in scores]
    peaks = [jnp.max(part, axis=-1, keepdims=True) for part in scores]
    weights = [jnp.exp(part - peak) for part, peak in zip(scores, peaks, strict=True)]
    totals = [1.0 / jnp.sum(part, axis=-1, keepdims=True) for part in weights]
    return [part * total for part, total in zip(weights, totals, strict=True)]


def joined(parts, pair):
    return jnp.concatenate([part.astype(bf16) for part in parts[2 * pair : 2 * pair + 2]], 1)


def barred_slots(slots, count):
    return lax.broadcasted_iota(jnp.int32, (slots, slots), 1) >= count


def pages_of(rows, slots, body):
    def step(page, carry):
        body(page, pl.ds(pl.multiple_of(page * slots, slots), slots))
        return carry

    lax.fori_loop(0, rows // slots, step, 0, unroll=2)


def column_sum(values):
    return jnp.sum(values.astype(f32), axis=0, keepdims=True)


def attend_kernel(grid, cross, slots, held, at_table, info_ref, counts_ref, vec_ref, *refs):
    if cross:
        inputs, refs = refs[:4], refs[4:]
    else:
        residual_ref, low_ref = refs[:2]
        refs = refs[2:]
    sources, refs = refs[:held], refs[held:]

    def row(i):
        return vec_ref[at_table[i] : at_table[i] + 1, :]

    q_ref, k_ref, v_ref, o_ref, sum_ref, norm_ref, norm_low_ref = refs[:7]
    blocks, sem = refs[7:9]
    rows = q_ref.shape[0]
    half = rows // 2
    wait_blocks = load_blocks(grid, info_ref, sources, blocks, sem)
    if cross:
        src_ref, oth_ref, in_sem = refs[9:12]
        load_inputs(info_ref, *inputs, src_ref, oth_ref, in_sem)()
    else:
        src_ref = oth_ref = low_ref
    wait_blocks()
    width = q_ref.shape[1]
    q_ref[...] = (nn(src_ref[...], matrix(blocks[0])) + row(0)).astype(bf16)
    k_ref[...] = nn(oth_ref[...], matrix(blocks[1])).astype(bf16)
    v_ref[...] = (nn(oth_ref[...], matrix(blocks[2])) + row(1)).astype(bf16)
    unused, left, right = lane_masks()
    cuts = [slice(at, at + 128) for at in range(0, width, 128)]

    def one_page(page, at):
        soft = softened(
            [q_ref[at, cut] for cut in cuts],
            [two_heads(k_ref[at, cut], left, right) for cut in cuts],
            barred_slots(slots, counts_ref[page]),
        )
        for i, cut in enumerate(cuts):
            mixed = nn(joined(soft, i), two_heads(v_ref[at, cut], left, right))
            o_ref[at, cut] = mixed.astype(bf16)

    pages_of(rows, slots, one_page)
    residual = src_ref[...].astype(f32) if cross else residual_ref[...]
    total = residual + nn(o_ref[...], matrix(blocks[3])) + row(2)
    sum_ref[...] = total
    result = normalised(total)[0] * row(3) + row(4)
    norm_ref[...] = result
    norm_low_ref[...] = result.astype(bf16)


def attend(grid, cross, slots, info, counts, vectors, at_table, inputs, weights):
    width = weights[0].shape[-1]
    rows = counts.shape[0] * slots
    blocks = block_shapes(grid, 4, grid.rows, width)
    scratch = [pltpu.VMEM(blocks, bf16), pltpu.SemaphoreType.DMA]
    if cross:
        scratch += [pltpu.VMEM((rows, width), bf16)] * 2 + [pltpu.SemaphoreType.DMA((4,))]
    return call(
        functools.partial(attend_kernel, grid, cross, slots, len(weights), at_table),
        [((rows, width), bf16)] * 4 + [((rows, width), f32)] * 2 + [((rows, width), bf16)],
        [info, counts, vectors] + list(inputs) + list(weights),
        [SMEM, SMEM, VMEM] + ([HBM] * 4 if cross else [VMEM] * 2) + [HBM] * len(weights),
        [VMEM] * 7,
        scratch,
        flops=8 * rows * width * width + 8 * rows * slots * width,
        moved=4 * width * width * 2 + rows * width * 20,
    )


def hidden_kernel(grid, held, info_ref, shift_ref, low_ref, *refs):
    sources = refs[:held]
    active_ref, slope_ref, blocks, sem = refs[held:]
    load_blocks(grid, info_ref, sources, blocks, sem)()
    width = low_ref.shape[1]
    for b in range(4):
        at = slice(b * width, (b + 1) * width)
        hidden = nn(low_ref[...], matrix(blocks[b])) + shift_ref[0:1, at]
        square = hidden * hidden
        bent = jnp.tanh(0.7978845608028654 * (hidden + 0.044715 * square * hidden))
        active_ref[:, at] = (0.5 * hidden * (1.0 + bent)).astype(bf16)
        slope = 0.5 * (1.0 + bent) + 0.5 * hidden * (1.0 - bent * bent) * (
            0.7978845608028654 * (1.0 + 3.0 * 0.044715 * square)
        )
        slope_ref[:, at] = slope.astype(bf16)


def hidden_layer(grid, info, shift, low, weights):
    rows, width = low.shape
    return call(
        functools.partial(hidden_kernel, grid, len(weights)),
        [((rows, 4 * width), bf16)] * 2,
        [info, shift, low] + list(weights),
        [SMEM, VMEM, VMEM] + [HBM] * len(weights),
        [VMEM, VMEM],
        [pltpu.VMEM(block_shapes(grid, 4, grid.rows, width), bf16), pltpu.SemaphoreType.DMA],
        flops=8 * rows * width * width,
        moved=8 * width * width + rows * width * 18,
    )


def store_wide(core, wide, keep, send, sem):
    copies = []
    for j in range(2):
        for which, target in ((core, keep), (1 - core, send)):
            copies.append(pltpu.make_async_copy(wide.at[:, 2 * which + j], target.at[j], sem))
    for copy in copies:
        copy.start()
    pltpu.make_async_copy(wide, wide, sem).wait()


def branch_kernel(grid, held, info_ref, vec_ref, active_ref, residual_ref, *refs):
    sources = refs[:held]
    sum_ref, norm_ref, far_ref, wide, sem = refs[held:]
    load_blocks(grid, info_ref, sources, wide, sem, mixed=True)()
    half = residual_ref.shape[0] // 2
    total = residual_ref[...] + nn(active_ref[...], matrix(wide[...])) + vec_ref[12:13, :]
    sum_ref[...] = total
    result = normalised(total)[0] * vec_ref[8:9, :] + vec_ref[11:12, :]
    norm_ref[...] = result[:half]
    far_ref[...] = result[half:].astype(bf16)


def branch_layer(grid, info, vectors, active, residual, weights):
    rows, width = residual.shape
    return call(
        functools.partial(branch_kernel, grid, len(weights)),
        [((rows, width), f32), ((rows // 2, width), f32), ((rows // 2, width), bf16)],
        [info, vectors, active, residual] + list(weights),
        [SMEM, VMEM, VMEM, VMEM] + [HBM] * len(weights),
        [VMEM] * 3,
        [pltpu.VMEM(block_shapes(grid, 4, grid.rows, width, True), bf16), pltpu.SemaphoreType.DMA],
        flops=8 * rows * width * width,
        moved=8 * width * width + rows * width * 20,
    )


def gate_kernel(grid, held, info_ref, shift_ref, third_ref, far_ref, cotangent_ref, *refs):
    sources = refs[:held]
    united_ref, grad_own_ref, grad_far_ref, grad_shift_ref, keep_ref, send_ref = refs[held : held + 6]
    blocks, sem, grads, mix_ref, low_ref, out_sem = refs[held + 6 :]
    load_blocks(grid, info_ref, sources, blocks, sem, 2)()
    first = info_ref[0] == 0
    low_ref[...] = third_ref[...].astype(bf16)
    logits = nn(low_ref[...], matrix(blocks[0])) + nn(far_ref[...], matrix(blocks[1])) + shift_ref[13:14, :]
    mixing = 1.0 / (1.0 + jnp.exp(-logits))
    share = jnp.where(first, mixing, 1.0 - mixing)
    mine, other = third_ref[...], far_ref[...].astype(f32)
    united_ref[...] = (share * mine + (1.0 - share) * other).astype(bf16)
    cotangent = cotangent_ref[...].astype(f32)
    gap = jnp.where(first, mine - other, other - mine)
    grad = (cotangent * gap * mixing * (1.0 - mixing)).astype(bf16)
    mix_ref[...] = grad
    grad_shift_ref[0:1, :] = column_sum(grad)
    direct = cotangent * share
    grad_own_ref[...] = direct + nt(mix_ref[...], matrix(blocks[0]))
    grad_far_ref[...] = (cotangent - direct + nt(mix_ref[...], matrix(blocks[1]))).astype(bf16)
    grads[0] = tn(low_ref[...], mix_ref[...]).astype(bf16)
    grads[1] = tn(far_ref[...], mix_ref[...]).astype(bf16)
    store_blocks(info_ref[1], grads, keep_ref, send_ref, out_sem)()


def gate_layer(grid, info, shift, third, far, cotangent, weights):
    rows, width = third.shape
    blocks = (2, width, width)
    return call(
        functools.partial(gate_kernel, grid, len(weights)),
        [
            ((rows, width), bf16),
            ((rows, width), f32),
            ((rows, width), bf16),
            ((8, width), f32),
            ((1,) + blocks[1:], bf16),
            ((1,) + blocks[1:], bf16),
        ],
        [info, shift, third, far, cotangent] + list(weights),
        [SMEM] + [VMEM] * 4 + [HBM] * len(weights),
        [VMEM] * 4 + [HBM] * 2,
        [
            pltpu.VMEM(block_shapes(grid, 2, grid.rows, width), bf16),
            pltpu.SemaphoreType.DMA,
            pltpu.VMEM(blocks, bf16),
            pltpu.VMEM((rows, width), bf16),
            pltpu.VMEM((rows, width), bf16),
            pltpu.SemaphoreType.DMA((2,)),
        ],
        flops=12 * rows * width * width,
        moved=8 * width * width + rows * width * 14,
    )


def branch_back_kernel(
    wide_out,
    info_ref,
    gain_ref,
    sum_ref,
    grad_own_ref,
    grad_far_ref,
    active_ref,
    grad_sum_ref,
    grad_low_ref,
    vec_ref,
    *refs,
):
    rows, width = sum_ref.shape
    half = rows // 2
    vec_ref[...] = jnp.zeros_like(vec_ref)
    for offset, grads_ref in ((0, grad_own_ref), (half, grad_far_ref)):
        at = slice(offset, offset + half)
        grads = grads_ref[...].astype(f32)
        back, gain_rows = norm_back(sum_ref[at, :], grads, gain_ref[8:9, :])
        low = back.astype(bf16)
        grad_sum_ref[at, :] = back
        grad_low_ref[at, :] = low
        vec_ref[0:1, :] += column_sum(gain_rows)
        vec_ref[1:2, :] += column_sum(grads)
        vec_ref[2:3, :] += column_sum(low)
    wide, sem = refs[-2:]
    for b in range(4):
        at = slice(b * width, (b + 1) * width)
        part = tn(active_ref[:, at], grad_low_ref[...]).astype(bf16)
        if wide_out:
            devices = wide.shape[0] // 4
            wide[b * devices : (b + 1) * devices] = part.reshape((devices,) + wide.shape[1:])
        else:
            wide[at, :] = part
    if wide_out:
        store_wide(info_ref[1], wide, refs[0], refs[1], sem)
    else:
        copy = pltpu.make_async_copy(wide, refs[0], sem)
        copy.start()
        copy.wait()


def branch_back(grid, info, gain, sums, grad_own, grad_far, active, piece):
    rows, width = sums.shape
    wide_out = piece % 16 == 0
    target = (2, grid.n, piece, width) if wide_out else (4 * width, width)
    outs = [(target, bf16)] * (2 if wide_out else 1)
    return call(
        functools.partial(branch_back_kernel, wide_out),
        [((rows, width), f32), ((rows, width), bf16), ((8, width), f32)] + outs,
        [info, gain, sums, grad_own, grad_far, active],
        [SMEM] + [VMEM] * 5,
        [VMEM] * 3 + [HBM] * len(outs),
        [
            pltpu.VMEM((grid.n, 4, piece, width) if wide_out else (4 * width, width), bf16),
            pltpu.SemaphoreType.DMA,
        ],
        flops=8 * rows * width * width,
        moved=8 * width * width + rows * width * 24,
    )


def hidden_back_kernel(grid, held, info_ref, grad_low_ref, slope_ref, low_ref, *refs):
    core = info_ref[1]
    grad_hidden_ref, vec_ref, keep_ref, send_ref, wide, sem, grads, out_sem = refs[held:]
    load_blocks(grid, info_ref, refs[:held], wide, sem, mixed=True)()
    whole_wide = matrix(wide[...])
    width = low_ref.shape[1]
    for b in range(4):
        at = slice(b * width, (b + 1) * width)
        low = (nt(grad_low_ref[...], whole_wide[at, :]) * slope_ref[:, at].astype(f32)).astype(bf16)
        grad_hidden_ref[:, at] = low
        vec_ref[0:1, at] = column_sum(low)
        grads[b] = tn(low_ref[...], low).astype(bf16)
    store_blocks(core, grads, keep_ref, send_ref, out_sem)()


def hidden_back(grid, info, grad_low, slope, low, weights):
    rows, width = low.shape
    blocks = (4, width, width)
    return call(
        functools.partial(hidden_back_kernel, grid, len(weights)),
        [((rows, 4 * width), bf16), ((8, 4 * width), f32)] + [((2,) + blocks[1:], bf16)] * 2,
        [info, grad_low, slope, low] + list(weights),
        [SMEM] + [VMEM] * 3 + [HBM] * len(weights),
        [VMEM] * 2 + [HBM] * 2,
        [
            pltpu.VMEM(block_shapes(grid, 4, grid.rows, width, True), bf16),
            pltpu.SemaphoreType.DMA,
            pltpu.VMEM(blocks, bf16),
            pltpu.SemaphoreType.DMA((4,)),
        ],
        flops=16 * rows * width * width,
        moved=16 * width * width + rows * width * 30,
    )


def second_back_kernel(
    grid, held, info_ref, gain_ref, sum_ref, grad_ref, grad_hidden_ref, *refs
):
    grad_sum_ref, vec_ref, blocks, sem = refs[held:]
    load_blocks(grid, info_ref, refs[:held], blocks, sem)()
    width = sum_ref.shape[1]
    total = grad_ref[...]
    for b in range(4):
        total += nt(grad_hidden_ref[:, b * width : (b + 1) * width], matrix(blocks[b]))
    grad_sum_ref[...] = norm_back_into(vec_ref, sum_ref[...], total, gain_ref[7:8, :])


def norm_back_into(vec_ref, sums, grads, gain):
    back, gain_rows = norm_back(sums, grads, gain)
    vec_ref[0:1, :] = column_sum(gain_rows)
    vec_ref[1:2, :] = column_sum(grads)
    return back


def second_back(grid, info, gain, sums, grads, grad_hidden, weights):
    rows, width = sums.shape
    return call(
        functools.partial(second_back_kernel, grid, len(weights)),
        [((rows, width), f32), ((8, width), f32)],
        [info, gain, sums, grads, grad_hidden] + list(weights),
        [SMEM] + [VMEM] * 4 + [HBM] * len(weights),
        [VMEM] * 2,
        [pltpu.VMEM(block_shapes(grid, 4, grid.rows, width), bf16), pltpu.SemaphoreType.DMA],
        flops=8 * rows * width * width,
        moved=8 * width * width + rows * width * 20,
    )


def scores_back_kernel(grid, slots, held, info_ref, counts_ref, grad_ref, *refs):
    q_ref, k_ref, v_ref, o_ref = refs[:4]
    dq_ref, dk_ref, dv_ref, vec_ref, out_grad_ref, weight, sem, low_grad, grad_o = refs[4 + held :]
    wait_block = load_blocks(grid, info_ref, refs[4 : 4 + held], weight, sem, 1, 1)
    rows, width = q_ref.shape
    low = grad_ref[...].astype(bf16)
    low_grad[...] = low
    vec_ref[2:3, :] = column_sum(low)
    out_grad_ref[...] = tn(o_ref[...], low_grad[...]).astype(bf16)
    wait_block()
    grad_o[...] = nt(low_grad[...], matrix(weight[0])).astype(bf16)
    left_lanes, left, right = lane_masks()
    cuts = [slice(at, at + 128) for at in range(0, width, 128)]

    def one_page(page, at):
        keys = [two_heads(k_ref[at, cut], left, right) for cut in cuts]
        soft = softened(
            [q_ref[at, cut] for cut in cuts], keys, barred_slots(slots, counts_ref[page])
        )
        grad_soft = []
        for cut in cuts:
            both = nt(grad_o[at, cut], two_heads(v_ref[at, cut], left, right))
            grad_soft += [both[:, :slots], both[:, slots:]]
        weighted = [a * b for a, b in zip(soft, grad_soft, strict=True)]
        sums = [jnp.sum(part, axis=-1, keepdims=True) for part in weighted]
        grad_scores = [w - p * t for w, p, t in zip(weighted, soft, sums, strict=True)]
        for i, cut in enumerate(cuts):
            dv = tn(joined(soft, i), grad_o[at, cut])
            dv_ref[at, cut] = jnp.where(left_lanes, dv[:slots], dv[slots:]).astype(bf16)
        for i, cut in enumerate(cuts):
            pair = joined(grad_scores, i)
            dq_ref[at, cut] = (nn(pair, keys[i]) * HEAD ** (-0.5)).astype(bf16)
            dk = tn(pair, q_ref[at, cut]) * HEAD ** (-0.5)
            dk_ref[at, cut] = jnp.where(left_lanes, dk[:slots], dk[slots:]).astype(bf16)

    pages_of(rows, slots, one_page)
    vec_ref[0:1, :] = column_sum(dq_ref[...])
    vec_ref[1:2, :] = column_sum(dv_ref[...])


def scores_back(grid, slots, info, counts, grad, saved, weights):
    rows, width = grad.shape
    full = pltpu.VMEM((rows, width), bf16)
    return call(
        functools.partial(scores_back_kernel, grid, slots, len(weights)),
        [((rows, width), bf16)] * 3 + [((8, width), f32), ((width, width), bf16)],
        [info, counts, grad] + list(saved) + list(weights),
        [SMEM, SMEM] + [VMEM] * 5 + [HBM] * len(weights),
        [VMEM] * 5,
        [
            pltpu.VMEM(block_shapes(grid, 1, grid.rows, width), bf16),
            pltpu.SemaphoreType.DMA,
            full,
            full,
        ],
        flops=4 * rows * width * width + 24 * rows * slots * width,
        moved=4 * width * width + rows * width * 18,
    )


def project_back_kernel(grid, cross, held, info_ref, gain_ref, grad_ref, *refs):
    dq_ref, dk_ref, dv_ref, out_grad_ref = refs[:4]
    refs = refs[4:]
    if cross:
        inputs = refs[:4]
        sources, refs = refs[4 : 4 + held], refs[4 + held :]
        mine_ref, other_ref, far_ref, keep_ref, send_ref = refs[:5]
        blocks, sem, grads, out_sem, src_ref, oth_ref, in_sem = refs[5:]
    else:
        src_ref, sum_ref = refs[:2]
        oth_ref = src_ref
        sources, refs = refs[2 : 2 + held], refs[2 + held :]
        out_ref, vec_ref, keep_ref, send_ref, blocks, sem, grads, out_sem = refs
    half = grad_ref.shape[0] // 2
    if cross:
        load_inputs(info_ref, *inputs, src_ref, oth_ref, in_sem)()
    wait_blocks = load_blocks(grid, info_ref, sources, blocks, sem)
    grads[0] = tn(src_ref[...], dq_ref[...]).astype(bf16)
    grads[1] = tn(oth_ref[...], dk_ref[...]).astype(bf16)
    grads[2] = tn(oth_ref[...], dv_ref[...]).astype(bf16)
    grads[3] = out_grad_ref[...]
    wait_stores = store_blocks(info_ref[1], grads, keep_ref, send_ref, out_sem)
    wait_blocks()
    mine = grad_ref[...] + nt(dq_ref[...], matrix(blocks[0]))
    other = nt(dk_ref[...], matrix(blocks[1])) + nt(dv_ref[...], matrix(blocks[2]))
    if cross:
        mine_ref[...] = mine[:half]
        other_ref[...] = other[:half]
        far_ref[:half] = other[half:].astype(bf16)
        far_ref[half:] = mine[half:].astype(bf16)
    else:
        vec_ref[...] = jnp.zeros_like(vec_ref)
        out_ref[...] = norm_back_into(vec_ref, sum_ref[...], mine + other, gain_ref[6:7, :])
    wait_stores()


def project_back(grid, cross, info, gain, grad, parts, inputs, weights):
    rows, width = grad.shape
    blocks = (4, width, width)
    scratch = [
        pltpu.VMEM(block_shapes(grid, 4, grid.rows, width), bf16),
        pltpu.SemaphoreType.DMA,
        pltpu.VMEM(blocks, bf16),
        pltpu.SemaphoreType.DMA((4,)),
    ]
    half = (rows // 2, width)
    if cross:
        full = pltpu.VMEM((rows, width), bf16)
        scratch += [full, full, pltpu.SemaphoreType.DMA((4,))]
        outs = [(half, f32), (half, f32), ((rows, width), bf16)]
    else:
        outs = [((rows, width), f32), ((8, width), f32)]
    return call(
        functools.partial(project_back_kernel, grid, cross, len(weights)),
        outs + [((2,) + blocks[1:], bf16)] * 2,
        [info, gain, grad] + list(parts) + list(inputs) + list(weights),
        [SMEM] + [VMEM] * 6 + ([HBM] * 4 if cross else [VMEM] * 2) + [HBM] * len(weights),
        [VMEM] * len(outs) + [HBM] * 2,
        scratch,
        flops=12 * rows * width * width,
        moved=14 * width * width + rows * width * 18,
    )


SPOTS = (
    [(i, 0, 1) for i in range(3)]
    + [(i, 128, 1) for i in range(3)]
    + [(i, 256, 1) for i in range(3)]
    + [(i, 384, 1) for i in range(3)]
    + [(4, 0, 1), (4, 128, 1), (3, 0, 4)]
)
EXTRA = 16


def lay_vectors(cross_bias, self_bias, gains, shifts, out_bias, gate_bias, in_bias, width):
    def at(values, row, lane):
        depth, length = values.shape[1:]
        return jnp.pad(
            values, ((0, 0), (row, EXTRA - row - depth), (lane, width - lane - length))
        )

    gate = jnp.broadcast_to(gate_bias[None, None], (2, 1) + gate_bias.shape)
    return (
        at(cross_bias, 0, 0)
        + at(self_bias, 0, 128)
        + at(gains, 0, 256)
        + at(shifts, 0, 384)
        + at(out_bias[:, None], 4, 0)
        + at(gate, 4, 128)
        + at(in_bias[:, None], 3, 0)
    )


def unlay_kernel(grid, start, info_ref, mine_ref, other_ref, table_ref, wide_ref, held, found, sem):
    copies = []
    for k, ref in enumerate((mine_ref, other_ref)):
        source = ref.at[:, :, pl.ds(start, EXTRA)]
        copies.append(pltpu.make_async_copy(source, held.at[k], sem.at[k]))
    for copy in copies:
        copy.start()
    for copy in copies:
        copy.wait()
    unused, unused, second, first_step, second_step = grid.place(info_ref)
    for g in range(4):
        for a in range(2):
            for k, b in ((0, second), (1, 1 - second)):
                place = 4 * g + a * first_step + b * second_step
                found[place] = held[k, g, a].astype(f32)
    rows = grid.rows
    for p in range(grid.n):
        for i, (row, lane, unused) in enumerate(SPOTS[:-1]):
            table_ref[i : i + 1, p * rows : (p + 1) * rows] = found[p, row : row + 1, lane : lane + rows]
        row, lane, length = SPOTS[-1]
        wide_ref[0:1, p * length * rows : (p + 1) * length * rows] = found[
            p, row : row + 1, lane : lane + length * rows
        ]


def unlay_vectors(grid, info, pieces, start):
    width = pieces[0].shape[-1]
    rows = grid.rows
    if len(pieces) == 1:
        found = extra_rows(grid, info, pieces, start, EXTRA).astype(f32)
        parts = [
            found[:, row, lane : lane + length * rows].reshape(-1) for row, lane, length in SPOTS
        ]
        table = jnp.pad(jnp.stack(parts[:-1]), ((0, 2), (0, 0)))
        return table, jnp.pad(parts[-1][None], ((0, 7), (0, 0)))
    return call(
        functools.partial(unlay_kernel, grid, start),
        [((16, width), f32), ((8, 4 * width), f32)],
        [info] + pieces[:2],
        [SMEM, HBM, HBM],
        [VMEM, VMEM],
        [
            pltpu.VMEM((2, 4, 2, EXTRA, width), bf16),
            pltpu.VMEM((grid.n, EXTRA, width), f32),
            pltpu.SemaphoreType.DMA((2,)),
        ],
        room=GLUE_LIMIT,
    )


def relay_kernel(grid, where, *refs):
    out, held = refs[-2:]
    rows = grid.rows
    held[...] = jnp.zeros_like(held)
    for p in range(grid.n):
        for (table, i), (row, lane, length) in zip(where, SPOTS, strict=True):
            size = length * rows
            held[p, row : row + 1, lane : lane + size] = refs[table][i : i + 1, p * size : (p + 1) * size]
    out[...] = held[...].astype(bf16)


def relay_vectors(grid, tables, where):
    width = tables[0].shape[1]
    rows = grid.rows
    if rows % 16:
        out = jnp.zeros((grid.n, EXTRA, width), f32)
        for (table, i), (row, lane, length) in zip(where, SPOTS, strict=True):
            part = tables[table][i].reshape(grid.n, length * rows)
            out = out.at[:, row, lane : lane + length * rows].set(part)
        return out.astype(bf16)
    return call(
        functools.partial(relay_kernel, grid, where),
        [((grid.n, EXTRA, width), bf16)],
        tables,
        [VMEM] * len(tables),
        [VMEM],
        [pltpu.VMEM((grid.n, EXTRA, width), f32)],
        room=GLUE_LIMIT,
    )[0]


def on_device(
    grid,
    language_in,
    vision_in,
    language_count,
    vision_count,
    cross_qkv,
    cross_proj,
    cross_bias,
    norm_gain,
    norm_bias,
    self_qkv,
    self_proj,
    self_bias,
    ffn_in,
    ffn_in_bias,
    ffn_out,
    ffn_out_bias,
    gate_weight,
    gate_bias,
    cotangent,
):
    n = grid.n
    grid.rows = cross_proj.shape[1]
    me = lax.axis_index("dp")
    core = lax.axis_index("rep")
    side = ((me // grid.high) ^ (me // grid.partner)) & 1
    first = side == 0
    info = jnp.stack([side, core, me]).astype(jnp.int32)
    rows, width = cross_proj.shape[1:]
    dim = n * rows
    pages, slots = language_in.shape[:2]
    wide_ok = rows % 16 == 0

    def own(pair):
        return lax.dynamic_index_in_dim(pair, side, 0, keepdims=False)

    def other(pair):
        return lax.dynamic_index_in_dim(pair, 1 - side, 0, keepdims=False)

    vectors = lay_vectors(
        cross_bias, self_bias, norm_gain, norm_bias, ffn_out_bias, gate_bias, ffn_in_bias, width
    )
    groups = [
        [cross_qkv[:, 0], cross_qkv[:, 1], vectors, cross_qkv[:, 2], cross_proj, vectors],
        [self_qkv[:, 0], self_qkv[:, 1], self_qkv[:, 2], self_proj],
        [ffn_in[:, :, i * width : (i + 1) * width] for i in range(4)],
        [ffn_out[:, i * rows : (i + 1) * rows] for i in range(2)]
        + [gate_weight]
        + [ffn_out[:, i * rows : (i + 1) * rows] for i in range(2, 4)]
        + [gate_weight[::-1]],
    ]

    def shards(blocks):
        half = len(blocks) // 2
        parts = [jnp.concatenate(blocks[:half], 1), jnp.concatenate(blocks[half:], 1)]
        mine = lax.dynamic_index_in_dim(jnp.stack(parts), core, 0, keepdims=False)
        return own(mine), other(mine)

    sent = [shards(blocks) for blocks in groups]
    later = [jnp.concatenate([part[k] for part in sent[1:]], 0) for k in range(2)]
    parts = [part[0].shape[0] for part in sent[1:]]
    language = language_in.reshape(pages * slots, width)
    vision = vision_in.reshape(pages * slots, width)
    counts_mine = jnp.stack([language_count, vision_count])
    counts_wide = jnp.pad(counts_mine.astype(bf16), ((0, 14), (0, width - pages)))
    vision_more = jnp.concatenate([vision, counts_wide], 0)

    t0 = grid.across(sent[0][1], grid.partner)
    t0, later = tie(t0, later)
    t1, place_t = meet(grid, info, pair(info, grid.high_bit - 1, sent[0][0], t0)[0])
    later_far = grid.across(later[1], grid.partner)
    t1, later_far, language = tie(t1, later_far, language)
    t2 = second_hops(grid, place_t())
    u0, w0, x0 = pair(info, grid.high_bit - 1, later[0], later_far, parts)
    u1, place_u = meet(grid, info, u0)
    language_far = grid.across(language, grid.partner)
    t2, u1, language_far, vision_more, w0 = tie(t2, u1, language_far, vision_more, w0)
    t3 = third_hops(grid, info, t2)
    u2 = second_hops(grid, place_u())
    w1, place_w = meet(grid, info, w0)
    vision_far = grid.across(vision_more, grid.partner)
    t3, u2, w1, vision_far, x0 = tie(t3, u2, w1, vision_far, x0)
    cross_w = whole(grid, info, t3, rows, 2)
    table, ffn_in_shift = unlay_vectors(grid, info, t3, 2 * rows)
    counts_far = vision_far[pages * slots :, :pages][:2].astype(jnp.int32)
    counts = jnp.concatenate([own(counts_mine), own(counts_far)])
    other_counts = jnp.concatenate([other(counts_mine), other(counts_far)])
    inputs = [language, vision, language_far, vision_far]
    u3 = third_hops(grid, info, u2)
    w2 = second_hops(grid, place_w())
    x1, place_x = meet(grid, info, x0)
    cq, ck, cv, co, first_sum, first_norm, first_low = attend(
        grid, True, slots, info, other_counts, table, (0, 1, 2, 6, 9), inputs, cross_w
    )
    first_norm, first_low, u3, w2, x1 = tie(first_norm, first_low, u3, w2, x1)
    self_w = whole(grid, info, u3, rows, 2)
    w3 = third_hops(grid, info, w2)
    x2 = second_hops(grid, place_x())
    sq, sk, sv, so, second_sum, second_norm, second_low = attend(
        grid,
        False,
        slots,
        info,
        counts,
        table,
        (3, 4, 5, 7, 10),
        [first_norm, first_low],
        self_w,
    )
    second_norm, second_low, w3, x2 = tie(second_norm, second_low, w3, x2)
    in_w = whole(grid, info, w3, rows, 2)
    x3 = third_hops(grid, info, x2)
    active, slope = hidden_layer(grid, info, ffn_in_shift, second_low, in_w)
    active, second_norm, x3 = tie(active, second_norm, x3)
    gate_w = out_w = whole(grid, info, x3, rows, 3)
    if len(out_w) == 2:
        both = jnp.where(core == 0, jnp.stack(out_w), jnp.stack(out_w[::-1]))[:, :2]
        both = both.reshape(4, n, rows, width).transpose(1, 0, 2, 3)
        out_w = [both.reshape(4 * dim, width)]
    third_sum, third_own, third_send = branch_layer(
        grid, info, table, active, second_norm, out_w
    )
    third_far = grid.across(third_send, grid.partner)
    cotangent_rows = cotangent.reshape(pages * slots, width)
    united, grad_third_own, grad_third_send, grad_gate_shift, gate_keep, gate_send = gate_layer(
        grid, info, table, third_own, third_far, cotangent_rows, gate_w
    )

    def by_piece(values):
        return values.reshape(values.shape[0], n, rows, width)

    gate_keep, gate_send = by_piece(gate_keep), by_piece(gate_send)
    gate_got = grid.swap_cores(gate_send)
    grad_third_far = grid.across(grad_third_send, grid.partner)
    gate = first_returns(grid, info, gate_keep, gate_got)
    gate[0], grad_third_far = tie(gate[0], grad_third_far)
    grad_third_sum, grad_branch_low, vec_third, *out_grads = branch_back(
        grid, info, table, third_sum, grad_third_own, grad_third_far, active, rows
    )
    if len(out_grads) == 1:
        by_core = out_grads[0].reshape(n, 2, 2, rows, width).transpose(1, 2, 0, 3, 4)
        out_grads = [
            lax.dynamic_index_in_dim(by_core, c, 0, keepdims=False) for c in (core, 1 - core)
        ]
    out_keep, out_send = out_grads
    gate, grad_branch_low, out_keep, out_send = tie(gate, grad_branch_low, out_keep, out_send)
    out_got = grid.swap_cores(out_send)
    grad_hidden, vec_hidden, in_keep, in_send = hidden_back(
        grid, info, grad_branch_low, slope, second_low, out_w
    )
    out_got, grad_hidden, in_keep, in_send = tie(out_got, grad_hidden, in_keep, in_send)
    in_keep, in_send = by_piece(in_keep), by_piece(in_send)
    in_got = grid.swap_cores(in_send)
    outs = first_returns(grid, info, out_keep, out_got)
    grad_second_sum, vec_second = second_back(
        grid, info, table, second_sum, grad_third_sum, grad_hidden, in_w
    )
    outs, in_got, grad_second_sum = tie(outs, in_got, grad_second_sum)
    ins = first_returns(grid, info, in_keep, in_got)
    outs = second_returns(grid, info, gate, outs)
    *self_parts, vec_self, self_out = scores_back(
        grid, slots, info, counts, grad_second_sum, [sq, sk, sv, so], self_w
    )
    self_parts.append(self_out)
    outs, self_parts = tie(outs, self_parts)
    outs = third_returns(grid, info, outs)
    grad_first_sum, vec_first, self_keep, self_send = project_back(
        grid, False, info, table, grad_second_sum, self_parts, [first_low, first_sum], self_w
    )
    ins, outs, grad_first_sum, self_keep, self_send = tie(
        ins, outs, grad_first_sum, self_keep, self_send
    )
    self_keep, self_send = by_piece(self_keep), by_piece(self_send)
    self_got = grid.swap_cores(self_send)
    ins = second_returns(grid, info, ins)
    *cross_parts, vec_cross, cross_out = scores_back(
        grid, slots, info, other_counts, grad_first_sum, [cq, ck, cv, co], cross_w
    )
    cross_parts.append(cross_out)
    ins, self_got, cross_parts, vec_cross = tie(ins, self_got, cross_parts, vec_cross)
    tables = [vec_cross, vec_self, vec_first, vec_second, vec_third, grad_gate_shift, vec_hidden]
    where = [(0, 0), (0, 1), (0, 2), (1, 0), (1, 1), (1, 2)]
    where += [(2, 0), (3, 0), (4, 0), (2, 1), (3, 1), (4, 1), (4, 2), (5, 0), (6, 0)]
    grad_vec = relay_vectors(grid, tables, where)
    selfs = first_returns(grid, info, self_keep, self_got, grad_vec)
    ins = third_returns(grid, info, ins)
    grad_mine, grad_theirs, outgoing, cross_keep, cross_send = project_back(
        grid, True, info, table, grad_first_sum, cross_parts, inputs, cross_w
    )
    selfs, ins, outgoing, cross_keep, cross_send = tie(selfs, ins, outgoing, cross_keep, cross_send)
    cross_keep, cross_send = by_piece(cross_keep), by_piece(cross_send)
    cross_got = grid.swap_cores(cross_send)
    selfs = second_returns(grid, info, selfs)
    incoming = grid.across(outgoing, grid.partner)
    out_done = last_swap(grid, outs)
    selfs, cross_got, out_done = tie(selfs, cross_got, out_done)
    crosses = first_returns(grid, info, cross_keep, cross_got)
    selfs = third_returns(grid, info, selfs)
    in_done = last_swap(grid, ins)
    crosses, selfs, incoming, in_done = tie(crosses, selfs, incoming, in_done)
    crosses = second_returns(grid, info, crosses)
    self_done = last_swap(grid, selfs)
    crosses, self_done = tie(crosses, self_done)
    crosses = third_returns(grid, info, crosses)
    cross_done = last_swap(grid, crosses)
    page_shape = language_in.shape
    got = incoming.astype(f32)
    grad_mine = grad_mine + got[: pages * slots]
    grad_theirs = grad_theirs + got[pages * slots :]
    grad_language = jnp.where(first, grad_mine, grad_theirs).astype(bf16).reshape(page_shape)
    grad_vision = jnp.where(first, grad_theirs, grad_mine).astype(bf16).reshape(page_shape)

    def sides(near, far):
        return jnp.where(first, jnp.stack([near, far]), jnp.stack([far, near]))

    def finished(done, count, start=0):
        mine, far = [part[:, start * rows : (start + count) * rows] for part in done]
        mine, far = [part.reshape(2, count, rows, width) for part in (mine, far)]
        both = jnp.where(core == 0, jnp.concatenate([mine, far], 1), jnp.concatenate([far, mine], 1))
        return both.astype(f32)

    def by_side(both):
        return jnp.where(first, both, both[::-1])

    cross_all = by_side(finished(cross_done, 2))
    self_all = by_side(finished(self_done, 2))
    in_all = by_side(finished(in_done, 2))
    gate_all = finished(out_done, 1)
    out_all = by_side(finished(out_done, 2, 1))
    gate_both = sides(gate_all[0, 0] + gate_all[1, 1], gate_all[0, 1] + gate_all[1, 0])
    vec_sum = (self_done[0].astype(f32) + self_done[1].astype(f32))[:, 2 * rows :]
    vec_both = by_side(vec_sum)
    gate_vec = vec_sum[0, 4, 128 : 128 + rows] + vec_sum[1, 4, 128 : 128 + rows]
    return (
        united.reshape(page_shape),
        grad_language,
        grad_vision,
        cross_all[:, 0:3],
        cross_all[:, 3],
        vec_both[:, 0:3, :rows],
        vec_both[:, 0:3, 256 : 256 + rows],
        vec_both[:, 0:3, 384 : 384 + rows],
        self_all[:, 0:3],
        self_all[:, 3],
        vec_both[:, 0:3, 128 : 128 + rows],
        in_all.transpose(0, 2, 1, 3).reshape(2, rows, 4 * width),
        vec_both[:, 3, : 4 * rows],
        out_all.reshape(2, 4 * rows, width),
        vec_both[:, 4, :rows],
        gate_both,
        gate_vec,
    )


def solution(mesh):
    whole = P(("dp", "rep"), None, None)
    weights = (
        P(None, None, "dp", None),
        P(None, "dp", None),
        P(None, None, "dp"),
        P(None, None, "dp"),
        P(None, None, "dp"),
        P(None, None, "dp", None),
        P(None, "dp", None),
        P(None, None, "dp"),
        P(None, "dp", None),
        P(None, "dp"),
        P(None, "dp", None),
        P(None, "dp"),
        P(None, "dp", None),
        P("dp"),
    )
    return jax.shard_map(
        functools.partial(on_device, Grid(mesh)),
        mesh=mesh,
        in_specs=(whole, whole, P(("dp", "rep")), P(("dp", "rep"))) + weights + (whole,),
        out_specs=(whole, whole, whole) + weights,
        check_vma=False,
    )
```

```python
import functools

import jax
import jax.numpy as jnp
from jax import lax
from jax.experimental import pallas as pl
from jax.experimental.pallas import tpu as pltpu
from jax.sharding import PartitionSpec as P

HEADS = 12
HEAD = 64
norm_epsilon = 1e-05
bf16 = jnp.bfloat16
f32 = jnp.float32
AXES = ("dp", "rep")
VMEM_LIMIT = 32 << 20
GLUE_LIMIT = 20 << 20
HBM = pl.BlockSpec(memory_space=pltpu.HBM)
VMEM = pl.BlockSpec(memory_space=pltpu.VMEM)
SMEM = pl.BlockSpec(memory_space=pltpu.SMEM)


class Grid:
    def __init__(self, mesh):
        self.n = mesh.shape["dp"]
        self.r = mesh.shape["rep"]
        self.high = self.n >> 1
        self.partner = self.n >> 2
        self.groups = [0, self.partner, self.high, self.high | self.partner]
        low = []
        bit = 1
        while bit < self.partner:
            low.append(bit)
            bit *= 2
        self.orders = [low, low[::-1]]
        self.high_bit = len(low) + 1

    def across(self, values, mask):
        pairs = [
            (d * self.r + c, (d ^ mask) * self.r + c) for d in range(self.n) for c in range(self.r)
        ]
        return lax.ppermute(values, AXES, pairs)

    def swap_cores(self, values):
        pairs = [
            (d * self.r + c, d * self.r + (c ^ 1)) for d in range(self.n) for c in range(self.r)
        ]
        return lax.ppermute(values, AXES, pairs)

    def hop(self, values, step):
        pairs = []
        for d in range(self.n):
            for c in range(self.r):
                mask = self.orders[c % 2][step]
                pairs.append((d * self.r + c, (d ^ mask) * self.r + c))
        return lax.ppermute(values, AXES, pairs)

    def place(self, info):
        core, me = info[1], info[2]
        first = jnp.right_shift(me, core) & 1
        second = jnp.right_shift(me, 1 - core) & 1
        return jnp.right_shift(me, 2), first, second, 1 + core, 2 - core

    def masks(self, core):
        found = [0]
        for low, high in zip(*self.orders, strict=True):
            bit = low + core * (high - low)
            found = found + [m ^ bit for m in found]
        return found


def call(kernel, outs, ins, specs, out_specs, scratch=(), flops=0, moved=0, room=VMEM_LIMIT):
    results = pl.pallas_call(
        kernel,
        out_shape=[jax.ShapeDtypeStruct(shape, dtype) for shape, dtype in outs],
        in_specs=specs,
        out_specs=out_specs,
        scratch_shapes=list(scratch),
        compiler_params=pltpu.CompilerParams(vmem_limit_bytes=room),
        cost_estimate=pl.CostEstimate(flops=flops, bytes_accessed=moved, transcendentals=0),
    )(*ins)
    return list(results)


def pair_kernel(bit_of, info_ref, *refs):
    mine, other = refs[:2]
    bit = jnp.right_shift(info_ref[2], bit_of) & 1
    start = 0
    for out in refs[2:]:
        end = start + out.shape[-2]
        out[bit] = mine[..., start:end, :]
        out[1 - bit] = other[..., start:end, :]
        start = end


def pair(info, bit_of, mine, other, parts=None):
    shape = mine.shape
    parts = [shape[-2]] if parts is None else parts
    if shape[-2] % 16:
        bit = jnp.right_shift(info[2], bit_of) & 1
        both = jnp.where(bit == 0, jnp.stack([mine, other]), jnp.stack([other, mine]))
        starts = [sum(parts[:i]) for i in range(len(parts))]
        return [both[..., s : s + p, :] for s, p in zip(starts, parts, strict=True)]
    return call(
        functools.partial(pair_kernel, bit_of),
        [((2,) + shape[:-2] + (part, shape[-1]), bf16) for part in parts],
        [info, mine, other],
        [SMEM, VMEM, VMEM],
        [VMEM] * len(parts),
        room=GLUE_LIMIT,
    )


def group_kernel(high_bit, info_ref, *refs):
    group = jnp.right_shift(info_ref[2], high_bit - 1)
    for k, source in enumerate(refs[:4]):
        refs[4][jnp.bitwise_xor(group, k)] = source[...]


def all_meet(grid, info, mine, theirs):
    return [
        mine,
        grid.across(theirs, grid.groups[1]),
        grid.across(theirs, grid.groups[2]),
        grid.across(mine, grid.groups[3]),
    ]


def grouped(grid, info, sources):
    shape = sources[0].shape
    if shape[0] % 16:
        group = jnp.right_shift(info[2], grid.high_bit - 1)
        return jnp.take(jnp.stack(sources), jnp.arange(4) ^ group, axis=0)
    return call(
        functools.partial(group_kernel, grid.high_bit),
        [((4,) + shape, bf16)],
        [info] + sources,
        [SMEM] + [VMEM] * 4,
        [VMEM],
        room=GLUE_LIMIT,
    )[0]


def join_kernel(grid, info_ref, mine, other, out):
    bit = grid.place(info_ref)[1]
    for g in range(4):
        out[g, bit] = mine[g]
        out[g, 1 - bit] = other[g]


def join_pair(grid, info, pieces):
    shape = pieces[0].shape
    return call(
        functools.partial(join_kernel, grid),
        [((4, 2) + shape[1:], bf16)],
        [info] + pieces,
        [SMEM] + [VMEM] * 2,
        [VMEM],
        room=GLUE_LIMIT,
    )[0]


def tie(*values):
    flat, tree = jax.tree.flatten(values)
    return jax.tree.unflatten(tree, lax.optimization_barrier(flat))


def meet(grid, info, held):
    rows, width = held.shape[1:]
    received = grid.across(held, grid.groups[3])

    def place(received):
        return pair(info, grid.high_bit, held, received)[0].reshape(4, rows, width)

    return received, place


def second_hops(grid, held):
    if len(grid.orders[0]) == 2:
        return [held, grid.hop(held, 0)]
    for step in range(len(grid.orders[0])):
        held = jnp.concatenate([held, grid.hop(held, step)], 0)
    return [held]


def third_hops(grid, info, pieces):
    if len(pieces) == 1:
        return pieces
    held = join_pair(grid, info, pieces)
    return [held, grid.hop(held, 1), grid.swap_cores(held)]


def extra_rows(grid, info, pieces, start, keep):
    held = pieces[0][:, start : start + keep]
    return jnp.take(held, jnp.argsort(slots_of(grid, info)), axis=0)


def slots_of(grid, info):
    masks = jnp.stack(grid.masks(info[1])).astype(jnp.int32)[:, None]
    groups = jnp.arange(4, dtype=jnp.int32)[None, :] * grid.partner
    return ((masks ^ (info[2] & (grid.partner - 1))) | groups).reshape(-1)


def whole(grid, info, pieces, rows, count):
    if len(pieces) == 3:
        return [pieces[0], pieces[1], pieces[2], grid.swap_cores(pieces[1])]
    held = pieces[0][:, : count * rows]
    held = jnp.take(held, jnp.argsort(slots_of(grid, info)), axis=0).reshape(grid.n, count, rows, -1).transpose(1, 0, 2, 3)
    held = held.reshape(count, grid.n * rows, -1)
    return [held, grid.swap_cores(held)]


def split_kernel(grid, extra, info_ref, keep, received, *refs):
    outs = refs[-2:]
    count, rows = keep.shape[0], keep.shape[2]
    unused, unused, second, first_step, second_step = grid.place(info_ref)
    for g in range(4):
        for a in range(2):
            for b, out in ((second, outs[0]), (1 - second, outs[1])):
                source = 4 * g + a * first_step + b * second_step
                for j in range(count):
                    total = keep[j, source].astype(f32) + received[j, source].astype(f32)
                    out[g, a, j * rows : (j + 1) * rows] = total.astype(bf16)
                if extra:
                    out[g, a, count * rows :] = refs[0][source]


def added(a, b):
    return (a.astype(f32) + b.astype(f32)).astype(bf16)


def first_returns(grid, info, keep, received, more=None):
    blocks, n, rows, width = keep.shape
    depth = blocks * rows + (0 if more is None else more.shape[1])
    extra = [] if more is None else [more]
    if len(grid.orders[0]) != 2:
        total = added(keep, received).transpose(1, 0, 2, 3).reshape(n, blocks * rows, width)
        total = jnp.concatenate([total] + extra, 1)
        held = jnp.take(total, slots_of(grid, info), axis=0)
        for step in reversed(range(len(grid.orders[0]))):
            half = held.shape[0] // 2
            held = added(held[:half], grid.hop(held[half:], step))
        return [held]
    held, sent = call(
        functools.partial(split_kernel, grid, len(extra)),
        [((4, 2, depth, width), bf16)] * 2,
        [info, keep, received] + extra,
        [SMEM, VMEM, VMEM] + [VMEM] * len(extra),
        [VMEM] * 2,
        room=GLUE_LIMIT,
    )
    return [held, grid.hop(sent, 1)]


def merge_kernel(grid, info_ref, *refs):
    near, far = refs[-2:]
    bit = grid.place(info_ref)[1]
    start = 0
    for held, received in zip(refs[:-2:2], refs[1:-2:2], strict=True):
        at = slice(start, start + held.shape[2])
        for g in range(4):
            for which, out in ((bit, near), (1 - bit, far)):
                out[g, at] = added(held[g, which], received[g, which])
        start += held.shape[2]


def second_returns(grid, info, *parts):
    if len(parts[0]) == 1:
        return [jnp.concatenate([part[0] for part in parts], 1)]
    depth = sum(part[0].shape[2] for part in parts)
    near, far = call(
        functools.partial(merge_kernel, grid),
        [((4, depth, parts[0][0].shape[3]), bf16)] * 2,
        [info] + [array for part in parts for array in part],
        [SMEM] + [VMEM] * (2 * len(parts)),
        [VMEM] * 2,
        room=GLUE_LIMIT,
    )
    return [near, grid.hop(far, 0)]


def collect_kernel(grid, info_ref, held, received, *outs):
    group = grid.place(info_ref)[0]
    for k, out in enumerate(outs):
        at = jnp.bitwise_xor(group, k)
        out[...] = added(held[at], received[at])


def third_returns(grid, info, pieces):
    if len(pieces) == 1:
        group = jnp.right_shift(info[2], grid.high_bit - 1)
        totals = [
            lax.dynamic_index_in_dim(pieces[0], group ^ g, 0, keepdims=False) for g in range(4)
        ]
    else:
        totals = call(
            functools.partial(collect_kernel, grid),
            [(pieces[0].shape[1:], bf16)] * 4,
            [info] + pieces,
            [SMEM] + [VMEM] * 2,
            [VMEM] * 4,
            room=GLUE_LIMIT,
        )
    return [totals[0]] + [grid.across(totals[g], grid.groups[g]) for g in (3, 1, 2)]


def last_kernel(near_a, near_b, far_a, far_b, out):
    out[0] = (near_a[...].astype(f32) + near_b[...].astype(f32)).astype(bf16)
    out[1] = (far_a[...].astype(f32) + far_b[...].astype(f32)).astype(bf16)


def last_swap(grid, terms):
    mine = call(
        last_kernel,
        [((2,) + terms[0].shape, bf16)],
        terms,
        [VMEM] * 4,
        [VMEM],
        room=GLUE_LIMIT,
    )[0]
    return mine, grid.swap_cores(mine)


def finish_kernel(layout, rows, info_ref, mine_ref, far_ref, *outs):
    side, core = info_ref[0], info_ref[1]

    def write(which, ref):
        for j, (out, at) in enumerate(layout[which]):
            for k in range(2):
                value = ref[k, j * rows : (j + 1) * rows].astype(f32)
                outs[out][(jnp.bitwise_xor(side, k),) + at] = value

    for which in range(2):
        pl.when(core == which)(functools.partial(write, which, mine_ref))
        pl.when(core != which)(functools.partial(write, which, far_ref))


def finish(info, done, layout, rows, shapes):
    return call(
        functools.partial(finish_kernel, layout, rows),
        [(shape, f32) for shape in shapes],
        [info] + list(done),
        [SMEM, VMEM, VMEM],
        [VMEM] * len(shapes),
        room=GLUE_LIMIT,
    )


def finish_gate_kernel(info_ref, mine_ref, far_ref, out):
    side, core = info_ref[0], info_ref[1]
    rows = out.shape[1]

    def write(own_ref, other_ref):
        for k in range(2):
            own = own_ref[k, :rows].astype(f32)
            out[jnp.bitwise_xor(side, k)] = own + other_ref[1 - k, :rows].astype(f32)

    pl.when(core == 0)(functools.partial(write, mine_ref, far_ref))
    pl.when(core != 0)(functools.partial(write, far_ref, mine_ref))


def nn(a, b):
    return lax.dot_general(a, b, (((1,), (0,)), ((), ())), preferred_element_type=f32)


def nt(a, b):
    return lax.dot_general(a, b, (((1,), (1,)), ((), ())), preferred_element_type=f32)


def tn(a, b):
    return lax.dot_general(a, b, (((0,), (0,)), ((), ())), preferred_element_type=f32)


def block_shapes(grid, count, rows, width, mixed=False):
    if rows % 16 or len(grid.orders[0]) != 2:
        return (4 * grid.n * rows, width) if mixed else (count, grid.n * rows, width)
    inner = (4, rows, width) if mixed else (rows, width)
    return ((4, 2, 2) if mixed else (count, 4, 2, 2)) + inner


def load_blocks(grid, info_ref, sources, blocks, sem, start=0, only=None, mixed=False):
    core = info_ref[1]
    middle = len(sources) // 2

    def load(which, refs):
        count = 1 if only is not None else 2 if mixed else blocks.shape[0] // 2
        first = 0 if only is not None else which * count
        if len(refs) == 1:
            for j in range(count):
                pltpu.make_async_copy(refs[0].at[start + j], blocks.at[first + j], sem).start()
            return
        rows = blocks.shape[-2]
        bit = jnp.right_shift(info_ref[2], 1 - which) & 1
        for j in range(count):
            for ref, b in ((refs[0], bit), (refs[1], 1 - bit)):
                source = ref.at[:, :, pl.ds((start + j) * rows, rows)]

                def low_first(b=b, j=j, source=source):
                    target = blocks.at[:, b, :, first + j] if mixed else blocks.at[first + j, :, b]
                    pltpu.make_async_copy(source, target, sem).start()

                def high_first(b=b, j=j, source=source):
                    target = (
                        blocks.at[:, :, b, first + j] if mixed else blocks.at[first + j, :, :, b]
                    )
                    pltpu.make_async_copy(source, target, sem).start()

                pl.when(which == 0)(low_first)
                pl.when(which != 0)(high_first)

    if len(sources) == 1:
        pltpu.make_async_copy(sources[0], blocks, sem).start()
    elif only is None:
        load(core, sources[:middle])
        load(1 - core, sources[middle:])
    else:
        pl.when(core == only)(lambda: load(only, sources[:middle]))
        pl.when(core != only)(lambda: load(only, sources[middle:]))
    return pltpu.make_async_copy(blocks, blocks, sem).wait


def matrix(values):
    return values.reshape(-1, values.shape[-1])


def load_inputs(info_ref, language, vision, both_far, src_ref, oth_ref, sem):
    half = language.shape[0]

    def copies(mine, mine_at, other, other_at):
        return [
            pltpu.make_async_copy(mine, src_ref.at[pl.ds(0, half)], sem.at[0]),
            pltpu.make_async_copy(
                both_far.at[pl.ds(mine_at, half)], src_ref.at[pl.ds(half, half)], sem.at[1]
            ),
            pltpu.make_async_copy(other, oth_ref.at[pl.ds(0, half)], sem.at[2]),
            pltpu.make_async_copy(
                both_far.at[pl.ds(other_at, half)], oth_ref.at[pl.ds(half, half)], sem.at[3]
            ),
        ]

    @pl.when(info_ref[0] == 0)
    def _():
        for copy in copies(language, 0, vision, half):
            copy.start()

    @pl.when(info_ref[0] != 0)
    def _():
        for copy in copies(vision, half, language, 0):
            copy.start()

    def wait():
        for copy in copies(language, 0, vision, half):
            copy.wait()

    return wait


def store_blocks(core, blocks, keep, send, sem):
    count = keep.shape[0]
    copies = []
    for j in range(count):
        copies.append(pltpu.make_async_copy(blocks.at[core * count + j], keep.at[j], sem.at[j]))
        copies.append(
            pltpu.make_async_copy(
                blocks.at[(1 - core) * count + j], send.at[j], sem.at[count + j]
            )
        )
    for copy in copies:
        copy.start()

    def wait():
        for copy in copies:
            copy.wait()

    return wait


def normalised(values):
    mean_row = jnp.mean(values, axis=-1, keepdims=True)
    centred = values - mean_row
    variance = jnp.mean(centred * centred, axis=-1, keepdims=True)
    scale = lax.rsqrt(variance + norm_epsilon)
    return centred * scale, scale


def norm_back(values, grads, gain):
    unit, scale = normalised(values)
    scaled = grads * gain
    first = jnp.mean(scaled, axis=-1, keepdims=True)
    second = jnp.mean(scaled * unit, axis=-1, keepdims=True)
    return (scaled - first - unit * second) * scale, grads * unit


def lane_masks():
    lanes = lax.broadcasted_iota(jnp.int32, (128, 2 * HEAD), 1)
    left = (lanes < HEAD).astype(f32).astype(bf16)
    right = (lanes >= HEAD).astype(f32).astype(bf16)
    return lanes < HEAD, left, right


def two_heads(values, left, right):
    return jnp.concatenate([values * left, values * right], 0)


def softened(queries, keys_both, barred):
    scores = []
    for pair, keys in zip(queries, keys_both, strict=True):
        both = nt(pair, keys) * HEAD ** (-0.5)
        slots = both.shape[0]
        scores += [both[:, :slots], both[:, slots:]]
    scores = [jnp.where(barred, -1000000000.0, part) for part in scores]
    peaks = [jnp.max(part, axis=-1, keepdims=True) for part in scores]
    weights = [jnp.exp(part - peak) for part, peak in zip(scores, peaks, strict=True)]
    totals = [1.0 / jnp.sum(part, axis=-1, keepdims=True) for part in weights]
    return [part * total for part, total in zip(weights, totals, strict=True)]


def joined(parts, pair):
    return jnp.concatenate([part.astype(bf16) for part in parts[2 * pair : 2 * pair + 2]], 1)


def barred_slots(slots, count):
    return lax.broadcasted_iota(jnp.int32, (slots, slots), 1) >= count


def pages_of(rows, slots, body):
    def step(page, carry):
        body(page, pl.ds(pl.multiple_of(page * slots, slots), slots))
        return carry

    lax.fori_loop(0, rows // slots, step, 0, unroll=2)


def column_sum(values):
    return jnp.sum(values.astype(f32), axis=0, keepdims=True)


def attend_kernel(grid, cross, slots, held, at_table, info_ref, counts_ref, vec_ref, *refs):
    if cross:
        inputs, refs = refs[:3], refs[3:]
    else:
        residual_ref, low_ref = refs[:2]
        refs = refs[2:]
    sources, refs = refs[:held], refs[held:]

    def row(i):
        return vec_ref[at_table[i] : at_table[i] + 1, :]

    q_ref, k_ref, v_ref, o_ref, sum_ref, norm_ref, norm_low_ref = refs[:7]
    blocks, sem = refs[7:9]
    rows = q_ref.shape[0]
    half = rows // 2
    wait_blocks = load_blocks(grid, info_ref, sources, blocks, sem)
    if cross:
        src_ref, oth_ref, in_sem = refs[9:12]
        load_inputs(info_ref, *inputs, src_ref, oth_ref, in_sem)()
    else:
        src_ref = oth_ref = low_ref
    wait_blocks()
    width = q_ref.shape[1]
    q_ref[...] = (nn(src_ref[...], matrix(blocks[0])) + row(0)).astype(bf16)
    k_ref[...] = nn(oth_ref[...], matrix(blocks[1])).astype(bf16)
    v_ref[...] = (nn(oth_ref[...], matrix(blocks[2])) + row(1)).astype(bf16)
    unused, left, right = lane_masks()
    cuts = [slice(at, at + 128) for at in range(0, width, 128)]

    def one_page(page, at):
        soft = softened(
            [q_ref[at, cut] for cut in cuts],
            [two_heads(k_ref[at, cut], left, right) for cut in cuts],
            barred_slots(slots, counts_ref[page]),
        )
        for i, cut in enumerate(cuts):
            mixed = nn(joined(soft, i), two_heads(v_ref[at, cut], left, right))
            o_ref[at, cut] = mixed.astype(bf16)

    pages_of(rows, slots, one_page)
    residual = src_ref[...].astype(f32) if cross else residual_ref[...]
    total = residual + nn(o_ref[...], matrix(blocks[3])) + row(2)
    sum_ref[...] = total
    result = normalised(total)[0] * row(3) + row(4)
    norm_ref[...] = result
    norm_low_ref[...] = result.astype(bf16)


def attend(grid, cross, slots, info, counts, vectors, at_table, inputs, weights):
    width = weights[0].shape[-1]
    rows = counts.shape[0] * slots
    blocks = block_shapes(grid, 4, grid.rows, width)
    scratch = [pltpu.VMEM(blocks, bf16), pltpu.SemaphoreType.DMA]
    if cross:
        scratch += [pltpu.VMEM((rows, width), bf16)] * 2 + [pltpu.SemaphoreType.DMA((4,))]
    return call(
        functools.partial(attend_kernel, grid, cross, slots, len(weights), at_table),
        [((rows, width), bf16)] * 4 + [((rows, width), f32)] * 2 + [((rows, width), bf16)],
        [info, counts, vectors] + list(inputs) + list(weights),
        [SMEM, SMEM, VMEM] + ([HBM] * 3 if cross else [VMEM] * 2) + [HBM] * len(weights),
        [VMEM] * 7,
        scratch,
        flops=8 * rows * width * width + 8 * rows * slots * width,
        moved=4 * width * width * 2 + rows * width * 20,
    )


def hidden_kernel(grid, held, info_ref, shift_ref, low_ref, *refs):
    sources = refs[:held]
    active_ref, slope_ref, blocks, sem = refs[held:]
    load_blocks(grid, info_ref, sources, blocks, sem)()
    width = low_ref.shape[1]
    for b in range(4):
        at = slice(b * width, (b + 1) * width)
        hidden = nn(low_ref[...], matrix(blocks[b])) + shift_ref[0:1, at]
        square = hidden * hidden
        bent = jnp.tanh(0.7978845608028654 * (hidden + 0.044715 * square * hidden))
        active_ref[:, at] = (0.5 * hidden * (1.0 + bent)).astype(bf16)
        slope = 0.5 * (1.0 + bent) + 0.5 * hidden * (1.0 - bent * bent) * (
            0.7978845608028654 * (1.0 + 3.0 * 0.044715 * square)
        )
        slope_ref[:, at] = slope.astype(bf16)


def hidden_layer(grid, info, shift, low, weights):
    rows, width = low.shape
    return call(
        functools.partial(hidden_kernel, grid, len(weights)),
        [((rows, 4 * width), bf16)] * 2,
        [info, shift, low] + list(weights),
        [SMEM, VMEM, VMEM] + [HBM] * len(weights),
        [VMEM, VMEM],
        [pltpu.VMEM(block_shapes(grid, 4, grid.rows, width), bf16), pltpu.SemaphoreType.DMA],
        flops=8 * rows * width * width,
        moved=8 * width * width + rows * width * 18,
    )


def store_wide(core, wide, keep, send, sem):
    copies = []
    for j in range(2):
        for which, target in ((core, keep), (1 - core, send)):
            copies.append(pltpu.make_async_copy(wide.at[:, 2 * which + j], target.at[j], sem))
    for copy in copies:
        copy.start()
    pltpu.make_async_copy(wide, wide, sem).wait()


def branch_kernel(grid, held, info_ref, vec_ref, active_ref, residual_ref, *refs):
    sources = refs[:held]
    sum_ref, norm_ref, far_ref, wide, sem = refs[held:]
    load_blocks(grid, info_ref, sources, wide, sem, mixed=True)()
    half = residual_ref.shape[0] // 2
    total = residual_ref[...] + nn(active_ref[...], matrix(wide[...])) + vec_ref[12:13, :]
    sum_ref[...] = total
    result = normalised(total)[0] * vec_ref[8:9, :] + vec_ref[11:12, :]
    norm_ref[...] = result[:half]
    far_ref[...] = result[half:].astype(bf16)


def branch_layer(grid, info, vectors, active, residual, weights):
    rows, width = residual.shape
    return call(
        functools.partial(branch_kernel, grid, len(weights)),
        [((rows, width), f32), ((rows // 2, width), f32), ((rows // 2, width), bf16)],
        [info, vectors, active, residual] + list(weights),
        [SMEM, VMEM, VMEM, VMEM] + [HBM] * len(weights),
        [VMEM] * 3,
        [pltpu.VMEM(block_shapes(grid, 4, grid.rows, width, True), bf16), pltpu.SemaphoreType.DMA],
        flops=8 * rows * width * width,
        moved=8 * width * width + rows * width * 20,
    )


def gate_kernel(grid, held, info_ref, shift_ref, third_ref, far_ref, cotangent_ref, *refs):
    sources = refs[:held]
    united_ref, grad_own_ref, grad_far_ref, grad_shift_ref, keep_ref, send_ref = refs[held : held + 6]
    blocks, sem, grads, mix_ref, low_ref, out_sem = refs[held + 6 :]
    load_blocks(grid, info_ref, sources, blocks, sem, 2)()
    first = info_ref[0] == 0
    low_ref[...] = third_ref[...].astype(bf16)
    logits = nn(low_ref[...], matrix(blocks[0])) + nn(far_ref[...], matrix(blocks[1])) + shift_ref[13:14, :]
    mixing = 1.0 / (1.0 + jnp.exp(-logits))
    share = jnp.where(first, mixing, 1.0 - mixing)
    mine, other = third_ref[...], far_ref[...].astype(f32)
    united_ref[...] = (share * mine + (1.0 - share) * other).astype(bf16)
    cotangent = cotangent_ref[...].astype(f32)
    gap = jnp.where(first, mine - other, other - mine)
    grad = (cotangent * gap * mixing * (1.0 - mixing)).astype(bf16)
    mix_ref[...] = grad
    grad_shift_ref[0:1, :] = column_sum(grad)
    direct = cotangent * share
    grad_own_ref[...] = direct + nt(mix_ref[...], matrix(blocks[0]))
    grad_far_ref[...] = (cotangent - direct + nt(mix_ref[...], matrix(blocks[1]))).astype(bf16)
    grads[0] = tn(low_ref[...], mix_ref[...]).astype(bf16)
    grads[1] = tn(far_ref[...], mix_ref[...]).astype(bf16)
    store_blocks(info_ref[1], grads, keep_ref, send_ref, out_sem)()


def gate_layer(grid, info, shift, third, far, cotangent, weights):
    rows, width = third.shape
    blocks = (2, width, width)
    return call(
        functools.partial(gate_kernel, grid, len(weights)),
        [
            ((rows, width), bf16),
            ((rows, width), f32),
            ((rows, width), bf16),
            ((8, width), f32),
            ((1,) + blocks[1:], bf16),
            ((1,) + blocks[1:], bf16),
        ],
        [info, shift, third, far, cotangent] + list(weights),
        [SMEM] + [VMEM] * 4 + [HBM] * len(weights),
        [VMEM] * 4 + [HBM] * 2,
        [
            pltpu.VMEM(block_shapes(grid, 2, grid.rows, width), bf16),
            pltpu.SemaphoreType.DMA,
            pltpu.VMEM(blocks, bf16),
            pltpu.VMEM((rows, width), bf16),
            pltpu.VMEM((rows, width), bf16),
            pltpu.SemaphoreType.DMA((2,)),
        ],
        flops=12 * rows * width * width,
        moved=8 * width * width + rows * width * 14,
    )


def branch_back_kernel(
    wide_out,
    info_ref,
    gain_ref,
    sum_ref,
    grad_own_ref,
    grad_far_ref,
    active_ref,
    grad_sum_ref,
    grad_low_ref,
    vec_ref,
    *refs,
):
    rows, width = sum_ref.shape
    half = rows // 2
    vec_ref[...] = jnp.zeros_like(vec_ref)
    for offset, grads_ref in ((0, grad_own_ref), (half, grad_far_ref)):
        at = slice(offset, offset + half)
        grads = grads_ref[...].astype(f32)
        back, gain_rows = norm_back(sum_ref[at, :], grads, gain_ref[8:9, :])
        low = back.astype(bf16)
        grad_sum_ref[at, :] = back
        grad_low_ref[at, :] = low
        vec_ref[0:1, :] += column_sum(gain_rows)
        vec_ref[1:2, :] += column_sum(grads)
        vec_ref[2:3, :] += column_sum(low)
    wide, sem = refs[-2:]
    for b in range(4):
        at = slice(b * width, (b + 1) * width)
        part = tn(active_ref[:, at], grad_low_ref[...]).astype(bf16)
        if wide_out:
            devices = wide.shape[0] // 4
            wide[b * devices : (b + 1) * devices] = part.reshape((devices,) + wide.shape[1:])
        else:
            wide[at, :] = part
    if wide_out:
        store_wide(info_ref[1], wide, refs[0], refs[1], sem)
    else:
        copy = pltpu.make_async_copy(wide, refs[0], sem)
        copy.start()
        copy.wait()


def branch_back(grid, info, gain, sums, grad_own, grad_far, active, piece):
    rows, width = sums.shape
    wide_out = piece % 16 == 0
    target = (2, grid.n, piece, width) if wide_out else (4 * width, width)
    outs = [(target, bf16)] * (2 if wide_out else 1)
    return call(
        functools.partial(branch_back_kernel, wide_out),
        [((rows, width), f32), ((rows, width), bf16), ((8, width), f32)] + outs,
        [info, gain, sums, grad_own, grad_far, active],
        [SMEM] + [VMEM] * 5,
        [VMEM] * 3 + [HBM] * len(outs),
        [
            pltpu.VMEM((grid.n, 4, piece, width) if wide_out else (4 * width, width), bf16),
            pltpu.SemaphoreType.DMA,
        ],
        flops=8 * rows * width * width,
        moved=8 * width * width + rows * width * 24,
    )


def hidden_back_kernel(grid, held, info_ref, grad_low_ref, slope_ref, low_ref, *refs):
    core = info_ref[1]
    grad_hidden_ref, vec_ref, keep_ref, send_ref, wide, sem, grads, out_sem = refs[held:]
    load_blocks(grid, info_ref, refs[:held], wide, sem, mixed=True)()
    whole_wide = matrix(wide[...])
    width = low_ref.shape[1]
    for b in range(4):
        at = slice(b * width, (b + 1) * width)
        low = (nt(grad_low_ref[...], whole_wide[at, :]) * slope_ref[:, at].astype(f32)).astype(bf16)
        grad_hidden_ref[:, at] = low
        vec_ref[0:1, at] = column_sum(low)
        grads[b] = tn(low_ref[...], low).astype(bf16)
    store_blocks(core, grads, keep_ref, send_ref, out_sem)()


def hidden_back(grid, info, grad_low, slope, low, weights):
    rows, width = low.shape
    blocks = (4, width, width)
    return call(
        functools.partial(hidden_back_kernel, grid, len(weights)),
        [((rows, 4 * width), bf16), ((8, 4 * width), f32)] + [((2,) + blocks[1:], bf16)] * 2,
        [info, grad_low, slope, low] + list(weights),
        [SMEM] + [VMEM] * 3 + [HBM] * len(weights),
        [VMEM] * 2 + [HBM] * 2,
        [
            pltpu.VMEM(block_shapes(grid, 4, grid.rows, width, True), bf16),
            pltpu.SemaphoreType.DMA,
            pltpu.VMEM(blocks, bf16),
            pltpu.SemaphoreType.DMA((4,)),
        ],
        flops=16 * rows * width * width,
        moved=16 * width * width + rows * width * 30,
    )


def second_back_kernel(
    grid, held, info_ref, gain_ref, sum_ref, grad_ref, grad_hidden_ref, *refs
):
    grad_sum_ref, vec_ref, blocks, sem = refs[held:]
    load_blocks(grid, info_ref, refs[:held], blocks, sem)()
    width = sum_ref.shape[1]
    total = grad_ref[...]
    for b in range(4):
        total += nt(grad_hidden_ref[:, b * width : (b + 1) * width], matrix(blocks[b]))
    grad_sum_ref[...] = norm_back_into(vec_ref, sum_ref[...], total, gain_ref[7:8, :])


def norm_back_into(vec_ref, sums, grads, gain):
    back, gain_rows = norm_back(sums, grads, gain)
    vec_ref[0:1, :] = column_sum(gain_rows)
    vec_ref[1:2, :] = column_sum(grads)
    return back


def second_back(grid, info, gain, sums, grads, grad_hidden, weights):
    rows, width = sums.shape
    return call(
        functools.partial(second_back_kernel, grid, len(weights)),
        [((rows, width), f32), ((8, width), f32)],
        [info, gain, sums, grads, grad_hidden] + list(weights),
        [SMEM] + [VMEM] * 4 + [HBM] * len(weights),
        [VMEM] * 2,
        [pltpu.VMEM(block_shapes(grid, 4, grid.rows, width), bf16), pltpu.SemaphoreType.DMA],
        flops=8 * rows * width * width,
        moved=8 * width * width + rows * width * 20,
    )


def scores_back_kernel(
    grid, cross, slots, held, info_ref, counts_ref, grad_ref, q_ref, k_ref, v_ref, o_ref, *refs
):
    count = 3 if cross else 1
    inputs, sources, refs = refs[:count], refs[count : count + held], refs[count + held :]
    dq_ref, dk_ref, dv_ref, vec_ref, keep_ref, send_ref = refs[:6]
    weight, sem, low_grad, grad_o, grads, out_sem = refs[6:12]
    wait_block = load_blocks(grid, info_ref, sources, weight, sem, 1, 1)
    if cross:
        src_ref, oth_ref, in_sem = refs[12:]
        wait_inputs = load_inputs(info_ref, *inputs, src_ref, oth_ref, in_sem)
    else:
        src_ref = oth_ref = inputs[0]
    rows, width = q_ref.shape
    low = grad_ref[...].astype(bf16)
    low_grad[...] = low
    vec_ref[2:3, :] = column_sum(low)
    grads[3] = tn(o_ref[...], low_grad[...]).astype(bf16)
    wait_block()
    grad_o[...] = nt(low_grad[...], matrix(weight[0])).astype(bf16)
    left_lanes, left, right = lane_masks()
    cuts = [slice(at, at + 128) for at in range(0, width, 128)]

    def one_page(page, at):
        keys = [two_heads(k_ref[at, cut], left, right) for cut in cuts]
        soft = softened(
            [q_ref[at, cut] for cut in cuts], keys, barred_slots(slots, counts_ref[page])
        )
        grad_soft = []
        for cut in cuts:
            both = nt(grad_o[at, cut], two_heads(v_ref[at, cut], left, right))
            grad_soft += [both[:, :slots], both[:, slots:]]
        weighted = [a * b for a, b in zip(soft, grad_soft, strict=True)]
        sums = [jnp.sum(part, axis=-1, keepdims=True) for part in weighted]
        grad_scores = [w - p * t for w, p, t in zip(weighted, soft, sums, strict=True)]
        for i, cut in enumerate(cuts):
            dv = tn(joined(soft, i), grad_o[at, cut])
            dv_ref[at, cut] = jnp.where(left_lanes, dv[:slots], dv[slots:]).astype(bf16)
        for i, cut in enumerate(cuts):
            pair = joined(grad_scores, i)
            dq_ref[at, cut] = (nn(pair, keys[i]) * HEAD ** (-0.5)).astype(bf16)
            dk = tn(pair, q_ref[at, cut]) * HEAD ** (-0.5)
            dk_ref[at, cut] = jnp.where(left_lanes, dk[:slots], dk[slots:]).astype(bf16)

    pages_of(rows, slots, one_page)
    vec_ref[0:1, :] = column_sum(dq_ref[...])
    vec_ref[1:2, :] = column_sum(dv_ref[...])
    if cross:
        wait_inputs()
    grads[0] = tn(src_ref[...], dq_ref[...]).astype(bf16)
    grads[1] = tn(oth_ref[...], dk_ref[...]).astype(bf16)
    grads[2] = tn(oth_ref[...], dv_ref[...]).astype(bf16)
    store_blocks(info_ref[1], grads, keep_ref, send_ref, out_sem)()


def scores_back(grid, cross, slots, info, counts, grad, saved, inputs, weights):
    rows, width = grad.shape
    full = pltpu.VMEM((rows, width), bf16)
    blocks = (4, width, width)
    scratch = [
        pltpu.VMEM(block_shapes(grid, 1, grid.rows, width), bf16),
        pltpu.SemaphoreType.DMA,
        full,
        full,
        pltpu.VMEM(blocks, bf16),
        pltpu.SemaphoreType.DMA((4,)),
    ]
    if cross:
        scratch += [full, full, pltpu.SemaphoreType.DMA((4,))]
    return call(
        functools.partial(scores_back_kernel, grid, cross, slots, len(weights)),
        [((rows, width), bf16)] * 3 + [((8, width), f32)] + [((2,) + blocks[1:], bf16)] * 2,
        [info, counts, grad] + list(saved) + list(inputs) + list(weights),
        [SMEM, SMEM] + [VMEM] * 5 + ([HBM] * 3 if cross else [VMEM]) + [HBM] * len(weights),
        [VMEM] * 4 + [HBM] * 2,
        scratch,
        flops=10 * rows * width * width + 24 * rows * slots * width,
        moved=12 * width * width + rows * width * 20,
    )


def project_back_kernel(grid, cross, held, info_ref, gain_ref, grad_ref, *refs):
    dq_ref, dk_ref, dv_ref = refs[:3]
    refs = refs[3:]
    if cross:
        sources = refs[:held]
        mine_ref, other_ref, far_ref, blocks, sem = refs[held:]
    else:
        sum_ref, sources = refs[0], refs[1 : 1 + held]
        out_ref, vec_ref, blocks, sem = refs[1 + held :]
    load_blocks(grid, info_ref, sources, blocks, sem)()
    half = grad_ref.shape[0] // 2
    mine = grad_ref[...] + nt(dq_ref[...], matrix(blocks[0]))
    other = nt(dk_ref[...], matrix(blocks[1])) + nt(dv_ref[...], matrix(blocks[2]))
    if cross:
        mine_ref[...] = mine[:half]
        other_ref[...] = other[:half]
        far_ref[:half] = other[half:].astype(bf16)
        far_ref[half:] = mine[half:].astype(bf16)
    else:
        vec_ref[...] = jnp.zeros_like(vec_ref)
        out_ref[...] = norm_back_into(vec_ref, sum_ref[...], mine + other, gain_ref[6:7, :])


def project_back(grid, cross, info, gain, grad, parts, sums, weights):
    rows, width = grad.shape
    half = (rows // 2, width)
    if cross:
        outs = [(half, f32), (half, f32), ((rows, width), bf16)]
    else:
        outs = [((rows, width), f32), ((8, width), f32)]
    return call(
        functools.partial(project_back_kernel, grid, cross, len(weights)),
        outs,
        [info, gain, grad] + list(parts) + list(sums) + list(weights),
        [SMEM] + [VMEM] * (5 + len(sums)) + [HBM] * len(weights),
        [VMEM] * len(outs),
        [pltpu.VMEM(block_shapes(grid, 4, grid.rows, width), bf16), pltpu.SemaphoreType.DMA],
        flops=6 * rows * width * width,
        moved=8 * width * width + rows * width * 18,
    )


SPOTS = (
    [(i, 0, 1) for i in range(3)]
    + [(i, 128, 1) for i in range(3)]
    + [(i, 256, 1) for i in range(3)]
    + [(i, 384, 1) for i in range(3)]
    + [(4, 0, 1), (4, 128, 1), (3, 0, 4)]
)
EXTRA = 16


def lay_vectors(cross_bias, self_bias, gains, shifts, out_bias, gate_bias, in_bias, width):
    def at(values, row, lane):
        depth, length = values.shape[1:]
        return jnp.pad(
            values, ((0, 0), (row, EXTRA - row - depth), (lane, width - lane - length))
        )

    gate = jnp.broadcast_to(gate_bias[None, None], (2, 1) + gate_bias.shape)
    return (
        at(cross_bias, 0, 0)
        + at(self_bias, 0, 128)
        + at(gains, 0, 256)
        + at(shifts, 0, 384)
        + at(out_bias[:, None], 4, 0)
        + at(gate, 4, 128)
        + at(in_bias[:, None], 3, 0)
    )


def unlay_kernel(grid, start, info_ref, mine_ref, other_ref, table_ref, wide_ref, held, found, sem):
    copies = []
    for k, ref in enumerate((mine_ref, other_ref)):
        source = ref.at[:, :, pl.ds(start, EXTRA)]
        copies.append(pltpu.make_async_copy(source, held.at[k], sem.at[k]))
    for copy in copies:
        copy.start()
    for copy in copies:
        copy.wait()
    unused, unused, second, first_step, second_step = grid.place(info_ref)
    for g in range(4):
        for a in range(2):
            for k, b in ((0, second), (1, 1 - second)):
                place = 4 * g + a * first_step + b * second_step
                found[place] = held[k, g, a].astype(f32)
    rows = grid.rows
    for p in range(grid.n):
        for i, (row, lane, unused) in enumerate(SPOTS[:-1]):
            table_ref[i : i + 1, p * rows : (p + 1) * rows] = found[p, row : row + 1, lane : lane + rows]
        row, lane, length = SPOTS[-1]
        wide_ref[0:1, p * length * rows : (p + 1) * length * rows] = found[
            p, row : row + 1, lane : lane + length * rows
        ]


def unlay_vectors(grid, info, pieces, start):
    width = pieces[0].shape[-1]
    rows = grid.rows
    if len(pieces) == 1:
        found = extra_rows(grid, info, pieces, start, EXTRA).astype(f32)
        parts = [
            found[:, row, lane : lane + length * rows].reshape(-1) for row, lane, length in SPOTS
        ]
        table = jnp.pad(jnp.stack(parts[:-1]), ((0, 2), (0, 0)))
        return table, jnp.pad(parts[-1][None], ((0, 7), (0, 0)))
    return call(
        functools.partial(unlay_kernel, grid, start),
        [((16, width), f32), ((8, 4 * width), f32)],
        [info] + pieces[:2],
        [SMEM, HBM, HBM],
        [VMEM, VMEM],
        [
            pltpu.VMEM((2, 4, 2, EXTRA, width), bf16),
            pltpu.VMEM((grid.n, EXTRA, width), f32),
            pltpu.SemaphoreType.DMA((2,)),
        ],
        room=GLUE_LIMIT,
    )


def relay_kernel(grid, where, *refs):
    out, held = refs[-2:]
    rows = grid.rows
    held[...] = jnp.zeros_like(held)
    for p in range(grid.n):
        for (table, i), (row, lane, length) in zip(where, SPOTS, strict=True):
            size = length * rows
            held[p, row : row + 1, lane : lane + size] = refs[table][i : i + 1, p * size : (p + 1) * size]
    out[...] = held[...].astype(bf16)


def relay_vectors(grid, tables, where):
    width = tables[0].shape[1]
    rows = grid.rows
    if rows % 16:
        out = jnp.zeros((grid.n, EXTRA, width), f32)
        for (table, i), (row, lane, length) in zip(where, SPOTS, strict=True):
            part = tables[table][i].reshape(grid.n, length * rows)
            out = out.at[:, row, lane : lane + length * rows].set(part)
        return out.astype(bf16)
    return call(
        functools.partial(relay_kernel, grid, where),
        [((grid.n, EXTRA, width), bf16)],
        tables,
        [VMEM] * len(tables),
        [VMEM],
        [pltpu.VMEM((grid.n, EXTRA, width), f32)],
        room=GLUE_LIMIT,
    )[0]


def on_device(
    grid,
    language_in,
    vision_in,
    language_count,
    vision_count,
    cross_qkv,
    cross_proj,
    cross_bias,
    norm_gain,
    norm_bias,
    self_qkv,
    self_proj,
    self_bias,
    ffn_in,
    ffn_in_bias,
    ffn_out,
    ffn_out_bias,
    gate_weight,
    gate_bias,
    cotangent,
):
    n = grid.n
    grid.rows = cross_proj.shape[1]
    me = lax.axis_index("dp")
    core = lax.axis_index("rep")
    side = ((me // grid.high) ^ (me // grid.partner)) & 1
    first = side == 0
    info = jnp.stack([side, core, me]).astype(jnp.int32)
    rows, width = cross_proj.shape[1:]
    dim = n * rows
    pages, slots = language_in.shape[:2]
    wide_ok = rows % 16 == 0

    def own(pair):
        return lax.dynamic_index_in_dim(pair, side, 0, keepdims=False)

    def other(pair):
        return lax.dynamic_index_in_dim(pair, 1 - side, 0, keepdims=False)

    vectors = lay_vectors(
        cross_bias, self_bias, norm_gain, norm_bias, ffn_out_bias, gate_bias, ffn_in_bias, width
    )
    groups = [
        [cross_qkv[:, 0], cross_qkv[:, 1], vectors, cross_qkv[:, 2], cross_proj, vectors],
        [self_qkv[:, 0], self_qkv[:, 1], self_qkv[:, 2], self_proj],
        [ffn_in[:, :, i * width : (i + 1) * width] for i in range(4)],
        [ffn_out[:, i * rows : (i + 1) * rows] for i in range(2)]
        + [gate_weight]
        + [ffn_out[:, i * rows : (i + 1) * rows] for i in range(2, 4)]
        + [gate_weight[::-1]],
    ]

    def shards(blocks):
        half = len(blocks) // 2
        parts = [jnp.concatenate(blocks[:half], 1), jnp.concatenate(blocks[half:], 1)]
        mine = lax.dynamic_index_in_dim(jnp.stack(parts), core, 0, keepdims=False)
        return own(mine), other(mine)

    sent = [shards(blocks) for blocks in groups]
    later = [jnp.concatenate([part[k] for part in sent[2:]], 0) for k in range(2)]
    parts = [part[0].shape[0] for part in sent[2:]]
    language = language_in.reshape(pages * slots, width)
    vision = vision_in.reshape(pages * slots, width)
    counts_mine = jnp.stack([language_count, vision_count])
    counts_wide = jnp.pad(counts_mine.astype(bf16), ((0, 14), (0, width - pages)))
    seen = jnp.concatenate([language, vision, counts_wide], 0)

    t1 = all_meet(grid, info, *sent[0])
    u0 = grid.across(sent[1][1], grid.partner)
    t1, u0, later = tie(t1, u0, later)
    t2 = second_hops(grid, grouped(grid, info, t1))
    u1, place_u = meet(grid, info, pair(info, grid.high_bit - 1, sent[1][0], u0)[0])
    later_far = grid.across(later[1], grid.partner)
    t2, u1, later_far, seen = tie(t2, u1, later_far, seen)
    t3 = third_hops(grid, info, t2)
    u2 = second_hops(grid, place_u(u1))
    w0, x0 = pair(info, grid.high_bit - 1, later[0], later_far, parts)
    w1, place_w = meet(grid, info, w0)
    seen_far = grid.across(seen, grid.partner)
    t3, u2, w1, seen_far, x0 = tie(t3, u2, w1, seen_far, x0)
    cross_w = whole(grid, info, t3, rows, 2)
    table, ffn_in_shift = unlay_vectors(grid, info, t3, 2 * rows)
    counts_far = seen_far[2 * pages * slots :, :pages][:2].astype(jnp.int32)
    counts = jnp.concatenate([own(counts_mine), own(counts_far)])
    other_counts = jnp.concatenate([other(counts_mine), other(counts_far)])
    inputs = [language, vision, seen_far]
    u3 = third_hops(grid, info, u2)
    w2 = second_hops(grid, place_w(w1))
    x1, place_x = meet(grid, info, x0)
    cq, ck, cv, co, first_sum, first_norm, first_low = attend(
        grid, True, slots, info, other_counts, table, (0, 1, 2, 6, 9), inputs, cross_w
    )
    first_norm, first_low, u3, w2, x1 = tie(first_norm, first_low, u3, w2, x1)
    self_w = whole(grid, info, u3, rows, 2)
    w3 = third_hops(grid, info, w2)
    x2 = second_hops(grid, place_x(x1))
    sq, sk, sv, so, second_sum, second_norm, second_low = attend(
        grid,
        False,
        slots,
        info,
        counts,
        table,
        (3, 4, 5, 7, 10),
        [first_norm, first_low],
        self_w,
    )
    second_norm, second_low, w3, x2 = tie(second_norm, second_low, w3, x2)
    in_w = whole(grid, info, w3, rows, 2)
    x3 = third_hops(grid, info, x2)
    active, slope = hidden_layer(grid, info, ffn_in_shift, second_low, in_w)
    active, second_norm, x3 = tie(active, second_norm, x3)
    gate_w = out_w = whole(grid, info, x3, rows, 3)
    if len(out_w) == 2:
        both = jnp.where(core == 0, jnp.stack(out_w), jnp.stack(out_w[::-1]))[:, :2]
        both = both.reshape(4, n, rows, width).transpose(1, 0, 2, 3)
        out_w = [both.reshape(4 * dim, width)]
    third_sum, third_own, third_send = branch_layer(
        grid, info, table, active, second_norm, out_w
    )
    third_far = grid.across(third_send, grid.partner)
    cotangent_rows = cotangent.reshape(pages * slots, width)
    united, grad_third_own, grad_third_send, grad_gate_shift, gate_keep, gate_send = gate_layer(
        grid, info, table, third_own, third_far, cotangent_rows, gate_w
    )

    def by_piece(values):
        return values.reshape(values.shape[0], n, rows, width)

    gate_keep, gate_send = by_piece(gate_keep), by_piece(gate_send)
    gate_got = grid.swap_cores(gate_send)
    grad_third_far = grid.across(grad_third_send, grid.partner)
    gate = first_returns(grid, info, gate_keep, gate_got)
    gate[0], grad_third_far = tie(gate[0], grad_third_far)
    grad_third_sum, grad_branch_low, vec_third, *out_grads = branch_back(
        grid, info, table, third_sum, grad_third_own, grad_third_far, active, rows
    )
    if len(out_grads) == 1:
        by_core = out_grads[0].reshape(n, 2, 2, rows, width).transpose(1, 2, 0, 3, 4)
        out_grads = [
            lax.dynamic_index_in_dim(by_core, c, 0, keepdims=False) for c in (core, 1 - core)
        ]
    out_keep, out_send = out_grads
    gate, grad_branch_low, out_keep, out_send = tie(gate, grad_branch_low, out_keep, out_send)
    out_got = grid.swap_cores(out_send)
    grad_hidden, vec_hidden, in_keep, in_send = hidden_back(
        grid, info, grad_branch_low, slope, second_low, out_w
    )
    out_got, grad_hidden, in_keep, in_send = tie(out_got, grad_hidden, in_keep, in_send)
    in_keep, in_send = by_piece(in_keep), by_piece(in_send)
    in_got = grid.swap_cores(in_send)
    outs = first_returns(grid, info, out_keep, out_got)
    grad_second_sum, vec_second = second_back(
        grid, info, table, second_sum, grad_third_sum, grad_hidden, in_w
    )
    outs, in_got, grad_second_sum = tie(outs, in_got, grad_second_sum)
    ins = first_returns(grid, info, in_keep, in_got)
    outs = second_returns(grid, info, gate, outs)
    *self_parts, vec_self, self_keep, self_send = scores_back(
        grid, False, slots, info, counts, grad_second_sum, [sq, sk, sv, so], [first_low], self_w
    )
    outs, ins, self_parts, self_keep, self_send = tie(outs, ins, self_parts, self_keep, self_send)
    self_keep, self_send = by_piece(self_keep), by_piece(self_send)
    self_got = grid.swap_cores(self_send)
    ins = second_returns(grid, info, ins)
    outs = third_returns(grid, info, outs)
    grad_first_sum, vec_first = project_back(
        grid, False, info, table, grad_second_sum, self_parts, [first_sum], self_w
    )
    ins, self_got, grad_first_sum = tie(ins, self_got, grad_first_sum)
    selfs = first_returns(grid, info, self_keep, self_got)
    ins = third_returns(grid, info, ins)
    *cross_parts, vec_cross, cross_keep, cross_send = scores_back(
        grid, True, slots, info, other_counts, grad_first_sum, [cq, ck, cv, co], inputs, cross_w
    )
    selfs, outs, cross_parts, cross_keep, cross_send = tie(
        selfs, outs, cross_parts, cross_keep, cross_send
    )
    cross_keep, cross_send = by_piece(cross_keep), by_piece(cross_send)
    cross_got = grid.swap_cores(cross_send)
    selfs = second_returns(grid, info, selfs)
    tables = [vec_cross, vec_self, vec_first, vec_second, vec_third, grad_gate_shift, vec_hidden]
    where = [(0, 0), (0, 1), (0, 2), (1, 0), (1, 1), (1, 2)]
    where += [(2, 0), (3, 0), (4, 0), (2, 1), (3, 1), (4, 1), (4, 2), (5, 0), (6, 0)]
    grad_vec = relay_vectors(grid, tables, where)
    grad_mine, grad_theirs, outgoing = project_back(
        grid, True, info, table, grad_first_sum, cross_parts, [], cross_w
    )
    cross_got, outgoing, selfs, ins, outs, grad_vec = tie(
        cross_got, outgoing, selfs, ins, outs, grad_vec
    )
    crosses = first_returns(grid, info, cross_keep, cross_got, grad_vec)
    incoming = grid.across(outgoing, grid.partner)
    selfs = third_returns(grid, info, selfs)
    crosses, selfs = tie(crosses, selfs)
    crosses = second_returns(grid, info, crosses)
    crosses[0], outs, ins = tie(crosses[0], outs, ins)
    out_done = last_swap(grid, outs)
    in_done = last_swap(grid, ins)

    def sides(near, far):
        return jnp.where(first, jnp.stack([near, far]), jnp.stack([far, near]))

    def finished(done, count, start=0):
        mine, far = [part[:, start * rows : (start + count) * rows] for part in done]
        mine, far = [part.reshape(2, count, rows, width) for part in (mine, far)]
        both = jnp.where(core == 0, jnp.concatenate([mine, far], 1), jnp.concatenate([far, mine], 1))
        return both.astype(f32)

    def by_side(both):
        return jnp.where(first, both, both[::-1])

    def attention_grads(done):
        if rows % 16:
            both = by_side(finished(done, 2))
            return [both[:, 0:3], both[:, 3]]
        layout = (((0, (0,)), (0, (1,))), ((0, (2,)), (1, ())))
        return finish(info, done, layout, rows, [(2, 3, rows, width), (2, rows, width)])

    if rows % 16:
        in_all = by_side(finished(in_done, 2)).transpose(0, 2, 1, 3).reshape(2, rows, 4 * width)
        gate_all = finished(out_done, 1)
        gate_both = sides(gate_all[0, 0] + gate_all[1, 1], gate_all[0, 1] + gate_all[1, 0])
        out_all = by_side(finished(out_done, 2, 1)).reshape(2, 4 * rows, width)
    else:
        every = slice(None)
        cuts = [(0, (every, slice(i * width, (i + 1) * width))) for i in range(4)]
        in_all = finish(info, in_done, (cuts[:2], cuts[2:]), rows, [(2, rows, 4 * width)])[0]
        gate_both = call(
            finish_gate_kernel,
            [((2, rows, width), f32)],
            [info] + list(out_done),
            [SMEM, VMEM, VMEM],
            [VMEM],
            room=GLUE_LIMIT,
        )[0]
        places = [(1, ())] + [(0, (slice(i * rows, (i + 1) * rows),)) for i in range(4)]
        layout = ((places[0], places[1], places[2]), (places[0], places[3], places[4]))
        shapes = [(2, 4 * rows, width), (2, rows, width)]
        out_all = finish(info, out_done, layout, rows, shapes)[0]
    crosses, in_all, out_all, gate_both = tie(crosses, in_all, out_all, gate_both)
    crosses = third_returns(grid, info, crosses)
    selfs, crosses[0], incoming = tie(selfs, crosses[0], incoming)
    self_done = last_swap(grid, selfs)
    page_shape = language_in.shape
    got = incoming.astype(f32)
    grad_mine = grad_mine + got[: pages * slots]
    grad_theirs = grad_theirs + got[pages * slots :]
    grad_language = jnp.where(first, grad_mine, grad_theirs).astype(bf16).reshape(page_shape)
    grad_vision = jnp.where(first, grad_theirs, grad_mine).astype(bf16).reshape(page_shape)

    self_qkv_grad, self_proj_grad = attention_grads(self_done)
    crosses, self_qkv_grad, self_proj_grad, grad_language, grad_vision = tie(
        crosses, self_qkv_grad, self_proj_grad, grad_language, grad_vision
    )
    cross_done = last_swap(grid, crosses)
    cross_qkv_grad, cross_proj_grad = attention_grads(cross_done)
    vec_sum = (cross_done[0].astype(f32) + cross_done[1].astype(f32))[:, 2 * rows :]
    vec_both = by_side(vec_sum)
    gate_vec = vec_sum[0, 4, 128 : 128 + rows] + vec_sum[1, 4, 128 : 128 + rows]
    return (
        united.reshape(page_shape),
        grad_language,
        grad_vision,
        cross_qkv_grad,
        cross_proj_grad,
        vec_both[:, 0:3, :rows],
        vec_both[:, 0:3, 256 : 256 + rows],
        vec_both[:, 0:3, 384 : 384 + rows],
        self_qkv_grad,
        self_proj_grad,
        vec_both[:, 0:3, 128 : 128 + rows],
        in_all,
        vec_both[:, 3, : 4 * rows],
        out_all,
        vec_both[:, 4, :rows],
        gate_both,
        gate_vec,
    )


def solution(mesh):
    whole = P(("dp", "rep"), None, None)
    weights = (
        P(None, None, "dp", None),
        P(None, "dp", None),
        P(None, None, "dp"),
        P(None, None, "dp"),
        P(None, None, "dp"),
        P(None, None, "dp", None),
        P(None, "dp", None),
        P(None, None, "dp"),
        P(None, "dp", None),
        P(None, "dp"),
        P(None, "dp", None),
        P(None, "dp"),
        P(None, "dp", None),
        P("dp"),
    )
    return jax.shard_map(
        functools.partial(on_device, Grid(mesh)),
        mesh=mesh,
        in_specs=(whole, whole, P(("dp", "rep")), P(("dp", "rep"))) + weights + (whole,),
        out_specs=(whole, whole, whole) + weights,
        check_vma=False,
    )
```

```python
import functools

import jax
import jax.numpy as jnp
from jax import lax
from jax.experimental import pallas as pl
from jax.experimental.pallas import tpu as pltpu
from jax.sharding import PartitionSpec as P

HEADS = 12
HEAD = 64
norm_epsilon = 1e-05
bf16 = jnp.bfloat16
f32 = jnp.float32
AXES = ("dp", "rep")
VMEM_LIMIT = 27 << 20
GLUE_LIMIT = 20 << 20
HBM = pl.BlockSpec(memory_space=pltpu.HBM)
VMEM = pl.BlockSpec(memory_space=pltpu.VMEM)
SMEM = pl.BlockSpec(memory_space=pltpu.SMEM)


class Grid:
    def __init__(self, mesh):
        self.n = mesh.shape["dp"]
        self.r = mesh.shape["rep"]
        self.high = self.n >> 1
        self.partner = self.n >> 2
        self.groups = [0, self.partner, self.high, self.high | self.partner]
        low = []
        bit = 1
        while bit < self.partner:
            low.append(bit)
            bit *= 2
        self.orders = [low, low[::-1]]
        self.high_bit = len(low) + 1

    def across(self, values, mask):
        pairs = [
            (d * self.r + c, (d ^ mask) * self.r + c) for d in range(self.n) for c in range(self.r)
        ]
        return lax.ppermute(values, AXES, pairs)

    def swap_cores(self, values):
        pairs = [
            (d * self.r + c, d * self.r + (c ^ 1)) for d in range(self.n) for c in range(self.r)
        ]
        return lax.ppermute(values, AXES, pairs)

    def hop(self, values, step):
        pairs = []
        for d in range(self.n):
            for c in range(self.r):
                mask = self.orders[c % 2][step]
                pairs.append((d * self.r + c, (d ^ mask) * self.r + c))
        return lax.ppermute(values, AXES, pairs)

    def place(self, info):
        core, me = info[1], info[2]
        first = jnp.right_shift(me, core) & 1
        second = jnp.right_shift(me, 1 - core) & 1
        return jnp.right_shift(me, 2), first, second, 1 + core, 2 - core

    def masks(self, core):
        found = [0]
        for low, high in zip(*self.orders, strict=True):
            bit = low + core * (high - low)
            found = found + [m ^ bit for m in found]
        return found


def call(kernel, outs, ins, specs, out_specs, scratch=(), flops=0, moved=0, room=VMEM_LIMIT):
    results = pl.pallas_call(
        kernel,
        out_shape=[jax.ShapeDtypeStruct(shape, dtype) for shape, dtype in outs],
        in_specs=specs,
        out_specs=out_specs,
        scratch_shapes=list(scratch),
        compiler_params=pltpu.CompilerParams(vmem_limit_bytes=room),
        cost_estimate=pl.CostEstimate(flops=flops, bytes_accessed=moved, transcendentals=0),
    )(*ins)
    return list(results)


def pair_kernel(bit_of, info_ref, *refs):
    mine, other = refs[:2]
    bit = jnp.right_shift(info_ref[2], bit_of) & 1
    start = 0
    for out in refs[2:]:
        end = start + out.shape[-2]
        out[bit] = mine[..., start:end, :]
        out[1 - bit] = other[..., start:end, :]
        start = end


def pair(info, bit_of, mine, other, parts=None):
    shape = mine.shape
    parts = [shape[-2]] if parts is None else parts
    if shape[-2] % 16:
        bit = jnp.right_shift(info[2], bit_of) & 1
        both = jnp.where(bit == 0, jnp.stack([mine, other]), jnp.stack([other, mine]))
        starts = [sum(parts[:i]) for i in range(len(parts))]
        return [both[..., s : s + p, :] for s, p in zip(starts, parts, strict=True)]
    return call(
        functools.partial(pair_kernel, bit_of),
        [((2,) + shape[:-2] + (part, shape[-1]), bf16) for part in parts],
        [info, mine, other],
        [SMEM, VMEM, VMEM],
        [VMEM] * len(parts),
        room=GLUE_LIMIT,
    )


def group_kernel(high_bit, info_ref, *refs):
    group = jnp.right_shift(info_ref[2], high_bit - 1)
    for k, source in enumerate(refs[:4]):
        refs[4][jnp.bitwise_xor(group, k)] = source[...]


def all_meet(grid, info, mine, theirs):
    return [
        mine,
        grid.across(theirs, grid.groups[1]),
        grid.across(theirs, grid.groups[2]),
        grid.across(mine, grid.groups[3]),
    ]


def grouped(grid, info, sources):
    shape = sources[0].shape
    if shape[0] % 16:
        group = jnp.right_shift(info[2], grid.high_bit - 1)
        return jnp.take(jnp.stack(sources), jnp.arange(4) ^ group, axis=0)
    return call(
        functools.partial(group_kernel, grid.high_bit),
        [((4,) + shape, bf16)],
        [info] + sources,
        [SMEM] + [VMEM] * 4,
        [VMEM],
        room=GLUE_LIMIT,
    )[0]


def join_kernel(grid, info_ref, mine, other, out):
    bit = grid.place(info_ref)[1]
    for g in range(4):
        out[g, bit] = mine[g]
        out[g, 1 - bit] = other[g]


def join_pair(grid, info, pieces):
    shape = pieces[0].shape
    return call(
        functools.partial(join_kernel, grid),
        [((4, 2) + shape[1:], bf16)],
        [info] + pieces,
        [SMEM] + [VMEM] * 2,
        [VMEM],
        room=GLUE_LIMIT,
    )[0]


def tie(*values):
    flat, tree = jax.tree.flatten(values)
    return jax.tree.unflatten(tree, lax.optimization_barrier(flat))


def meet(grid, info, held):
    rows, width = held.shape[1:]
    received = grid.across(held, grid.groups[3])

    def place(received):
        return pair(info, grid.high_bit, held, received)[0].reshape(4, rows, width)

    return received, place


def join_all_kernel(grid, info_ref, mine, first_away, second_away, both_away, out):
    unused, first, second, unused, unused = grid.place(info_ref)
    for g in range(4):
        out[g, second, first] = mine[g]
        out[g, second, 1 - first] = first_away[g]
        out[g, 1 - second, first] = second_away[g]
        out[g, 1 - second, 1 - first] = both_away[g]


def second_hops(grid, held):
    if len(grid.orders[0]) == 2:
        return [held, grid.hop(held, 0), grid.hop(held, 1)]
    for step in range(len(grid.orders[0])):
        held = jnp.concatenate([held, grid.hop(held, step)], 0)
    return [held]


def third_hops(grid, pieces):
    return pieces + [grid.hop(pieces[1], 1)] if len(pieces) == 3 else pieces


def ahead(grid, info, pieces):
    if len(pieces) == 1:
        return []
    held = join_pair(grid, info, pieces[:2])
    return [held, pieces[2], grid.swap_cores(held), grid.swap_cores(pieces[2])]


def extra_rows(grid, info, pieces, start, keep):
    held = pieces[0][:, start : start + keep]
    return jnp.take(held, jnp.argsort(slots_of(grid, info)), axis=0)


def slots_of(grid, info):
    masks = jnp.stack(grid.masks(info[1])).astype(jnp.int32)[:, None]
    groups = jnp.arange(4, dtype=jnp.int32)[None, :] * grid.partner
    return ((masks ^ (info[2] & (grid.partner - 1))) | groups).reshape(-1)


def whole(grid, info, pieces, rows, count, early=()):
    if early:
        mine, away, mine_swapped, away_swapped = early
        return [mine, away, pieces[3], mine_swapped, away_swapped, grid.swap_cores(pieces[3])]
    if len(pieces) == 4:
        shape = pieces[0].shape
        held = call(
            functools.partial(join_all_kernel, grid),
            [((4, 2, 2) + shape[1:], bf16)],
            [info] + pieces,
            [SMEM] + [VMEM] * 4,
            [VMEM],
            room=GLUE_LIMIT,
        )[0]
        return [held, grid.swap_cores(held)]
    held = pieces[0][:, : count * rows]
    held = jnp.take(held, jnp.argsort(slots_of(grid, info)), axis=0).reshape(grid.n, count, rows, -1).transpose(1, 0, 2, 3)
    held = held.reshape(count, grid.n * rows, -1)
    return [held, grid.swap_cores(held)]


def split_kernel(grid, extra, info_ref, keep, received, *refs):
    outs = refs[-2:]
    count, rows = keep.shape[0], keep.shape[2]
    unused, unused, second, first_step, second_step = grid.place(info_ref)
    for g in range(4):
        for a in range(2):
            for b, out in ((second, outs[0]), (1 - second, outs[1])):
                source = 4 * g + a * first_step + b * second_step
                for j in range(count):
                    total = keep[j, source].astype(f32) + received[j, source].astype(f32)
                    out[g, a, j * rows : (j + 1) * rows] = total.astype(bf16)
                if extra:
                    out[g, a, count * rows :] = refs[0][source]


def added(a, b):
    return (a.astype(f32) + b.astype(f32)).astype(bf16)


def first_returns(grid, info, keep, received, more=None):
    blocks, n, rows, width = keep.shape
    depth = blocks * rows + (0 if more is None else more.shape[1])
    extra = [] if more is None else [more]
    if len(grid.orders[0]) != 2:
        total = added(keep, received).transpose(1, 0, 2, 3).reshape(n, blocks * rows, width)
        total = jnp.concatenate([total] + extra, 1)
        held = jnp.take(total, slots_of(grid, info), axis=0)
        for step in reversed(range(len(grid.orders[0]))):
            half = held.shape[0] // 2
            held = added(held[:half], grid.hop(held[half:], step))
        return [held]
    held, sent = call(
        functools.partial(split_kernel, grid, len(extra)),
        [((4, 2, depth, width), bf16)] * 2,
        [info, keep, received] + extra,
        [SMEM, VMEM, VMEM] + [VMEM] * len(extra),
        [VMEM] * 2,
        room=GLUE_LIMIT,
    )
    return [held, grid.hop(sent, 1)]


def merge_kernel(grid, info_ref, *refs):
    near, far = refs[-2:]
    bit = grid.place(info_ref)[1]
    start = 0
    for held, received in zip(refs[:-2:2], refs[1:-2:2], strict=True):
        at = slice(start, start + held.shape[2])
        for g in range(4):
            for which, out in ((bit, near), (1 - bit, far)):
                out[g, at] = added(held[g, which], received[g, which])
        start += held.shape[2]


def second_returns(grid, info, *parts):
    if len(parts[0]) == 1:
        return [jnp.concatenate([part[0] for part in parts], 1)]
    depth = sum(part[0].shape[2] for part in parts)
    near, far = call(
        functools.partial(merge_kernel, grid),
        [((4, depth, parts[0][0].shape[3]), bf16)] * 2,
        [info] + [array for part in parts for array in part],
        [SMEM] + [VMEM] * (2 * len(parts)),
        [VMEM] * 2,
        room=GLUE_LIMIT,
    )
    return [near, grid.hop(far, 0)]


def collect_kernel(grid, info_ref, held, received, *outs):
    group = grid.place(info_ref)[0]
    for k, out in enumerate(outs):
        at = jnp.bitwise_xor(group, k)
        out[...] = added(held[at], received[at])


def third_returns(grid, info, pieces):
    if len(pieces) == 1:
        group = jnp.right_shift(info[2], grid.high_bit - 1)
        totals = [
            lax.dynamic_index_in_dim(pieces[0], group ^ g, 0, keepdims=False) for g in range(4)
        ]
    else:
        totals = call(
            functools.partial(collect_kernel, grid),
            [(pieces[0].shape[1:], bf16)] * 4,
            [info] + pieces,
            [SMEM] + [VMEM] * 2,
            [VMEM] * 4,
            room=GLUE_LIMIT,
        )
    return [totals[0]] + [grid.across(totals[g], grid.groups[g]) for g in (3, 1, 2)]


def last_kernel(near_a, near_b, far_a, far_b, out):
    out[0] = (near_a[...].astype(f32) + near_b[...].astype(f32)).astype(bf16)
    out[1] = (far_a[...].astype(f32) + far_b[...].astype(f32)).astype(bf16)


def last_swap(grid, terms):
    mine = call(
        last_kernel,
        [((2,) + terms[0].shape, bf16)],
        terms,
        [VMEM] * 4,
        [VMEM],
        room=GLUE_LIMIT,
    )[0]
    return mine, grid.swap_cores(mine)


def finish_kernel(layout, rows, info_ref, mine_ref, far_ref, *outs):
    side, core = info_ref[0], info_ref[1]

    def write(which, ref):
        for j, (out, at) in enumerate(layout[which]):
            for k in range(2):
                value = ref[k, j * rows : (j + 1) * rows].astype(f32)
                outs[out][(jnp.bitwise_xor(side, k),) + at] = value

    for which in range(2):
        pl.when(core == which)(functools.partial(write, which, mine_ref))
        pl.when(core != which)(functools.partial(write, which, far_ref))


def finish(info, done, layout, rows, shapes):
    return call(
        functools.partial(finish_kernel, layout, rows),
        [(shape, f32) for shape in shapes],
        [info] + list(done),
        [SMEM, VMEM, VMEM],
        [VMEM] * len(shapes),
        room=GLUE_LIMIT,
    )


def finish_gate_kernel(info_ref, mine_ref, far_ref, out):
    side, core = info_ref[0], info_ref[1]
    rows = out.shape[1]

    def write(own_ref, other_ref):
        for k in range(2):
            own = own_ref[k, :rows].astype(f32)
            out[jnp.bitwise_xor(side, k)] = own + other_ref[1 - k, :rows].astype(f32)

    pl.when(core == 0)(functools.partial(write, mine_ref, far_ref))
    pl.when(core != 0)(functools.partial(write, far_ref, mine_ref))


def nn(a, b):
    return lax.dot_general(a, b, (((1,), (0,)), ((), ())), preferred_element_type=f32)


def nt(a, b):
    return lax.dot_general(a, b, (((1,), (1,)), ((), ())), preferred_element_type=f32)


def tn(a, b):
    return lax.dot_general(a, b, (((0,), (0,)), ((), ())), preferred_element_type=f32)


def block_shapes(grid, count, rows, width, mixed=False):
    if rows % 16 or len(grid.orders[0]) != 2:
        return (4 * grid.n * rows, width) if mixed else (count, grid.n * rows, width)
    inner = (4, rows, width) if mixed else (rows, width)
    return ((4, 2, 2) if mixed else (count, 4, 2, 2)) + inner


def load_blocks(grid, info_ref, sources, blocks, sem, start=0, only=None, mixed=False):
    core = info_ref[1]
    middle = len(sources) // 2

    def load(which, refs):
        count = 1 if only is not None else 2 if mixed else blocks.shape[0] // 2
        first = 0 if only is not None else which * count
        if len(refs[0].shape) == 3:
            for j in range(count):
                pltpu.make_async_copy(refs[0].at[start + j], blocks.at[first + j], sem).start()
            return
        rows = blocks.shape[-2]
        near = jnp.right_shift(info_ref[2], which) & 1
        bit = jnp.right_shift(info_ref[2], 1 - which) & 1

        def copy(source, target):
            pltpu.make_async_copy(source, target, sem).start()

        def place(j, *at):
            return blocks.at[at + (first + j,)] if mixed else blocks.at[(first + j,) + at]

        every = slice(None)
        for j in range(count):
            cut = pl.ds((start + j) * rows, rows)

            def low_first(j=j, cut=cut):
                if len(refs) == 1:
                    copy(refs[0].at[:, :, :, cut], place(j, every, every, every))
                    return
                copy(refs[0].at[:, :, cut], place(j, every, bit, every))
                copy(refs[1].at[:, cut], place(j, every, 1 - bit, near))
                copy(refs[2].at[:, cut], place(j, every, 1 - bit, 1 - near))

            def high_first(j=j, cut=cut):
                if len(refs) == 1:
                    for b in range(2):
                        copy(refs[0].at[:, b, :, cut], place(j, every, every, b))
                    return
                copy(refs[0].at[:, :, cut], place(j, every, every, bit))
                copy(refs[1].at[:, cut], place(j, every, near, 1 - bit))
                copy(refs[2].at[:, cut], place(j, every, 1 - near, 1 - bit))

            pl.when(which == 0)(low_first)
            pl.when(which != 0)(high_first)

    if len(sources) == 1:
        pltpu.make_async_copy(sources[0], blocks, sem).start()
    elif only is None:
        load(core, sources[:middle])
        load(1 - core, sources[middle:])
    else:
        pl.when(core == only)(lambda: load(only, sources[:middle]))
        pl.when(core != only)(lambda: load(only, sources[middle:]))
    return pltpu.make_async_copy(blocks, blocks, sem).wait


def matrix(values):
    return values.reshape(-1, values.shape[-1])


def load_inputs(info_ref, language, vision, both_far, src_ref, oth_ref, sem):
    half = language.shape[0]

    def copies(mine, mine_at, other, other_at):
        return [
            pltpu.make_async_copy(mine, src_ref.at[pl.ds(0, half)], sem.at[0]),
            pltpu.make_async_copy(
                both_far.at[pl.ds(mine_at, half)], src_ref.at[pl.ds(half, half)], sem.at[1]
            ),
            pltpu.make_async_copy(other, oth_ref.at[pl.ds(0, half)], sem.at[2]),
            pltpu.make_async_copy(
                both_far.at[pl.ds(other_at, half)], oth_ref.at[pl.ds(half, half)], sem.at[3]
            ),
        ]

    @pl.when(info_ref[0] == 0)
    def _():
        for copy in copies(language, 0, vision, half):
            copy.start()

    @pl.when(info_ref[0] != 0)
    def _():
        for copy in copies(vision, half, language, 0):
            copy.start()

    def wait():
        for copy in copies(language, 0, vision, half):
            copy.wait()

    return wait


def store_blocks(core, blocks, keep, send, sem):
    count = keep.shape[0]
    copies = []
    for j in range(count):
        copies.append(pltpu.make_async_copy(blocks.at[core * count + j], keep.at[j], sem.at[j]))
        copies.append(
            pltpu.make_async_copy(
                blocks.at[(1 - core) * count + j], send.at[j], sem.at[count + j]
            )
        )
    for copy in copies:
        copy.start()

    def wait():
        for copy in copies:
            copy.wait()

    return wait


def normalised(values):
    mean_row = jnp.mean(values, axis=-1, keepdims=True)
    centred = values - mean_row
    variance = jnp.mean(centred * centred, axis=-1, keepdims=True)
    scale = lax.rsqrt(variance + norm_epsilon)
    return centred * scale, scale


def norm_back(values, grads, gain):
    unit, scale = normalised(values)
    scaled = grads * gain
    first = jnp.mean(scaled, axis=-1, keepdims=True)
    second = jnp.mean(scaled * unit, axis=-1, keepdims=True)
    return (scaled - first - unit * second) * scale, grads * unit


def lane_masks():
    lanes = lax.broadcasted_iota(jnp.int32, (128, 2 * HEAD), 1)
    left = (lanes < HEAD).astype(f32).astype(bf16)
    right = (lanes >= HEAD).astype(f32).astype(bf16)
    return lanes < HEAD, left, right


def two_heads(values, left, right):
    return jnp.concatenate([values * left, values * right], 0)


def softened(queries, keys_both, barred):
    scores = []
    for pair, keys in zip(queries, keys_both, strict=True):
        both = nt(pair, keys) * HEAD ** (-0.5)
        slots = both.shape[0]
        scores += [both[:, :slots], both[:, slots:]]
    scores = [jnp.where(barred, -1000000000.0, part) for part in scores]
    peaks = [jnp.max(part, axis=-1, keepdims=True) for part in scores]
    weights = [jnp.exp(part - peak) for part, peak in zip(scores, peaks, strict=True)]
    totals = [1.0 / jnp.sum(part, axis=-1, keepdims=True) for part in weights]
    return [part * total for part, total in zip(weights, totals, strict=True)]


def joined(parts, pair):
    return jnp.concatenate([part.astype(bf16) for part in parts[2 * pair : 2 * pair + 2]], 1)


def barred_slots(slots, count):
    return lax.broadcasted_iota(jnp.int32, (slots, slots), 1) >= count


def pages_of(rows, slots, body):
    def step(page, carry):
        body(page, pl.ds(pl.multiple_of(page * slots, slots), slots))
        return carry

    lax.fori_loop(0, rows // slots, step, 0, unroll=2)


def column_sum(values):
    return jnp.sum(values.astype(f32), axis=0, keepdims=True)


def attend_kernel(grid, cross, slots, held, at_table, info_ref, counts_ref, vec_ref, *refs):
    if cross:
        inputs, refs = refs[:3], refs[3:]
    else:
        residual_ref, low_ref = refs[:2]
        refs = refs[2:]
    sources, refs = refs[:held], refs[held:]

    def row(i):
        return vec_ref[at_table[i] : at_table[i] + 1, :]

    q_ref, k_ref, v_ref, o_ref, sum_ref, norm_ref, norm_low_ref = refs[:7]
    blocks, sem = refs[7:9]
    rows = q_ref.shape[0]
    half = rows // 2
    wait_blocks = load_blocks(grid, info_ref, sources, blocks, sem)
    if cross:
        src_ref, oth_ref, in_sem = refs[9:12]
        load_inputs(info_ref, *inputs, src_ref, oth_ref, in_sem)()
    else:
        src_ref = oth_ref = low_ref
    wait_blocks()
    width = q_ref.shape[1]
    q_ref[...] = (nn(src_ref[...], matrix(blocks[0])) + row(0)).astype(bf16)
    k_ref[...] = nn(oth_ref[...], matrix(blocks[1])).astype(bf16)
    v_ref[...] = (nn(oth_ref[...], matrix(blocks[2])) + row(1)).astype(bf16)
    unused, left, right = lane_masks()
    cuts = [slice(at, at + 128) for at in range(0, width, 128)]

    def one_page(page, at):
        soft = softened(
            [q_ref[at, cut] for cut in cuts],
            [two_heads(k_ref[at, cut], left, right) for cut in cuts],
            barred_slots(slots, counts_ref[page]),
        )
        for i, cut in enumerate(cuts):
            mixed = nn(joined(soft, i), two_heads(v_ref[at, cut], left, right))
            o_ref[at, cut] = mixed.astype(bf16)

    pages_of(rows, slots, one_page)
    residual = src_ref[...].astype(f32) if cross else residual_ref[...]
    total = residual + nn(o_ref[...], matrix(blocks[3])) + row(2)
    sum_ref[...] = total
    result = normalised(total)[0] * row(3) + row(4)
    norm_ref[...] = result
    norm_low_ref[...] = result.astype(bf16)


def attend(grid, cross, slots, info, counts, vectors, at_table, inputs, weights):
    width = weights[0].shape[-1]
    rows = counts.shape[0] * slots
    blocks = block_shapes(grid, 4, grid.rows, width)
    scratch = [pltpu.VMEM(blocks, bf16), pltpu.SemaphoreType.DMA]
    if cross:
        scratch += [pltpu.VMEM((rows, width), bf16)] * 2 + [pltpu.SemaphoreType.DMA((4,))]
    return call(
        functools.partial(attend_kernel, grid, cross, slots, len(weights), at_table),
        [((rows, width), bf16)] * 4 + [((rows, width), f32)] * 2 + [((rows, width), bf16)],
        [info, counts, vectors] + list(inputs) + list(weights),
        [SMEM, SMEM, VMEM] + ([HBM] * 3 if cross else [VMEM] * 2) + [HBM] * len(weights),
        [VMEM] * 7,
        scratch,
        flops=8 * rows * width * width + 8 * rows * slots * width,
        moved=4 * width * width * 2 + rows * width * 20,
    )


def hidden_kernel(grid, held, info_ref, shift_ref, low_ref, *refs):
    sources = refs[:held]
    active_ref, slope_ref, blocks, sem = refs[held:]
    load_blocks(grid, info_ref, sources, blocks, sem)()
    width = low_ref.shape[1]
    for b in range(4):
        at = slice(b * width, (b + 1) * width)
        hidden = nn(low_ref[...], matrix(blocks[b])) + shift_ref[0:1, at]
        square = hidden * hidden
        bent = jnp.tanh(0.7978845608028654 * (hidden + 0.044715 * square * hidden))
        active_ref[:, at] = (0.5 * hidden * (1.0 + bent)).astype(bf16)
        slope = 0.5 * (1.0 + bent) + 0.5 * hidden * (1.0 - bent * bent) * (
            0.7978845608028654 * (1.0 + 3.0 * 0.044715 * square)
        )
        slope_ref[:, at] = slope.astype(bf16)


def hidden_layer(grid, info, shift, low, weights):
    rows, width = low.shape
    return call(
        functools.partial(hidden_kernel, grid, len(weights)),
        [((rows, 4 * width), bf16)] * 2,
        [info, shift, low] + list(weights),
        [SMEM, VMEM, VMEM] + [HBM] * len(weights),
        [VMEM, VMEM],
        [pltpu.VMEM(block_shapes(grid, 4, grid.rows, width), bf16), pltpu.SemaphoreType.DMA],
        flops=8 * rows * width * width,
        moved=8 * width * width + rows * width * 18,
    )


def store_wide(core, wide, keep, send, sem):
    copies = []
    for j in range(2):
        for which, target in ((core, keep), (1 - core, send)):
            copies.append(pltpu.make_async_copy(wide.at[:, 2 * which + j], target.at[j], sem))
    for copy in copies:
        copy.start()
    pltpu.make_async_copy(wide, wide, sem).wait()


def branch_kernel(grid, held, info_ref, vec_ref, active_ref, residual_ref, *refs):
    sources = refs[:held]
    sum_ref, norm_ref, far_ref, wide, sem = refs[held:]
    load_blocks(grid, info_ref, sources, wide, sem, mixed=True)()
    half = residual_ref.shape[0] // 2
    total = residual_ref[...] + nn(active_ref[...], matrix(wide[...])) + vec_ref[12:13, :]
    sum_ref[...] = total
    result = normalised(total)[0] * vec_ref[8:9, :] + vec_ref[11:12, :]
    norm_ref[...] = result[:half]
    far_ref[...] = result[half:].astype(bf16)


def branch_layer(grid, info, vectors, active, residual, weights):
    rows, width = residual.shape
    return call(
        functools.partial(branch_kernel, grid, len(weights)),
        [((rows, width), f32), ((rows // 2, width), f32), ((rows // 2, width), bf16)],
        [info, vectors, active, residual] + list(weights),
        [SMEM, VMEM, VMEM, VMEM] + [HBM] * len(weights),
        [VMEM] * 3,
        [pltpu.VMEM(block_shapes(grid, 4, grid.rows, width, True), bf16), pltpu.SemaphoreType.DMA],
        flops=8 * rows * width * width,
        moved=8 * width * width + rows * width * 20,
    )


def gate_kernel(grid, held, info_ref, shift_ref, third_ref, far_ref, cotangent_ref, *refs):
    sources = refs[:held]
    united_ref, grad_own_ref, grad_far_ref, grad_shift_ref, keep_ref, send_ref = refs[held : held + 6]
    blocks, sem, grads, mix_ref, low_ref, out_sem = refs[held + 6 :]
    load_blocks(grid, info_ref, sources, blocks, sem, 2)()
    first = info_ref[0] == 0
    low_ref[...] = third_ref[...].astype(bf16)
    logits = nn(low_ref[...], matrix(blocks[0])) + nn(far_ref[...], matrix(blocks[1])) + shift_ref[13:14, :]
    mixing = 1.0 / (1.0 + jnp.exp(-logits))
    share = jnp.where(first, mixing, 1.0 - mixing)
    mine, other = third_ref[...], far_ref[...].astype(f32)
    united_ref[...] = (share * mine + (1.0 - share) * other).astype(bf16)
    cotangent = cotangent_ref[...].astype(f32)
    gap = jnp.where(first, mine - other, other - mine)
    grad = (cotangent * gap * mixing * (1.0 - mixing)).astype(bf16)
    mix_ref[...] = grad
    grad_shift_ref[0:1, :] = column_sum(grad)
    direct = cotangent * share
    grad_own_ref[...] = direct + nt(mix_ref[...], matrix(blocks[0]))
    grad_far_ref[...] = (cotangent - direct + nt(mix_ref[...], matrix(blocks[1]))).astype(bf16)
    grads[0] = tn(low_ref[...], mix_ref[...]).astype(bf16)
    grads[1] = tn(far_ref[...], mix_ref[...]).astype(bf16)
    store_blocks(info_ref[1], grads, keep_ref, send_ref, out_sem)()


def gate_layer(grid, info, shift, third, far, cotangent, weights):
    rows, width = third.shape
    blocks = (2, width, width)
    return call(
        functools.partial(gate_kernel, grid, len(weights)),
        [
            ((rows, width), bf16),
            ((rows, width), f32),
            ((rows, width), bf16),
            ((8, width), f32),
            ((1,) + blocks[1:], bf16),
            ((1,) + blocks[1:], bf16),
        ],
        [info, shift, third, far, cotangent] + list(weights),
        [SMEM] + [VMEM] * 4 + [HBM] * len(weights),
        [VMEM] * 4 + [HBM] * 2,
        [
            pltpu.VMEM(block_shapes(grid, 2, grid.rows, width), bf16),
            pltpu.SemaphoreType.DMA,
            pltpu.VMEM(blocks, bf16),
            pltpu.VMEM((rows, width), bf16),
            pltpu.VMEM((rows, width), bf16),
            pltpu.SemaphoreType.DMA((2,)),
        ],
        flops=12 * rows * width * width,
        moved=8 * width * width + rows * width * 14,
    )


def branch_back_kernel(
    wide_out,
    info_ref,
    gain_ref,
    sum_ref,
    grad_own_ref,
    grad_far_ref,
    active_ref,
    grad_sum_ref,
    grad_low_ref,
    vec_ref,
    *refs,
):
    rows, width = sum_ref.shape
    half = rows // 2
    vec_ref[...] = jnp.zeros_like(vec_ref)
    for offset, grads_ref in ((0, grad_own_ref), (half, grad_far_ref)):
        at = slice(offset, offset + half)
        grads = grads_ref[...].astype(f32)
        back, gain_rows = norm_back(sum_ref[at, :], grads, gain_ref[8:9, :])
        low = back.astype(bf16)
        grad_sum_ref[at, :] = back
        grad_low_ref[at, :] = low
        vec_ref[0:1, :] += column_sum(gain_rows)
        vec_ref[1:2, :] += column_sum(grads)
        vec_ref[2:3, :] += column_sum(low)
    wide, sem = refs[-2:]
    for b in range(4):
        at = slice(b * width, (b + 1) * width)
        part = tn(active_ref[:, at], grad_low_ref[...]).astype(bf16)
        if wide_out:
            devices = wide.shape[0] // 4
            wide[b * devices : (b + 1) * devices] = part.reshape((devices,) + wide.shape[1:])
        else:
            wide[at, :] = part
    if wide_out:
        store_wide(info_ref[1], wide, refs[0], refs[1], sem)
    else:
        copy = pltpu.make_async_copy(wide, refs[0], sem)
        copy.start()
        copy.wait()


def branch_back(grid, info, gain, sums, grad_own, grad_far, active, piece):
    rows, width = sums.shape
    wide_out = piece % 16 == 0
    target = (2, grid.n, piece, width) if wide_out else (4 * width, width)
    outs = [(target, bf16)] * (2 if wide_out else 1)
    return call(
        functools.partial(branch_back_kernel, wide_out),
        [((rows, width), f32), ((rows, width), bf16), ((8, width), f32)] + outs,
        [info, gain, sums, grad_own, grad_far, active],
        [SMEM] + [VMEM] * 5,
        [VMEM] * 3 + [HBM] * len(outs),
        [
            pltpu.VMEM((grid.n, 4, piece, width) if wide_out else (4 * width, width), bf16),
            pltpu.SemaphoreType.DMA,
        ],
        flops=8 * rows * width * width,
        moved=8 * width * width + rows * width * 24,
    )


def hidden_back_kernel(grid, held, info_ref, grad_low_ref, slope_ref, low_ref, *refs):
    core = info_ref[1]
    grad_hidden_ref, vec_ref, keep_ref, send_ref, wide, sem, grads, out_sem = refs[held:]
    load_blocks(grid, info_ref, refs[:held], wide, sem, mixed=True)()
    whole_wide = matrix(wide[...])
    width = low_ref.shape[1]
    for b in range(4):
        at = slice(b * width, (b + 1) * width)
        low = (nt(grad_low_ref[...], whole_wide[at, :]) * slope_ref[:, at].astype(f32)).astype(bf16)
        grad_hidden_ref[:, at] = low
        vec_ref[0:1, at] = column_sum(low)
        grads[b] = tn(low_ref[...], low).astype(bf16)
    store_blocks(core, grads, keep_ref, send_ref, out_sem)()


def hidden_back(grid, info, grad_low, slope, low, weights):
    rows, width = low.shape
    blocks = (4, width, width)
    return call(
        functools.partial(hidden_back_kernel, grid, len(weights)),
        [((rows, 4 * width), bf16), ((8, 4 * width), f32)] + [((2,) + blocks[1:], bf16)] * 2,
        [info, grad_low, slope, low] + list(weights),
        [SMEM] + [VMEM] * 3 + [HBM] * len(weights),
        [VMEM] * 2 + [HBM] * 2,
        [
            pltpu.VMEM(block_shapes(grid, 4, grid.rows, width, True), bf16),
            pltpu.SemaphoreType.DMA,
            pltpu.VMEM(blocks, bf16),
            pltpu.SemaphoreType.DMA((4,)),
        ],
        flops=16 * rows * width * width,
        moved=16 * width * width + rows * width * 30,
    )


def second_back_kernel(
    grid, held, info_ref, gain_ref, sum_ref, grad_ref, grad_hidden_ref, *refs
):
    grad_sum_ref, vec_ref, blocks, sem = refs[held:]
    load_blocks(grid, info_ref, refs[:held], blocks, sem)()
    width = sum_ref.shape[1]
    total = grad_ref[...]
    for b in range(4):
        total += nt(grad_hidden_ref[:, b * width : (b + 1) * width], matrix(blocks[b]))
    grad_sum_ref[...] = norm_back_into(vec_ref, sum_ref[...], total, gain_ref[7:8, :])


def norm_back_into(vec_ref, sums, grads, gain):
    back, gain_rows = norm_back(sums, grads, gain)
    vec_ref[0:1, :] = column_sum(gain_rows)
    vec_ref[1:2, :] = column_sum(grads)
    return back


def second_back(grid, info, gain, sums, grads, grad_hidden, weights):
    rows, width = sums.shape
    return call(
        functools.partial(second_back_kernel, grid, len(weights)),
        [((rows, width), f32), ((8, width), f32)],
        [info, gain, sums, grads, grad_hidden] + list(weights),
        [SMEM] + [VMEM] * 4 + [HBM] * len(weights),
        [VMEM] * 2,
        [pltpu.VMEM(block_shapes(grid, 4, grid.rows, width), bf16), pltpu.SemaphoreType.DMA],
        flops=8 * rows * width * width,
        moved=8 * width * width + rows * width * 20,
    )


def scores_back_kernel(
    grid, cross, slots, held, info_ref, counts_ref, grad_ref, q_ref, k_ref, v_ref, o_ref, *refs
):
    count = 3 if cross else 1
    inputs, sources, refs = refs[:count], refs[count : count + held], refs[count + held :]
    dq_ref, dk_ref, dv_ref, vec_ref, keep_ref, send_ref = refs[:6]
    weight, sem, low_grad, grad_o, grads, out_sem = refs[6:12]
    wait_block = load_blocks(grid, info_ref, sources, weight, sem, 1, 1)
    if cross:
        src_ref, oth_ref, in_sem = refs[12:]
        wait_inputs = load_inputs(info_ref, *inputs, src_ref, oth_ref, in_sem)
    else:
        src_ref = oth_ref = inputs[0]
    rows, width = q_ref.shape
    low = grad_ref[...].astype(bf16)
    low_grad[...] = low
    vec_ref[2:3, :] = column_sum(low)
    grads[3] = tn(o_ref[...], low_grad[...]).astype(bf16)
    wait_block()
    grad_o[...] = nt(low_grad[...], matrix(weight[0])).astype(bf16)
    left_lanes, left, right = lane_masks()
    cuts = [slice(at, at + 128) for at in range(0, width, 128)]

    def one_page(page, at):
        keys = [two_heads(k_ref[at, cut], left, right) for cut in cuts]
        soft = softened(
            [q_ref[at, cut] for cut in cuts], keys, barred_slots(slots, counts_ref[page])
        )
        grad_soft = []
        for cut in cuts:
            both = nt(grad_o[at, cut], two_heads(v_ref[at, cut], left, right))
            grad_soft += [both[:, :slots], both[:, slots:]]
        weighted = [a * b for a, b in zip(soft, grad_soft, strict=True)]
        sums = [jnp.sum(part, axis=-1, keepdims=True) for part in weighted]
        grad_scores = [w - p * t for w, p, t in zip(weighted, soft, sums, strict=True)]
        for i, cut in enumerate(cuts):
            dv = tn(joined(soft, i), grad_o[at, cut])
            dv_ref[at, cut] = jnp.where(left_lanes, dv[:slots], dv[slots:]).astype(bf16)
        for i, cut in enumerate(cuts):
            pair = joined(grad_scores, i)
            dq_ref[at, cut] = (nn(pair, keys[i]) * HEAD ** (-0.5)).astype(bf16)
            dk = tn(pair, q_ref[at, cut]) * HEAD ** (-0.5)
            dk_ref[at, cut] = jnp.where(left_lanes, dk[:slots], dk[slots:]).astype(bf16)

    pages_of(rows, slots, one_page)
    vec_ref[0:1, :] = column_sum(dq_ref[...])
    vec_ref[1:2, :] = column_sum(dv_ref[...])
    if cross:
        wait_inputs()
    grads[0] = tn(src_ref[...], dq_ref[...]).astype(bf16)
    grads[1] = tn(oth_ref[...], dk_ref[...]).astype(bf16)
    grads[2] = tn(oth_ref[...], dv_ref[...]).astype(bf16)
    store_blocks(info_ref[1], grads, keep_ref, send_ref, out_sem)()


def scores_back(grid, cross, slots, info, counts, grad, saved, inputs, weights):
    rows, width = grad.shape
    full = pltpu.VMEM((rows, width), bf16)
    blocks = (4, width, width)
    scratch = [
        pltpu.VMEM(block_shapes(grid, 1, grid.rows, width), bf16),
        pltpu.SemaphoreType.DMA,
        full,
        full,
        pltpu.VMEM(blocks, bf16),
        pltpu.SemaphoreType.DMA((4,)),
    ]
    if cross:
        scratch += [full, full, pltpu.SemaphoreType.DMA((4,))]
    return call(
        functools.partial(scores_back_kernel, grid, cross, slots, len(weights)),
        [((rows, width), bf16)] * 3 + [((8, width), f32)] + [((2,) + blocks[1:], bf16)] * 2,
        [info, counts, grad] + list(saved) + list(inputs) + list(weights),
        [SMEM, SMEM] + [VMEM] * 5 + ([HBM] * 3 if cross else [VMEM]) + [HBM] * len(weights),
        [VMEM] * 4 + [HBM] * 2,
        scratch,
        flops=10 * rows * width * width + 24 * rows * slots * width,
        moved=12 * width * width + rows * width * 20,
    )


def project_back_kernel(grid, cross, held, info_ref, gain_ref, grad_ref, *refs):
    dq_ref, dk_ref, dv_ref = refs[:3]
    refs = refs[3:]
    if cross:
        sources = refs[:held]
        mine_ref, other_ref, far_ref, blocks, sem = refs[held:]
    else:
        sum_ref, sources = refs[0], refs[1 : 1 + held]
        out_ref, vec_ref, blocks, sem = refs[1 + held :]
    load_blocks(grid, info_ref, sources, blocks, sem)()
    half = grad_ref.shape[0] // 2
    mine = grad_ref[...] + nt(dq_ref[...], matrix(blocks[0]))
    other = nt(dk_ref[...], matrix(blocks[1])) + nt(dv_ref[...], matrix(blocks[2]))
    if cross:
        mine_ref[...] = mine[:half]
        other_ref[...] = other[:half]
        far_ref[:half] = other[half:].astype(bf16)
        far_ref[half:] = mine[half:].astype(bf16)
    else:
        vec_ref[...] = jnp.zeros_like(vec_ref)
        out_ref[...] = norm_back_into(vec_ref, sum_ref[...], mine + other, gain_ref[6:7, :])


def project_back(grid, cross, info, gain, grad, parts, sums, weights):
    rows, width = grad.shape
    half = (rows // 2, width)
    if cross:
        outs = [(half, f32), (half, f32), ((rows, width), bf16)]
    else:
        outs = [((rows, width), f32), ((8, width), f32)]
    return call(
        functools.partial(project_back_kernel, grid, cross, len(weights)),
        outs,
        [info, gain, grad] + list(parts) + list(sums) + list(weights),
        [SMEM] + [VMEM] * (5 + len(sums)) + [HBM] * len(weights),
        [VMEM] * len(outs),
        [pltpu.VMEM(block_shapes(grid, 4, grid.rows, width), bf16), pltpu.SemaphoreType.DMA],
        flops=6 * rows * width * width,
        moved=8 * width * width + rows * width * 18,
    )


SPOTS = (
    [(i, 0, 1) for i in range(3)]
    + [(i, 128, 1) for i in range(3)]
    + [(i, 256, 1) for i in range(3)]
    + [(i, 384, 1) for i in range(3)]
    + [(4, 0, 1), (4, 128, 1), (3, 0, 4)]
)
EXTRA = 16


def lay_vectors(cross_bias, self_bias, gains, shifts, out_bias, gate_bias, in_bias, width):
    def at(values, row, lane):
        depth, length = values.shape[1:]
        return jnp.pad(
            values, ((0, 0), (row, EXTRA - row - depth), (lane, width - lane - length))
        )

    gate = jnp.broadcast_to(gate_bias[None, None], (2, 1) + gate_bias.shape)
    return (
        at(cross_bias, 0, 0)
        + at(self_bias, 0, 128)
        + at(gains, 0, 256)
        + at(shifts, 0, 384)
        + at(out_bias[:, None], 4, 0)
        + at(gate, 4, 128)
        + at(in_bias[:, None], 3, 0)
    )


def unlay_kernel(grid, start, info_ref, all_ref, table_ref, wide_ref, held, found, sem):
    copy = pltpu.make_async_copy(all_ref.at[:, :, :, pl.ds(start, EXTRA)], held, sem)
    copy.start()
    copy.wait()
    unused, unused, unused, first_step, second_step = grid.place(info_ref)
    for g in range(4):
        for b in range(2):
            for a in range(2):
                found[4 * g + a * first_step + b * second_step] = held[g, b, a].astype(f32)
    rows = grid.rows
    for p in range(grid.n):
        for i, (row, lane, unused) in enumerate(SPOTS[:-1]):
            table_ref[i : i + 1, p * rows : (p + 1) * rows] = found[p, row : row + 1, lane : lane + rows]
        row, lane, length = SPOTS[-1]
        wide_ref[0:1, p * length * rows : (p + 1) * length * rows] = found[
            p, row : row + 1, lane : lane + length * rows
        ]


def unlay_vectors(grid, info, pieces, start):
    width = pieces[0].shape[-1]
    rows = grid.rows
    if len(pieces[0].shape) == 3:
        found = extra_rows(grid, info, pieces, start, EXTRA).astype(f32)
        parts = [
            found[:, row, lane : lane + length * rows].reshape(-1) for row, lane, length in SPOTS
        ]
        table = jnp.pad(jnp.stack(parts[:-1]), ((0, 2), (0, 0)))
        return table, jnp.pad(parts[-1][None], ((0, 7), (0, 0)))
    return call(
        functools.partial(unlay_kernel, grid, start),
        [((16, width), f32), ((8, 4 * width), f32)],
        [info, pieces[0]],
        [SMEM, HBM],
        [VMEM, VMEM],
        [
            pltpu.VMEM((4, 2, 2, EXTRA, width), bf16),
            pltpu.VMEM((grid.n, EXTRA, width), f32),
            pltpu.SemaphoreType.DMA,
        ],
        room=GLUE_LIMIT,
    )


def relay_kernel(grid, where, *refs):
    out, held = refs[-2:]
    rows = grid.rows
    held[...] = jnp.zeros_like(held)
    for p in range(grid.n):
        for (table, i), (row, lane, length) in zip(where, SPOTS, strict=True):
            size = length * rows
            held[p, row : row + 1, lane : lane + size] = refs[table][i : i + 1, p * size : (p + 1) * size]
    out[...] = held[...].astype(bf16)


def relay_vectors(grid, tables, where):
    width = tables[0].shape[1]
    rows = grid.rows
    if rows % 16:
        out = jnp.zeros((grid.n, EXTRA, width), f32)
        for (table, i), (row, lane, length) in zip(where, SPOTS, strict=True):
            part = tables[table][i].reshape(grid.n, length * rows)
            out = out.at[:, row, lane : lane + length * rows].set(part)
        return out.astype(bf16)
    return call(
        functools.partial(relay_kernel, grid, where),
        [((grid.n, EXTRA, width), bf16)],
        tables,
        [VMEM] * len(tables),
        [VMEM],
        [pltpu.VMEM((grid.n, EXTRA, width), f32)],
        room=GLUE_LIMIT,
    )[0]


def on_device(
    grid,
    language_in,
    vision_in,
    language_count,
    vision_count,
    cross_qkv,
    cross_proj,
    cross_bias,
    norm_gain,
    norm_bias,
    self_qkv,
    self_proj,
    self_bias,
    ffn_in,
    ffn_in_bias,
    ffn_out,
    ffn_out_bias,
    gate_weight,
    gate_bias,
    cotangent,
):
    n = grid.n
    grid.rows = cross_proj.shape[1]
    me = lax.axis_index("dp")
    core = lax.axis_index("rep")
    side = ((me // grid.high) ^ (me // grid.partner)) & 1
    first = side == 0
    info = jnp.stack([side, core, me]).astype(jnp.int32)
    rows, width = cross_proj.shape[1:]
    dim = n * rows
    pages, slots = language_in.shape[:2]
    wide_ok = rows % 16 == 0

    def own(pair):
        return lax.dynamic_index_in_dim(pair, side, 0, keepdims=False)

    def other(pair):
        return lax.dynamic_index_in_dim(pair, 1 - side, 0, keepdims=False)

    vectors = lay_vectors(
        cross_bias, self_bias, norm_gain, norm_bias, ffn_out_bias, gate_bias, ffn_in_bias, width
    )
    groups = [
        [cross_qkv[:, 0], cross_qkv[:, 1], vectors, cross_qkv[:, 2], cross_proj, vectors],
        [self_qkv[:, 0], self_qkv[:, 1], self_qkv[:, 2], self_proj],
        [ffn_in[:, :, i * width : (i + 1) * width] for i in range(4)],
        [ffn_out[:, i * rows : (i + 1) * rows] for i in range(2)]
        + [gate_weight]
        + [ffn_out[:, i * rows : (i + 1) * rows] for i in range(2, 4)]
        + [gate_weight[::-1]],
    ]

    def shards(blocks):
        half = len(blocks) // 2
        parts = [jnp.concatenate(blocks[:half], 1), jnp.concatenate(blocks[half:], 1)]
        mine = lax.dynamic_index_in_dim(jnp.stack(parts), core, 0, keepdims=False)
        return own(mine), other(mine)

    sent = [shards(blocks) for blocks in groups]
    later = [jnp.concatenate([part[k] for part in sent[2:]], 0) for k in range(2)]
    parts = [part[0].shape[0] for part in sent[2:]]
    language = language_in.reshape(pages * slots, width)
    vision = vision_in.reshape(pages * slots, width)
    counts_mine = jnp.stack([language_count, vision_count])
    counts_wide = jnp.pad(counts_mine.astype(bf16), ((0, 14), (0, width - pages)))
    seen = jnp.concatenate([language, vision, counts_wide], 0)

    t1 = all_meet(grid, info, *sent[0])
    u0 = grid.across(sent[1][1], grid.partner)
    t1, u0, later = tie(t1, u0, later)
    t2 = second_hops(grid, grouped(grid, info, t1))
    u1, place_u = meet(grid, info, pair(info, grid.high_bit - 1, sent[1][0], u0)[0])
    later_far = grid.across(later[1], grid.partner)
    t2, u1, later_far, seen = tie(t2, u1, later_far, seen)
    t3 = third_hops(grid, t2)
    u2 = second_hops(grid, place_u(u1))
    w0, x0 = pair(info, grid.high_bit - 1, later[0], later_far, parts)
    w1, place_w = meet(grid, info, w0)
    seen_far = grid.across(seen, grid.partner)
    t3, u2, w1, seen_far, x0 = tie(t3, u2, w1, seen_far, x0)
    cross_w = whole(grid, info, t3, rows, 2)
    table, ffn_in_shift = unlay_vectors(grid, info, cross_w if len(t3) == 4 else t3, 2 * rows)
    counts_far = seen_far[2 * pages * slots :, :pages][:2].astype(jnp.int32)
    counts = jnp.concatenate([own(counts_mine), own(counts_far)])
    other_counts = jnp.concatenate([other(counts_mine), other(counts_far)])
    inputs = [language, vision, seen_far]
    u3 = third_hops(grid, u2)
    w2 = second_hops(grid, place_w(w1))
    x1, place_x = meet(grid, info, x0)
    cq, ck, cv, co, first_sum, first_norm, first_low = attend(
        grid, True, slots, info, other_counts, table, (0, 1, 2, 6, 9), inputs, cross_w
    )
    first_norm, first_low, u3, w2, x1 = tie(first_norm, first_low, u3, w2, x1)
    self_w = whole(grid, info, u3, rows, 2)
    w3 = third_hops(grid, w2)
    x2 = second_hops(grid, place_x(x1))
    sq, sk, sv, so, second_sum, second_norm, second_low = attend(
        grid,
        False,
        slots,
        info,
        counts,
        table,
        (3, 4, 5, 7, 10),
        [first_norm, first_low],
        self_w,
    )
    second_norm, second_low, w3, x2 = tie(second_norm, second_low, w3, x2)
    in_w = whole(grid, info, w3, rows, 2)
    x3 = third_hops(grid, x2)
    early = ahead(grid, info, x2)
    active, slope = hidden_layer(grid, info, ffn_in_shift, second_low, in_w)
    active, second_norm, x3, early = tie(active, second_norm, x3, early)
    gate_w = out_w = whole(grid, info, x3, rows, 3, early)
    if len(out_w) == 2:
        both = jnp.where(core == 0, jnp.stack(out_w), jnp.stack(out_w[::-1]))[:, :2]
        both = both.reshape(4, n, rows, width).transpose(1, 0, 2, 3)
        out_w = [both.reshape(4 * dim, width)]
    third_sum, third_own, third_send = branch_layer(
        grid, info, table, active, second_norm, out_w
    )
    third_far = grid.across(third_send, grid.partner)
    cotangent_rows = cotangent.reshape(pages * slots, width)
    united, grad_third_own, grad_third_send, grad_gate_shift, gate_keep, gate_send = gate_layer(
        grid, info, table, third_own, third_far, cotangent_rows, gate_w
    )

    def by_piece(values):
        return values.reshape(values.shape[0], n, rows, width)

    gate_keep, gate_send = by_piece(gate_keep), by_piece(gate_send)
    gate_got = grid.swap_cores(gate_send)
    grad_third_far = grid.across(grad_third_send, grid.partner)
    gate = first_returns(grid, info, gate_keep, gate_got)
    gate[0], grad_third_far = tie(gate[0], grad_third_far)
    grad_third_sum, grad_branch_low, vec_third, *out_grads = branch_back(
        grid, info, table, third_sum, grad_third_own, grad_third_far, active, rows
    )
    if len(out_grads) == 1:
        by_core = out_grads[0].reshape(n, 2, 2, rows, width).transpose(1, 2, 0, 3, 4)
        out_grads = [
            lax.dynamic_index_in_dim(by_core, c, 0, keepdims=False) for c in (core, 1 - core)
        ]
    out_keep, out_send = out_grads
    gate, grad_branch_low, out_keep, out_send = tie(gate, grad_branch_low, out_keep, out_send)
    out_got = grid.swap_cores(out_send)
    grad_hidden, vec_hidden, in_keep, in_send = hidden_back(
        grid, info, grad_branch_low, slope, second_low, out_w
    )
    out_got, grad_hidden, in_keep, in_send = tie(out_got, grad_hidden, in_keep, in_send)
    in_keep, in_send = by_piece(in_keep), by_piece(in_send)
    in_got = grid.swap_cores(in_send)
    outs = first_returns(grid, info, out_keep, out_got)
    grad_second_sum, vec_second = second_back(
        grid, info, table, second_sum, grad_third_sum, grad_hidden, in_w
    )
    outs, in_got, grad_second_sum = tie(outs, in_got, grad_second_sum)
    ins = first_returns(grid, info, in_keep, in_got)
    outs = second_returns(grid, info, outs)
    *self_parts, vec_self, self_keep, self_send = scores_back(
        grid, False, slots, info, counts, grad_second_sum, [sq, sk, sv, so], [first_low], self_w
    )
    outs, ins, self_parts, self_keep, self_send = tie(outs, ins, self_parts, self_keep, self_send)
    self_keep, self_send = by_piece(self_keep), by_piece(self_send)
    self_got = grid.swap_cores(self_send)
    ins = second_returns(grid, info, gate, ins)
    outs = third_returns(grid, info, outs)
    grad_first_sum, vec_first = project_back(
        grid, False, info, table, grad_second_sum, self_parts, [first_sum], self_w
    )
    ins, outs, self_got, grad_first_sum = tie(ins, outs, self_got, grad_first_sum)
    selfs = first_returns(grid, info, self_keep, self_got)
    ins = third_returns(grid, info, ins)
    *cross_parts, vec_cross, cross_keep, cross_send = scores_back(
        grid, True, slots, info, other_counts, grad_first_sum, [cq, ck, cv, co], inputs, cross_w
    )
    selfs, ins, cross_parts, cross_keep, cross_send = tie(
        selfs, ins, cross_parts, cross_keep, cross_send
    )
    cross_keep, cross_send = by_piece(cross_keep), by_piece(cross_send)
    cross_got = grid.swap_cores(cross_send)
    selfs = second_returns(grid, info, selfs)
    tables = [vec_cross, vec_self, vec_first, vec_second, vec_third, grad_gate_shift, vec_hidden]
    where = [(0, 0), (0, 1), (0, 2), (1, 0), (1, 1), (1, 2)]
    where += [(2, 0), (3, 0), (4, 0), (2, 1), (3, 1), (4, 1), (4, 2), (5, 0), (6, 0)]
    grad_vec = relay_vectors(grid, tables, where)
    grad_mine, grad_theirs, outgoing = project_back(
        grid, True, info, table, grad_first_sum, cross_parts, [], cross_w
    )
    cross_got, outgoing, selfs, outs, grad_vec = tie(cross_got, outgoing, selfs, outs, grad_vec)
    crosses = first_returns(grid, info, cross_keep, cross_got, grad_vec)
    incoming = grid.across(outgoing, grid.partner)
    selfs = third_returns(grid, info, selfs)
    crosses, selfs = tie(crosses, selfs)
    crosses = second_returns(grid, info, crosses)
    crosses[0], outs, ins = tie(crosses[0], outs, ins)
    out_done = last_swap(grid, outs)
    in_done = last_swap(grid, ins)

    def sides(near, far):
        return jnp.where(first, jnp.stack([near, far]), jnp.stack([far, near]))

    def finished(done, count, start=0):
        mine, far = [part[:, start * rows : (start + count) * rows] for part in done]
        mine, far = [part.reshape(2, count, rows, width) for part in (mine, far)]
        both = jnp.where(core == 0, jnp.concatenate([mine, far], 1), jnp.concatenate([far, mine], 1))
        return both.astype(f32)

    def by_side(both):
        return jnp.where(first, both, both[::-1])

    def attention_grads(done):
        if rows % 16:
            both = by_side(finished(done, 2))
            return [both[:, 0:3], both[:, 3]]
        layout = (((0, (0,)), (0, (1,))), ((0, (2,)), (1, ())))
        return finish(info, done, layout, rows, [(2, 3, rows, width), (2, rows, width)])

    if rows % 16:
        in_all = by_side(finished(in_done, 2, 1)).transpose(0, 2, 1, 3).reshape(2, rows, 4 * width)
        gate_all = finished(in_done, 1)
        gate_both = sides(gate_all[0, 0] + gate_all[1, 1], gate_all[0, 1] + gate_all[1, 0])
        out_all = by_side(finished(out_done, 2)).reshape(2, 4 * rows, width)
    else:
        every = slice(None)
        cuts = [(0, (every, slice(i * width, (i + 1) * width))) for i in range(4)]
        layout = [[(1, ())] + cuts[:2], [(1, ())] + cuts[2:]]
        in_all = finish(info, in_done, layout, rows, [(2, rows, 4 * width), (2, rows, width)])[0]
        gate_both = call(
            finish_gate_kernel,
            [((2, rows, width), f32)],
            [info] + list(in_done),
            [SMEM, VMEM, VMEM],
            [VMEM],
            room=GLUE_LIMIT,
        )[0]
        places = [(0, (slice(i * rows, (i + 1) * rows),)) for i in range(4)]
        layout = (places[:2], places[2:])
        out_all = finish(info, out_done, layout, rows, [(2, 4 * rows, width)])[0]
    crosses, in_all, out_all, gate_both = tie(crosses, in_all, out_all, gate_both)
    crosses = third_returns(grid, info, crosses)
    selfs, crosses[0], incoming = tie(selfs, crosses[0], incoming)
    self_done = last_swap(grid, selfs)
    page_shape = language_in.shape
    got = incoming.astype(f32)
    grad_mine = grad_mine + got[: pages * slots]
    grad_theirs = grad_theirs + got[pages * slots :]
    grad_language = jnp.where(first, grad_mine, grad_theirs).astype(bf16).reshape(page_shape)
    grad_vision = jnp.where(first, grad_theirs, grad_mine).astype(bf16).reshape(page_shape)

    self_qkv_grad, self_proj_grad = attention_grads(self_done)
    crosses, self_qkv_grad, self_proj_grad, grad_language, grad_vision = tie(
        crosses, self_qkv_grad, self_proj_grad, grad_language, grad_vision
    )
    cross_done = last_swap(grid, crosses)
    cross_qkv_grad, cross_proj_grad = attention_grads(cross_done)
    vec_sum = (cross_done[0].astype(f32) + cross_done[1].astype(f32))[:, 2 * rows :]
    vec_both = by_side(vec_sum)
    gate_vec = vec_sum[0, 4, 128 : 128 + rows] + vec_sum[1, 4, 128 : 128 + rows]
    return (
        united.reshape(page_shape),
        grad_language,
        grad_vision,
        cross_qkv_grad,
        cross_proj_grad,
        vec_both[:, 0:3, :rows],
        vec_both[:, 0:3, 256 : 256 + rows],
        vec_both[:, 0:3, 384 : 384 + rows],
        self_qkv_grad,
        self_proj_grad,
        vec_both[:, 0:3, 128 : 128 + rows],
        in_all,
        vec_both[:, 3, : 4 * rows],
        out_all,
        vec_both[:, 4, :rows],
        gate_both,
        gate_vec,
    )


def solution(mesh):
    whole = P(("dp", "rep"), None, None)
    weights = (
        P(None, None, "dp", None),
        P(None, "dp", None),
        P(None, None, "dp"),
        P(None, None, "dp"),
        P(None, None, "dp"),
        P(None, None, "dp", None),
        P(None, "dp", None),
        P(None, None, "dp"),
        P(None, "dp", None),
        P(None, "dp"),
        P(None, "dp", None),
        P(None, "dp"),
        P(None, "dp", None),
        P("dp"),
    )
    return jax.shard_map(
        functools.partial(on_device, Grid(mesh)),
        mesh=mesh,
        in_specs=(whole, whole, P(("dp", "rep")), P(("dp", "rep"))) + weights + (whole,),
        out_specs=(whole, whole, whole) + weights,
        check_vma=False,
    )
```

```python
import functools

import jax
import jax.numpy as jnp
from jax import lax
from jax.experimental import pallas as pl
from jax.experimental.pallas import tpu as pltpu
from jax.sharding import PartitionSpec as P

HEADS = 12
HEAD = 64
norm_epsilon = 1e-05
bf16 = jnp.bfloat16
f32 = jnp.float32
AXES = ("dp", "rep")
VMEM_LIMIT = 27 << 20
GLUE_LIMIT = 20 << 20
HBM = pl.BlockSpec(memory_space=pltpu.HBM)
VMEM = pl.BlockSpec(memory_space=pltpu.VMEM)
SMEM = pl.BlockSpec(memory_space=pltpu.SMEM)


class Grid:
    def __init__(self, mesh):
        self.n = mesh.shape["dp"]
        self.r = mesh.shape["rep"]
        self.high = self.n >> 1
        self.partner = self.n >> 2
        self.groups = [0, self.partner, self.high, self.high | self.partner]
        low = []
        bit = 1
        while bit < self.partner:
            low.append(bit)
            bit *= 2
        self.orders = [low, low[::-1]]
        self.high_bit = len(low) + 1

    def across(self, values, mask):
        pairs = [
            (d * self.r + c, (d ^ mask) * self.r + c) for d in range(self.n) for c in range(self.r)
        ]
        return lax.ppermute(values, AXES, pairs)

    def swap_cores(self, values):
        pairs = [
            (d * self.r + c, d * self.r + (c ^ 1)) for d in range(self.n) for c in range(self.r)
        ]
        return lax.ppermute(values, AXES, pairs)

    def hop(self, values, step):
        pairs = []
        for d in range(self.n):
            for c in range(self.r):
                mask = self.orders[c % 2][step]
                pairs.append((d * self.r + c, (d ^ mask) * self.r + c))
        return lax.ppermute(values, AXES, pairs)

    def place(self, info):
        core, me = info[1], info[2]
        first = jnp.right_shift(me, core) & 1
        second = jnp.right_shift(me, 1 - core) & 1
        return jnp.right_shift(me, 2), first, second, 1 + core, 2 - core

    def masks(self, core):
        found = [0]
        for low, high in zip(*self.orders, strict=True):
            bit = low + core * (high - low)
            found = found + [m ^ bit for m in found]
        return found


def call(kernel, outs, ins, specs, out_specs, scratch=(), flops=0, moved=0, room=VMEM_LIMIT):
    results = pl.pallas_call(
        kernel,
        out_shape=[jax.ShapeDtypeStruct(shape, dtype) for shape, dtype in outs],
        in_specs=specs,
        out_specs=out_specs,
        scratch_shapes=list(scratch),
        compiler_params=pltpu.CompilerParams(vmem_limit_bytes=room),
        cost_estimate=pl.CostEstimate(flops=flops, bytes_accessed=moved, transcendentals=0),
    )(*ins)
    return list(results)


def pair_kernel(bit_of, info_ref, *refs):
    mine, other = refs[:2]
    bit = jnp.right_shift(info_ref[2], bit_of) & 1
    start = 0
    for out in refs[2:]:
        end = start + out.shape[-2]
        out[bit] = mine[..., start:end, :]
        out[1 - bit] = other[..., start:end, :]
        start = end


def pair(info, bit_of, mine, other, parts=None):
    shape = mine.shape
    parts = [shape[-2]] if parts is None else parts
    if shape[-2] % 16:
        bit = jnp.right_shift(info[2], bit_of) & 1
        both = jnp.where(bit == 0, jnp.stack([mine, other]), jnp.stack([other, mine]))
        starts = [sum(parts[:i]) for i in range(len(parts))]
        return [both[..., s : s + p, :] for s, p in zip(starts, parts, strict=True)]
    return call(
        functools.partial(pair_kernel, bit_of),
        [((2,) + shape[:-2] + (part, shape[-1]), bf16) for part in parts],
        [info, mine, other],
        [SMEM, VMEM, VMEM],
        [VMEM] * len(parts),
        room=GLUE_LIMIT,
    )


def group_kernel(high_bit, info_ref, *refs):
    group = jnp.right_shift(info_ref[2], high_bit - 1)
    for k, source in enumerate(refs[:4]):
        refs[4][jnp.bitwise_xor(group, k)] = source[...]


def all_meet(grid, info, mine, theirs):
    return [
        mine,
        grid.across(theirs, grid.groups[1]),
        grid.across(theirs, grid.groups[2]),
        grid.across(mine, grid.groups[3]),
    ]


def grouped(grid, info, sources):
    shape = sources[0].shape
    if shape[0] % 16:
        group = jnp.right_shift(info[2], grid.high_bit - 1)
        return jnp.take(jnp.stack(sources), jnp.arange(4) ^ group, axis=0)
    return call(
        functools.partial(group_kernel, grid.high_bit),
        [((4,) + shape, bf16)],
        [info] + sources,
        [SMEM] + [VMEM] * 4,
        [VMEM],
        room=GLUE_LIMIT,
    )[0]


def join_kernel(grid, info_ref, mine, other, out):
    bit = grid.place(info_ref)[1]
    for g in range(4):
        out[g, bit] = mine[g]
        out[g, 1 - bit] = other[g]


def join_pair(grid, info, pieces):
    shape = pieces[0].shape
    return call(
        functools.partial(join_kernel, grid),
        [((4, 2) + shape[1:], bf16)],
        [info] + pieces,
        [SMEM] + [VMEM] * 2,
        [VMEM],
        room=GLUE_LIMIT,
    )[0]


def tie(*values):
    flat, tree = jax.tree.flatten(values)
    return jax.tree.unflatten(tree, lax.optimization_barrier(flat))


def meet(grid, info, held):
    rows, width = held.shape[1:]
    received = grid.across(held, grid.groups[3])

    def place(received):
        return pair(info, grid.high_bit, held, received)[0].reshape(4, rows, width)

    return received, place


def join_all_kernel(grid, info_ref, mine, first_away, second_away, both_away, out):
    unused, first, second, unused, unused = grid.place(info_ref)
    for g in range(4):
        out[g, second, first] = mine[g]
        out[g, second, 1 - first] = first_away[g]
        out[g, 1 - second, first] = second_away[g]
        out[g, 1 - second, 1 - first] = both_away[g]


def second_hops(grid, held):
    if len(grid.orders[0]) == 2:
        return [held, grid.hop(held, 0), grid.hop(held, 1)]
    for step in range(len(grid.orders[0])):
        held = jnp.concatenate([held, grid.hop(held, step)], 0)
    return [held]


def third_hops(grid, pieces):
    return pieces + [grid.hop(pieces[1], 1)] if len(pieces) == 3 else pieces


def ahead(grid, info, pieces):
    if len(pieces) == 1:
        return []
    held = join_pair(grid, info, pieces[:2])
    return [held, pieces[2], grid.swap_cores(held), grid.swap_cores(pieces[2])]


def extra_rows(grid, info, pieces, start, keep):
    held = pieces[0][:, start : start + keep]
    return jnp.take(held, jnp.argsort(slots_of(grid, info)), axis=0)


def slots_of(grid, info):
    masks = jnp.stack(grid.masks(info[1])).astype(jnp.int32)[:, None]
    groups = jnp.arange(4, dtype=jnp.int32)[None, :] * grid.partner
    return ((masks ^ (info[2] & (grid.partner - 1))) | groups).reshape(-1)


def whole(grid, info, pieces, rows, count, early=()):
    if early:
        mine, away, mine_swapped, away_swapped = early
        return [mine, away, pieces[3], mine_swapped, away_swapped, grid.swap_cores(pieces[3])]
    if len(pieces) == 4:
        shape = pieces[0].shape
        held = call(
            functools.partial(join_all_kernel, grid),
            [((4, 2, 2) + shape[1:], bf16)],
            [info] + pieces,
            [SMEM] + [VMEM] * 4,
            [VMEM],
            room=GLUE_LIMIT,
        )[0]
        return [held, grid.swap_cores(held)]
    held = pieces[0][:, : count * rows]
    held = jnp.take(held, jnp.argsort(slots_of(grid, info)), axis=0).reshape(grid.n, count, rows, -1).transpose(1, 0, 2, 3)
    held = held.reshape(count, grid.n * rows, -1)
    return [held, grid.swap_cores(held)]


def split_kernel(grid, extra, info_ref, keep, received, *refs):
    outs = refs[-2:]
    count, rows = keep.shape[0], keep.shape[2]
    unused, unused, second, first_step, second_step = grid.place(info_ref)
    for g in range(4):
        for a in range(2):
            for b, out in ((second, outs[0]), (1 - second, outs[1])):
                source = 4 * g + a * first_step + b * second_step
                for j in range(count):
                    total = keep[j, source].astype(f32) + received[j, source].astype(f32)
                    out[g, a, j * rows : (j + 1) * rows] = total.astype(bf16)
                if extra:
                    out[g, a, count * rows :] = refs[0][source]


def added(a, b):
    return (a.astype(f32) + b.astype(f32)).astype(bf16)


def first_returns(grid, info, keep, received, more=None):
    blocks, n, rows, width = keep.shape
    depth = blocks * rows + (0 if more is None else more.shape[1])
    extra = [] if more is None else [more]
    if len(grid.orders[0]) != 2:
        total = added(keep, received).transpose(1, 0, 2, 3).reshape(n, blocks * rows, width)
        total = jnp.concatenate([total] + extra, 1)
        held = jnp.take(total, slots_of(grid, info), axis=0)
        for step in reversed(range(len(grid.orders[0]))):
            half = held.shape[0] // 2
            held = added(held[:half], grid.hop(held[half:], step))
        return [held]
    held, sent = call(
        functools.partial(split_kernel, grid, len(extra)),
        [((4, 2, depth, width), bf16)] * 2,
        [info, keep, received] + extra,
        [SMEM, VMEM, VMEM] + [VMEM] * len(extra),
        [VMEM] * 2,
        room=GLUE_LIMIT,
    )
    return [held, grid.hop(sent, 1)]


def merge_kernel(grid, info_ref, *refs):
    near, far = refs[-2:]
    bit = grid.place(info_ref)[1]
    start = 0
    for held, received in zip(refs[:-2:2], refs[1:-2:2], strict=True):
        at = slice(start, start + held.shape[2])
        for g in range(4):
            for which, out in ((bit, near), (1 - bit, far)):
                out[g, at] = added(held[g, which], received[g, which])
        start += held.shape[2]


def second_returns(grid, info, *parts):
    if len(parts[0]) == 1:
        return [jnp.concatenate([part[0] for part in parts], 1)]
    depth = sum(part[0].shape[2] for part in parts)
    near, far = call(
        functools.partial(merge_kernel, grid),
        [((4, depth, parts[0][0].shape[3]), bf16)] * 2,
        [info] + [array for part in parts for array in part],
        [SMEM] + [VMEM] * (2 * len(parts)),
        [VMEM] * 2,
        room=GLUE_LIMIT,
    )
    return [near, grid.hop(far, 0)]


def collect_kernel(grid, info_ref, held, received, *outs):
    group = grid.place(info_ref)[0]
    for k, out in enumerate(outs):
        at = jnp.bitwise_xor(group, k)
        out[...] = added(held[at], received[at])


def third_returns(grid, info, pieces):
    if len(pieces) == 1:
        group = jnp.right_shift(info[2], grid.high_bit - 1)
        totals = [
            lax.dynamic_index_in_dim(pieces[0], group ^ g, 0, keepdims=False) for g in range(4)
        ]
    else:
        totals = call(
            functools.partial(collect_kernel, grid),
            [(pieces[0].shape[1:], bf16)] * 4,
            [info] + pieces,
            [SMEM] + [VMEM] * 2,
            [VMEM] * 4,
            room=GLUE_LIMIT,
        )
    return [totals[0]] + [grid.across(totals[g], grid.groups[g]) for g in (3, 1, 2)]


def last_kernel(near_a, near_b, far_a, far_b, out):
    out[0] = (near_a[...].astype(f32) + near_b[...].astype(f32)).astype(bf16)
    out[1] = (far_a[...].astype(f32) + far_b[...].astype(f32)).astype(bf16)


def last_swap(grid, terms):
    mine = call(
        last_kernel,
        [((2,) + terms[0].shape, bf16)],
        terms,
        [VMEM] * 4,
        [VMEM],
        room=GLUE_LIMIT,
    )[0]
    return mine, grid.swap_cores(mine)


def finish_kernel(layout, rows, info_ref, mine_ref, far_ref, *outs):
    side, core = info_ref[0], info_ref[1]

    def write(which, ref):
        for j, (out, at) in enumerate(layout[which]):
            for k in range(2):
                value = ref[k, j * rows : (j + 1) * rows].astype(f32)
                outs[out][(jnp.bitwise_xor(side, k),) + at] = value

    for which in range(2):
        pl.when(core == which)(functools.partial(write, which, mine_ref))
        pl.when(core != which)(functools.partial(write, which, far_ref))


def finish(info, done, layout, rows, shapes):
    return call(
        functools.partial(finish_kernel, layout, rows),
        [(shape, f32) for shape in shapes],
        [info] + list(done),
        [SMEM, VMEM, VMEM],
        [VMEM] * len(shapes),
        room=GLUE_LIMIT,
    )


def finish_gate_kernel(info_ref, mine_ref, far_ref, out):
    side, core = info_ref[0], info_ref[1]
    rows = out.shape[1]

    def write(own_ref, other_ref):
        for k in range(2):
            own = own_ref[k, :rows].astype(f32)
            out[jnp.bitwise_xor(side, k)] = own + other_ref[1 - k, :rows].astype(f32)

    pl.when(core == 0)(functools.partial(write, mine_ref, far_ref))
    pl.when(core != 0)(functools.partial(write, far_ref, mine_ref))


def nn(a, b):
    return lax.dot_general(a, b, (((1,), (0,)), ((), ())), preferred_element_type=f32)


def nt(a, b):
    return lax.dot_general(a, b, (((1,), (1,)), ((), ())), preferred_element_type=f32)


def tn(a, b):
    return lax.dot_general(a, b, (((0,), (0,)), ((), ())), preferred_element_type=f32)


def block_shapes(grid, count, rows, width, mixed=False):
    if rows % 16 or len(grid.orders[0]) != 2:
        return (4 * grid.n * rows, width) if mixed else (count, grid.n * rows, width)
    inner = (4, rows, width) if mixed else (rows, width)
    return ((4, 2, 2) if mixed else (count, 4, 2, 2)) + inner


def load_blocks(grid, info_ref, sources, blocks, sem, start=0, only=None, mixed=False):
    core = info_ref[1]
    middle = len(sources) // 2

    def load(which, refs):
        count = 1 if only is not None else 2 if mixed else blocks.shape[0] // 2
        first = 0 if only is not None else which * count
        if len(refs[0].shape) == 3:
            for j in range(count):
                pltpu.make_async_copy(refs[0].at[start + j], blocks.at[first + j], sem).start()
            return
        rows = blocks.shape[-2]
        near = jnp.right_shift(info_ref[2], which) & 1
        bit = jnp.right_shift(info_ref[2], 1 - which) & 1

        def copy(source, target):
            pltpu.make_async_copy(source, target, sem).start()

        def place(j, *at):
            return blocks.at[at + (first + j,)] if mixed else blocks.at[(first + j,) + at]

        every = slice(None)
        for j in range(count):
            cut = pl.ds((start + j) * rows, rows)

            def low_first(j=j, cut=cut):
                if len(refs) == 1:
                    copy(refs[0].at[:, :, :, cut], place(j, every, every, every))
                    return
                copy(refs[0].at[:, :, cut], place(j, every, bit, every))
                copy(refs[1].at[:, cut], place(j, every, 1 - bit, near))
                copy(refs[2].at[:, cut], place(j, every, 1 - bit, 1 - near))

            def high_first(j=j, cut=cut):
                if len(refs) == 1:
                    for b in range(2):
                        copy(refs[0].at[:, b, :, cut], place(j, every, every, b))
                    return
                copy(refs[0].at[:, :, cut], place(j, every, every, bit))
                copy(refs[1].at[:, cut], place(j, every, near, 1 - bit))
                copy(refs[2].at[:, cut], place(j, every, 1 - near, 1 - bit))

            pl.when(which == 0)(low_first)
            pl.when(which != 0)(high_first)

    if len(sources) == 1:
        pltpu.make_async_copy(sources[0], blocks, sem).start()
    elif only is None:
        load(core, sources[:middle])
        load(1 - core, sources[middle:])
    else:
        pl.when(core == only)(lambda: load(only, sources[:middle]))
        pl.when(core != only)(lambda: load(only, sources[middle:]))
    return pltpu.make_async_copy(blocks, blocks, sem).wait


def matrix(values):
    return values.reshape(-1, values.shape[-1])


def load_inputs(info_ref, language, vision, both_far, src_ref, oth_ref, sem):
    half = language.shape[0]

    def copies(mine, mine_at, other, other_at):
        return [
            pltpu.make_async_copy(mine, src_ref.at[pl.ds(0, half)], sem.at[0]),
            pltpu.make_async_copy(
                both_far.at[pl.ds(mine_at, half)], src_ref.at[pl.ds(half, half)], sem.at[1]
            ),
            pltpu.make_async_copy(other, oth_ref.at[pl.ds(0, half)], sem.at[2]),
            pltpu.make_async_copy(
                both_far.at[pl.ds(other_at, half)], oth_ref.at[pl.ds(half, half)], sem.at[3]
            ),
        ]

    @pl.when(info_ref[0] == 0)
    def _():
        for copy in copies(language, 0, vision, half):
            copy.start()

    @pl.when(info_ref[0] != 0)
    def _():
        for copy in copies(vision, half, language, 0):
            copy.start()

    def wait():
        for copy in copies(language, 0, vision, half):
            copy.wait()

    return wait


def store_blocks(core, blocks, keep, send, sem):
    count = keep.shape[0]
    copies = []
    for j in range(count):
        copies.append(pltpu.make_async_copy(blocks.at[core * count + j], keep.at[j], sem.at[j]))
        copies.append(
            pltpu.make_async_copy(
                blocks.at[(1 - core) * count + j], send.at[j], sem.at[count + j]
            )
        )
    for copy in copies:
        copy.start()

    def wait():
        for copy in copies:
            copy.wait()

    return wait


def normalised(values):
    mean_row = jnp.mean(values, axis=-1, keepdims=True)
    centred = values - mean_row
    variance = jnp.mean(centred * centred, axis=-1, keepdims=True)
    scale = lax.rsqrt(variance + norm_epsilon)
    return centred * scale, scale


def norm_back(values, grads, gain):
    unit, scale = normalised(values)
    scaled = grads * gain
    first = jnp.mean(scaled, axis=-1, keepdims=True)
    second = jnp.mean(scaled * unit, axis=-1, keepdims=True)
    return (scaled - first - unit * second) * scale, grads * unit


def lane_masks():
    lanes = lax.broadcasted_iota(jnp.int32, (128, 2 * HEAD), 1)
    left = (lanes < HEAD).astype(f32).astype(bf16)
    right = (lanes >= HEAD).astype(f32).astype(bf16)
    return lanes < HEAD, left, right


def two_heads(values, left, right):
    return jnp.concatenate([values * left, values * right], 0)


def softened(queries, keys_both, barred):
    scores = []
    for pair, keys in zip(queries, keys_both, strict=True):
        both = nt(pair, keys) * HEAD ** (-0.5)
        slots = both.shape[0]
        scores += [both[:, :slots], both[:, slots:]]
    scores = [jnp.where(barred, -1000000000.0, part) for part in scores]
    peaks = [jnp.max(part, axis=-1, keepdims=True) for part in scores]
    weights = [jnp.exp(part - peak) for part, peak in zip(scores, peaks, strict=True)]
    totals = [1.0 / jnp.sum(part, axis=-1, keepdims=True) for part in weights]
    return [part * total for part, total in zip(weights, totals, strict=True)]


def joined(parts, pair):
    return jnp.concatenate([part.astype(bf16) for part in parts[2 * pair : 2 * pair + 2]], 1)


def barred_slots(slots, count):
    return lax.broadcasted_iota(jnp.int32, (slots, slots), 1) >= count


def pages_of(rows, slots, body):
    def step(page, carry):
        body(page, pl.ds(pl.multiple_of(page * slots, slots), slots))
        return carry

    lax.fori_loop(0, rows // slots, step, 0, unroll=2)


def column_sum(values):
    return jnp.sum(values.astype(f32), axis=0, keepdims=True)


def attend_kernel(grid, cross, slots, held, at_table, info_ref, counts_ref, vec_ref, *refs):
    if cross:
        inputs, refs = refs[:3], refs[3:]
    else:
        residual_ref, low_ref = refs[:2]
        refs = refs[2:]
    sources, refs = refs[:held], refs[held:]

    def row(i):
        return vec_ref[at_table[i] : at_table[i] + 1, :]

    q_ref, k_ref, v_ref, o_ref, sum_ref, norm_ref, norm_low_ref = refs[:7]
    blocks, sem = refs[7:9]
    rows = q_ref.shape[0]
    half = rows // 2
    wait_blocks = load_blocks(grid, info_ref, sources, blocks, sem)
    if cross:
        src_ref, oth_ref, in_sem = refs[9:12]
        load_inputs(info_ref, *inputs, src_ref, oth_ref, in_sem)()
    else:
        src_ref = oth_ref = low_ref
    wait_blocks()
    width = q_ref.shape[1]
    q_ref[...] = (nn(src_ref[...], matrix(blocks[0])) + row(0)).astype(bf16)
    k_ref[...] = nn(oth_ref[...], matrix(blocks[1])).astype(bf16)
    v_ref[...] = (nn(oth_ref[...], matrix(blocks[2])) + row(1)).astype(bf16)
    unused, left, right = lane_masks()
    cuts = [slice(at, at + 128) for at in range(0, width, 128)]

    def one_page(page, at):
        soft = softened(
            [q_ref[at, cut] for cut in cuts],
            [two_heads(k_ref[at, cut], left, right) for cut in cuts],
            barred_slots(slots, counts_ref[page]),
        )
        for i, cut in enumerate(cuts):
            mixed = nn(joined(soft, i), two_heads(v_ref[at, cut], left, right))
            o_ref[at, cut] = mixed.astype(bf16)

    pages_of(rows, slots, one_page)
    residual = src_ref[...].astype(f32) if cross else residual_ref[...]
    total = residual + nn(o_ref[...], matrix(blocks[3])) + row(2)
    sum_ref[...] = total
    result = normalised(total)[0] * row(3) + row(4)
    norm_ref[...] = result
    norm_low_ref[...] = result.astype(bf16)


def attend(grid, cross, slots, info, counts, vectors, at_table, inputs, weights):
    width = weights[0].shape[-1]
    rows = counts.shape[0] * slots
    blocks = block_shapes(grid, 4, grid.rows, width)
    scratch = [pltpu.VMEM(blocks, bf16), pltpu.SemaphoreType.DMA]
    if cross:
        scratch += [pltpu.VMEM((rows, width), bf16)] * 2 + [pltpu.SemaphoreType.DMA((4,))]
    return call(
        functools.partial(attend_kernel, grid, cross, slots, len(weights), at_table),
        [((rows, width), bf16)] * 4 + [((rows, width), f32)] * 2 + [((rows, width), bf16)],
        [info, counts, vectors] + list(inputs) + list(weights),
        [SMEM, SMEM, VMEM] + ([HBM] * 3 if cross else [VMEM] * 2) + [HBM] * len(weights),
        [VMEM] * 7,
        scratch,
        flops=8 * rows * width * width + 8 * rows * slots * width,
        moved=4 * width * width * 2 + rows * width * 20,
    )


def hidden_kernel(grid, held, info_ref, shift_ref, low_ref, *refs):
    sources = refs[:held]
    active_ref, slope_ref, blocks, sem = refs[held:]
    load_blocks(grid, info_ref, sources, blocks, sem)()
    width = low_ref.shape[1]
    for b in range(4):
        at = slice(b * width, (b + 1) * width)
        hidden = nn(low_ref[...], matrix(blocks[b])) + shift_ref[0:1, at]
        square = hidden * hidden
        bent = jnp.tanh(0.7978845608028654 * (hidden + 0.044715 * square * hidden))
        active_ref[:, at] = (0.5 * hidden * (1.0 + bent)).astype(bf16)
        slope = 0.5 * (1.0 + bent) + 0.5 * hidden * (1.0 - bent * bent) * (
            0.7978845608028654 * (1.0 + 3.0 * 0.044715 * square)
        )
        slope_ref[:, at] = slope.astype(bf16)


def hidden_layer(grid, info, shift, low, weights):
    rows, width = low.shape
    return call(
        functools.partial(hidden_kernel, grid, len(weights)),
        [((rows, 4 * width), bf16)] * 2,
        [info, shift, low] + list(weights),
        [SMEM, VMEM, VMEM] + [HBM] * len(weights),
        [VMEM, VMEM],
        [pltpu.VMEM(block_shapes(grid, 4, grid.rows, width), bf16), pltpu.SemaphoreType.DMA],
        flops=8 * rows * width * width,
        moved=8 * width * width + rows * width * 18,
    )


def store_wide(core, wide, keep, send, sem):
    copies = []
    for j in range(2):
        for which, target in ((core, keep), (1 - core, send)):
            copies.append(pltpu.make_async_copy(wide.at[:, 2 * which + j], target.at[j], sem))
    for copy in copies:
        copy.start()
    pltpu.make_async_copy(wide, wide, sem).wait()


def branch_kernel(grid, held, info_ref, vec_ref, active_ref, residual_ref, *refs):
    sources = refs[:held]
    sum_ref, norm_ref, far_ref, wide, sem = refs[held:]
    load_blocks(grid, info_ref, sources, wide, sem, mixed=True)()
    half = residual_ref.shape[0] // 2
    total = residual_ref[...] + nn(active_ref[...], matrix(wide[...])) + vec_ref[12:13, :]
    sum_ref[...] = total
    result = normalised(total)[0] * vec_ref[8:9, :] + vec_ref[11:12, :]
    norm_ref[...] = result[:half]
    far_ref[...] = result[half:].astype(bf16)


def branch_layer(grid, info, vectors, active, residual, weights):
    rows, width = residual.shape
    return call(
        functools.partial(branch_kernel, grid, len(weights)),
        [((rows, width), f32), ((rows // 2, width), f32), ((rows // 2, width), bf16)],
        [info, vectors, active, residual] + list(weights),
        [SMEM, VMEM, VMEM, VMEM] + [HBM] * len(weights),
        [VMEM] * 3,
        [pltpu.VMEM(block_shapes(grid, 4, grid.rows, width, True), bf16), pltpu.SemaphoreType.DMA],
        flops=8 * rows * width * width,
        moved=8 * width * width + rows * width * 20,
    )


def gate_kernel(grid, held, info_ref, shift_ref, third_ref, far_ref, cotangent_ref, *refs):
    sources = refs[:held]
    united_ref, grad_own_ref, grad_far_ref, grad_shift_ref, keep_ref, send_ref = refs[held : held + 6]
    blocks, sem, grads, mix_ref, low_ref, out_sem = refs[held + 6 :]
    load_blocks(grid, info_ref, sources, blocks, sem, 2)()
    first = info_ref[0] == 0
    low_ref[...] = third_ref[...].astype(bf16)
    logits = nn(low_ref[...], matrix(blocks[0])) + nn(far_ref[...], matrix(blocks[1])) + shift_ref[13:14, :]
    mixing = 1.0 / (1.0 + jnp.exp(-logits))
    share = jnp.where(first, mixing, 1.0 - mixing)
    mine, other = third_ref[...], far_ref[...].astype(f32)
    united_ref[...] = (share * mine + (1.0 - share) * other).astype(bf16)
    cotangent = cotangent_ref[...].astype(f32)
    gap = jnp.where(first, mine - other, other - mine)
    grad = (cotangent * gap * mixing * (1.0 - mixing)).astype(bf16)
    mix_ref[...] = grad
    grad_shift_ref[0:1, :] = column_sum(grad)
    direct = cotangent * share
    grad_own_ref[...] = direct + nt(mix_ref[...], matrix(blocks[0]))
    grad_far_ref[...] = (cotangent - direct + nt(mix_ref[...], matrix(blocks[1]))).astype(bf16)
    grads[0] = tn(low_ref[...], mix_ref[...]).astype(bf16)
    grads[1] = tn(far_ref[...], mix_ref[...]).astype(bf16)
    store_blocks(info_ref[1], grads, keep_ref, send_ref, out_sem)()


def gate_layer(grid, info, shift, third, far, cotangent, weights):
    rows, width = third.shape
    blocks = (2, width, width)
    return call(
        functools.partial(gate_kernel, grid, len(weights)),
        [
            ((rows, width), bf16),
            ((rows, width), f32),
            ((rows, width), bf16),
            ((8, width), f32),
            ((1,) + blocks[1:], bf16),
            ((1,) + blocks[1:], bf16),
        ],
        [info, shift, third, far, cotangent] + list(weights),
        [SMEM] + [VMEM] * 4 + [HBM] * len(weights),
        [VMEM] * 4 + [HBM] * 2,
        [
            pltpu.VMEM(block_shapes(grid, 2, grid.rows, width), bf16),
            pltpu.SemaphoreType.DMA,
            pltpu.VMEM(blocks, bf16),
            pltpu.VMEM((rows, width), bf16),
            pltpu.VMEM((rows, width), bf16),
            pltpu.SemaphoreType.DMA((2,)),
        ],
        flops=12 * rows * width * width,
        moved=8 * width * width + rows * width * 14,
    )


def branch_back_kernel(
    wide_out,
    info_ref,
    gain_ref,
    sum_ref,
    grad_own_ref,
    grad_far_ref,
    active_ref,
    grad_sum_ref,
    grad_low_ref,
    vec_ref,
    *refs,
):
    rows, width = sum_ref.shape
    half = rows // 2
    vec_ref[...] = jnp.zeros_like(vec_ref)
    for offset, grads_ref in ((0, grad_own_ref), (half, grad_far_ref)):
        at = slice(offset, offset + half)
        grads = grads_ref[...].astype(f32)
        back, gain_rows = norm_back(sum_ref[at, :], grads, gain_ref[8:9, :])
        low = back.astype(bf16)
        grad_sum_ref[at, :] = back
        grad_low_ref[at, :] = low
        vec_ref[0:1, :] += column_sum(gain_rows)
        vec_ref[1:2, :] += column_sum(grads)
        vec_ref[2:3, :] += column_sum(low)
    wide, sem = refs[-2:]
    for b in range(4):
        at = slice(b * width, (b + 1) * width)
        part = tn(active_ref[:, at], grad_low_ref[...]).astype(bf16)
        if wide_out:
            devices = wide.shape[0] // 4
            wide[b * devices : (b + 1) * devices] = part.reshape((devices,) + wide.shape[1:])
        else:
            wide[at, :] = part
    if wide_out:
        store_wide(info_ref[1], wide, refs[0], refs[1], sem)
    else:
        copy = pltpu.make_async_copy(wide, refs[0], sem)
        copy.start()
        copy.wait()


def branch_back(grid, info, gain, sums, grad_own, grad_far, active, piece):
    rows, width = sums.shape
    wide_out = piece % 16 == 0
    target = (2, grid.n, piece, width) if wide_out else (4 * width, width)
    outs = [(target, bf16)] * (2 if wide_out else 1)
    return call(
        functools.partial(branch_back_kernel, wide_out),
        [((rows, width), f32), ((rows, width), bf16), ((8, width), f32)] + outs,
        [info, gain, sums, grad_own, grad_far, active],
        [SMEM] + [VMEM] * 5,
        [VMEM] * 3 + [HBM] * len(outs),
        [
            pltpu.VMEM((grid.n, 4, piece, width) if wide_out else (4 * width, width), bf16),
            pltpu.SemaphoreType.DMA,
        ],
        flops=8 * rows * width * width,
        moved=8 * width * width + rows * width * 24,
    )


def hidden_back_kernel(grid, held, info_ref, grad_low_ref, slope_ref, low_ref, *refs):
    core = info_ref[1]
    grad_hidden_ref, vec_ref, keep_ref, send_ref, wide, sem, grads, out_sem = refs[held:]
    load_blocks(grid, info_ref, refs[:held], wide, sem, mixed=True)()
    whole_wide = matrix(wide[...])
    width = low_ref.shape[1]
    for b in range(4):
        at = slice(b * width, (b + 1) * width)
        low = (nt(grad_low_ref[...], whole_wide[at, :]) * slope_ref[:, at].astype(f32)).astype(bf16)
        grad_hidden_ref[:, at] = low
        vec_ref[0:1, at] = column_sum(low)
        grads[b] = tn(low_ref[...], low).astype(bf16)
    store_blocks(core, grads, keep_ref, send_ref, out_sem)()


def hidden_back(grid, info, grad_low, slope, low, weights):
    rows, width = low.shape
    blocks = (4, width, width)
    return call(
        functools.partial(hidden_back_kernel, grid, len(weights)),
        [((rows, 4 * width), bf16), ((8, 4 * width), f32)] + [((2,) + blocks[1:], bf16)] * 2,
        [info, grad_low, slope, low] + list(weights),
        [SMEM] + [VMEM] * 3 + [HBM] * len(weights),
        [VMEM] * 2 + [HBM] * 2,
        [
            pltpu.VMEM(block_shapes(grid, 4, grid.rows, width, True), bf16),
            pltpu.SemaphoreType.DMA,
            pltpu.VMEM(blocks, bf16),
            pltpu.SemaphoreType.DMA((4,)),
        ],
        flops=16 * rows * width * width,
        moved=16 * width * width + rows * width * 30,
    )


def second_back_kernel(
    grid, held, info_ref, gain_ref, sum_ref, grad_ref, grad_hidden_ref, *refs
):
    grad_sum_ref, vec_ref, blocks, sem = refs[held:]
    load_blocks(grid, info_ref, refs[:held], blocks, sem)()
    width = sum_ref.shape[1]
    total = grad_ref[...]
    for b in range(4):
        total += nt(grad_hidden_ref[:, b * width : (b + 1) * width], matrix(blocks[b]))
    grad_sum_ref[...] = norm_back_into(vec_ref, sum_ref[...], total, gain_ref[7:8, :])


def norm_back_into(vec_ref, sums, grads, gain):
    back, gain_rows = norm_back(sums, grads, gain)
    vec_ref[0:1, :] = column_sum(gain_rows)
    vec_ref[1:2, :] = column_sum(grads)
    return back


def second_back(grid, info, gain, sums, grads, grad_hidden, weights):
    rows, width = sums.shape
    return call(
        functools.partial(second_back_kernel, grid, len(weights)),
        [((rows, width), f32), ((8, width), f32)],
        [info, gain, sums, grads, grad_hidden] + list(weights),
        [SMEM] + [VMEM] * 4 + [HBM] * len(weights),
        [VMEM] * 2,
        [pltpu.VMEM(block_shapes(grid, 4, grid.rows, width), bf16), pltpu.SemaphoreType.DMA],
        flops=8 * rows * width * width,
        moved=8 * width * width + rows * width * 20,
    )


def scores_back_kernel(
    grid, cross, slots, held, info_ref, counts_ref, grad_ref, q_ref, k_ref, v_ref, o_ref, *refs
):
    count = 3 if cross else 1
    inputs, sources, refs = refs[:count], refs[count : count + held], refs[count + held :]
    dq_ref, dk_ref, dv_ref, vec_ref, keep_ref, send_ref = refs[:6]
    weight, sem, low_grad, grad_o, grads, out_sem = refs[6:12]
    wait_block = load_blocks(grid, info_ref, sources, weight, sem, 1, 1)
    if cross:
        src_ref, oth_ref, in_sem = refs[12:]
        wait_inputs = load_inputs(info_ref, *inputs, src_ref, oth_ref, in_sem)
    else:
        src_ref = oth_ref = inputs[0]
    rows, width = q_ref.shape
    low = grad_ref[...].astype(bf16)
    low_grad[...] = low
    vec_ref[2:3, :] = column_sum(low)
    grads[3] = tn(o_ref[...], low_grad[...]).astype(bf16)
    wait_block()
    grad_o[...] = nt(low_grad[...], matrix(weight[0])).astype(bf16)
    left_lanes, left, right = lane_masks()
    cuts = [slice(at, at + 128) for at in range(0, width, 128)]

    def one_page(page, at):
        keys = [two_heads(k_ref[at, cut], left, right) for cut in cuts]
        soft = softened(
            [q_ref[at, cut] for cut in cuts], keys, barred_slots(slots, counts_ref[page])
        )
        grad_soft = []
        for cut in cuts:
            both = nt(grad_o[at, cut], two_heads(v_ref[at, cut], left, right))
            grad_soft += [both[:, :slots], both[:, slots:]]
        weighted = [a * b for a, b in zip(soft, grad_soft, strict=True)]
        sums = [jnp.sum(part, axis=-1, keepdims=True) for part in weighted]
        grad_scores = [w - p * t for w, p, t in zip(weighted, soft, sums, strict=True)]
        for i, cut in enumerate(cuts):
            dv = tn(joined(soft, i), grad_o[at, cut])
            dv_ref[at, cut] = jnp.where(left_lanes, dv[:slots], dv[slots:]).astype(bf16)
        for i, cut in enumerate(cuts):
            pair = joined(grad_scores, i)
            dq_ref[at, cut] = (nn(pair, keys[i]) * HEAD ** (-0.5)).astype(bf16)
            dk = tn(pair, q_ref[at, cut]) * HEAD ** (-0.5)
            dk_ref[at, cut] = jnp.where(left_lanes, dk[:slots], dk[slots:]).astype(bf16)

    pages_of(rows, slots, one_page)
    vec_ref[0:1, :] = column_sum(dq_ref[...])
    vec_ref[1:2, :] = column_sum(dv_ref[...])
    if cross:
        wait_inputs()
    grads[0] = tn(src_ref[...], dq_ref[...]).astype(bf16)
    grads[1] = tn(oth_ref[...], dk_ref[...]).astype(bf16)
    grads[2] = tn(oth_ref[...], dv_ref[...]).astype(bf16)
    store_blocks(info_ref[1], grads, keep_ref, send_ref, out_sem)()


def scores_back(grid, cross, slots, info, counts, grad, saved, inputs, weights):
    rows, width = grad.shape
    full = pltpu.VMEM((rows, width), bf16)
    blocks = (4, width, width)
    scratch = [
        pltpu.VMEM(block_shapes(grid, 1, grid.rows, width), bf16),
        pltpu.SemaphoreType.DMA,
        full,
        full,
        pltpu.VMEM(blocks, bf16),
        pltpu.SemaphoreType.DMA((4,)),
    ]
    if cross:
        scratch += [full, full, pltpu.SemaphoreType.DMA((4,))]
    return call(
        functools.partial(scores_back_kernel, grid, cross, slots, len(weights)),
        [((rows, width), bf16)] * 3 + [((8, width), f32)] + [((2,) + blocks[1:], bf16)] * 2,
        [info, counts, grad] + list(saved) + list(inputs) + list(weights),
        [SMEM, SMEM] + [VMEM] * 5 + ([HBM] * 3 if cross else [VMEM]) + [HBM] * len(weights),
        [VMEM] * 4 + [HBM] * 2,
        scratch,
        flops=10 * rows * width * width + 24 * rows * slots * width,
        moved=12 * width * width + rows * width * 20,
    )


def project_back_kernel(grid, cross, held, info_ref, gain_ref, grad_ref, *refs):
    dq_ref, dk_ref, dv_ref = refs[:3]
    refs = refs[3:]
    if cross:
        sources = refs[:held]
        mine_ref, other_ref, far_ref, blocks, sem = refs[held:]
    else:
        sum_ref, sources = refs[0], refs[1 : 1 + held]
        out_ref, vec_ref, blocks, sem = refs[1 + held :]
    load_blocks(grid, info_ref, sources, blocks, sem)()
    half = grad_ref.shape[0] // 2
    mine = grad_ref[...] + nt(dq_ref[...], matrix(blocks[0]))
    other = nt(dk_ref[...], matrix(blocks[1])) + nt(dv_ref[...], matrix(blocks[2]))
    if cross:
        mine_ref[...] = mine[:half]
        other_ref[...] = other[:half]
        far_ref[:half] = other[half:].astype(bf16)
        far_ref[half:] = mine[half:].astype(bf16)
    else:
        vec_ref[...] = jnp.zeros_like(vec_ref)
        out_ref[...] = norm_back_into(vec_ref, sum_ref[...], mine + other, gain_ref[6:7, :])


def project_back(grid, cross, info, gain, grad, parts, sums, weights):
    rows, width = grad.shape
    half = (rows // 2, width)
    if cross:
        outs = [(half, f32), (half, f32), ((rows, width), bf16)]
    else:
        outs = [((rows, width), f32), ((8, width), f32)]
    return call(
        functools.partial(project_back_kernel, grid, cross, len(weights)),
        outs,
        [info, gain, grad] + list(parts) + list(sums) + list(weights),
        [SMEM] + [VMEM] * (5 + len(sums)) + [HBM] * len(weights),
        [VMEM] * len(outs),
        [pltpu.VMEM(block_shapes(grid, 4, grid.rows, width), bf16), pltpu.SemaphoreType.DMA],
        flops=6 * rows * width * width,
        moved=8 * width * width + rows * width * 18,
    )


SPOTS = (
    [(i, 0, 1) for i in range(3)]
    + [(i, 128, 1) for i in range(3)]
    + [(i, 256, 1) for i in range(3)]
    + [(i, 384, 1) for i in range(3)]
    + [(4, 0, 1), (4, 128, 1), (3, 0, 4)]
)
EXTRA = 16


def lay_vectors(cross_bias, self_bias, gains, shifts, out_bias, gate_bias, in_bias, width):
    def at(values, row, lane):
        depth, length = values.shape[1:]
        return jnp.pad(
            values, ((0, 0), (row, EXTRA - row - depth), (lane, width - lane - length))
        )

    gate = jnp.broadcast_to(gate_bias[None, None], (2, 1) + gate_bias.shape)
    return (
        at(cross_bias, 0, 0)
        + at(self_bias, 0, 128)
        + at(gains, 0, 256)
        + at(shifts, 0, 384)
        + at(out_bias[:, None], 4, 0)
        + at(gate, 4, 128)
        + at(in_bias[:, None], 3, 0)
    )


def unlay_kernel(grid, start, info_ref, all_ref, table_ref, wide_ref, held, found, sem):
    copy = pltpu.make_async_copy(all_ref.at[:, :, :, pl.ds(start, EXTRA)], held, sem)
    copy.start()
    copy.wait()
    unused, unused, unused, first_step, second_step = grid.place(info_ref)
    for g in range(4):
        for b in range(2):
            for a in range(2):
                found[4 * g + a * first_step + b * second_step] = held[g, b, a].astype(f32)
    rows = grid.rows
    for p in range(grid.n):
        for i, (row, lane, unused) in enumerate(SPOTS[:-1]):
            table_ref[i : i + 1, p * rows : (p + 1) * rows] = found[p, row : row + 1, lane : lane + rows]
        row, lane, length = SPOTS[-1]
        wide_ref[0:1, p * length * rows : (p + 1) * length * rows] = found[
            p, row : row + 1, lane : lane + length * rows
        ]


def unlay_vectors(grid, info, pieces, start):
    width = pieces[0].shape[-1]
    rows = grid.rows
    if len(pieces[0].shape) == 3:
        found = extra_rows(grid, info, pieces, start, EXTRA).astype(f32)
        parts = [
            found[:, row, lane : lane + length * rows].reshape(-1) for row, lane, length in SPOTS
        ]
        table = jnp.pad(jnp.stack(parts[:-1]), ((0, 2), (0, 0)))
        return table, jnp.pad(parts[-1][None], ((0, 7), (0, 0)))
    return call(
        functools.partial(unlay_kernel, grid, start),
        [((16, width), f32), ((8, 4 * width), f32)],
        [info, pieces[0]],
        [SMEM, HBM],
        [VMEM, VMEM],
        [
            pltpu.VMEM((4, 2, 2, EXTRA, width), bf16),
            pltpu.VMEM((grid.n, EXTRA, width), f32),
            pltpu.SemaphoreType.DMA,
        ],
        room=GLUE_LIMIT,
    )


def relay_kernel(grid, where, *refs):
    out, held = refs[-2:]
    rows = grid.rows
    held[...] = jnp.zeros_like(held)
    for p in range(grid.n):
        for (table, i), (row, lane, length) in zip(where, SPOTS, strict=True):
            size = length * rows
            held[p, row : row + 1, lane : lane + size] = refs[table][i : i + 1, p * size : (p + 1) * size]
    out[...] = held[...].astype(bf16)


def relay_vectors(grid, tables, where):
    width = tables[0].shape[1]
    rows = grid.rows
    if rows % 16:
        out = jnp.zeros((grid.n, EXTRA, width), f32)
        for (table, i), (row, lane, length) in zip(where, SPOTS, strict=True):
            part = tables[table][i].reshape(grid.n, length * rows)
            out = out.at[:, row, lane : lane + length * rows].set(part)
        return out.astype(bf16)
    return call(
        functools.partial(relay_kernel, grid, where),
        [((grid.n, EXTRA, width), bf16)],
        tables,
        [VMEM] * len(tables),
        [VMEM],
        [pltpu.VMEM((grid.n, EXTRA, width), f32)],
        room=GLUE_LIMIT,
    )[0]


def on_device(
    grid,
    language_in,
    vision_in,
    language_count,
    vision_count,
    cross_qkv,
    cross_proj,
    cross_bias,
    norm_gain,
    norm_bias,
    self_qkv,
    self_proj,
    self_bias,
    ffn_in,
    ffn_in_bias,
    ffn_out,
    ffn_out_bias,
    gate_weight,
    gate_bias,
    cotangent,
):
    n = grid.n
    grid.rows = cross_proj.shape[1]
    me = lax.axis_index("dp")
    core = lax.axis_index("rep")
    side = ((me // grid.high) ^ (me // grid.partner)) & 1
    first = side == 0
    info = jnp.stack([side, core, me]).astype(jnp.int32)
    rows, width = cross_proj.shape[1:]
    dim = n * rows
    pages, slots = language_in.shape[:2]
    wide_ok = rows % 16 == 0

    def own(pair):
        return lax.dynamic_index_in_dim(pair, side, 0, keepdims=False)

    def other(pair):
        return lax.dynamic_index_in_dim(pair, 1 - side, 0, keepdims=False)

    vectors = lay_vectors(
        cross_bias, self_bias, norm_gain, norm_bias, ffn_out_bias, gate_bias, ffn_in_bias, width
    )
    groups = [
        [cross_qkv[:, 0], cross_qkv[:, 1], vectors, cross_qkv[:, 2], cross_proj, vectors],
        [self_qkv[:, 0], self_qkv[:, 1], self_qkv[:, 2], self_proj],
        [ffn_in[:, :, i * width : (i + 1) * width] for i in range(4)],
        [ffn_out[:, i * rows : (i + 1) * rows] for i in range(2)]
        + [gate_weight]
        + [ffn_out[:, i * rows : (i + 1) * rows] for i in range(2, 4)]
        + [gate_weight[::-1]],
    ]

    def shards(blocks):
        half = len(blocks) // 2
        parts = [jnp.concatenate(blocks[:half], 1), jnp.concatenate(blocks[half:], 1)]
        mine = lax.dynamic_index_in_dim(jnp.stack(parts), core, 0, keepdims=False)
        return own(mine), other(mine)

    sent = [shards(blocks) for blocks in groups]
    later = [jnp.concatenate([part[k] for part in sent[2:]], 0) for k in range(2)]
    parts = [part[0].shape[0] for part in sent[2:]]
    language = language_in.reshape(pages * slots, width)
    vision = vision_in.reshape(pages * slots, width)
    counts_mine = jnp.stack([language_count, vision_count])
    counts_wide = jnp.pad(counts_mine.astype(bf16), ((0, 14), (0, width - pages)))
    seen = jnp.concatenate([language, vision, counts_wide], 0)

    t1 = all_meet(grid, info, *sent[0])
    u0 = grid.across(sent[1][1], grid.partner)
    t1, u0, later = tie(t1, u0, later)
    t2 = second_hops(grid, grouped(grid, info, t1))
    u1, place_u = meet(grid, info, pair(info, grid.high_bit - 1, sent[1][0], u0)[0])
    later_far = grid.across(later[1], grid.partner)
    t2, u1, later_far, seen = tie(t2, u1, later_far, seen)
    t3 = third_hops(grid, t2)
    u2 = second_hops(grid, place_u(u1))
    w0, x0 = pair(info, grid.high_bit - 1, later[0], later_far, parts)
    w1, place_w = meet(grid, info, w0)
    seen_far = grid.across(seen, grid.partner)
    t3, u2, w1, seen_far, x0 = tie(t3, u2, w1, seen_far, x0)
    cross_w = whole(grid, info, t3, rows, 2)
    table, ffn_in_shift = unlay_vectors(grid, info, cross_w if len(t3) == 4 else t3, 2 * rows)
    counts_far = seen_far[2 * pages * slots :, :pages][:2].astype(jnp.int32)
    counts = jnp.concatenate([own(counts_mine), own(counts_far)])
    other_counts = jnp.concatenate([other(counts_mine), other(counts_far)])
    inputs = [language, vision, seen_far]
    u3 = third_hops(grid, u2)
    w2 = second_hops(grid, place_w(w1))
    x1, place_x = meet(grid, info, x0)
    cq, ck, cv, co, first_sum, first_norm, first_low = attend(
        grid, True, slots, info, other_counts, table, (0, 1, 2, 6, 9), inputs, cross_w
    )
    first_norm, first_low, u3, w2, x1 = tie(first_norm, first_low, u3, w2, x1)
    self_w = whole(grid, info, u3, rows, 2)
    w3 = third_hops(grid, w2)
    x2 = second_hops(grid, place_x(x1))
    sq, sk, sv, so, second_sum, second_norm, second_low = attend(
        grid,
        False,
        slots,
        info,
        counts,
        table,
        (3, 4, 5, 7, 10),
        [first_norm, first_low],
        self_w,
    )
    second_norm, second_low, w3, x2 = tie(second_norm, second_low, w3, x2)
    in_w = whole(grid, info, w3, rows, 2)
    x3 = third_hops(grid, x2)
    early = ahead(grid, info, x2)
    active, slope = hidden_layer(grid, info, ffn_in_shift, second_low, in_w)
    active, second_norm, x3, early = tie(active, second_norm, x3, early)
    gate_w = out_w = whole(grid, info, x3, rows, 3, early)
    if len(out_w) == 2:
        both = jnp.where(core == 0, jnp.stack(out_w), jnp.stack(out_w[::-1]))[:, :2]
        both = both.reshape(4, n, rows, width).transpose(1, 0, 2, 3)
        out_w = [both.reshape(4 * dim, width)]
    third_sum, third_own, third_send = branch_layer(
        grid, info, table, active, second_norm, out_w
    )
    third_far = grid.across(third_send, grid.partner)
    cotangent_rows = cotangent.reshape(pages * slots, width)
    united, grad_third_own, grad_third_send, grad_gate_shift, gate_keep, gate_send = gate_layer(
        grid, info, table, third_own, third_far, cotangent_rows, gate_w
    )

    def by_piece(values):
        return values.reshape(values.shape[0], n, rows, width)

    gate_keep, gate_send = by_piece(gate_keep), by_piece(gate_send)
    gate_got = grid.swap_cores(gate_send)
    grad_third_far = grid.across(grad_third_send, grid.partner)
    gate = first_returns(grid, info, gate_keep, gate_got)
    gate[0], grad_third_far = tie(gate[0], grad_third_far)
    grad_third_sum, grad_branch_low, vec_third, *out_grads = branch_back(
        grid, info, table, third_sum, grad_third_own, grad_third_far, active, rows
    )
    if len(out_grads) == 1:
        by_core = out_grads[0].reshape(n, 2, 2, rows, width).transpose(1, 2, 0, 3, 4)
        out_grads = [
            lax.dynamic_index_in_dim(by_core, c, 0, keepdims=False) for c in (core, 1 - core)
        ]
    out_keep, out_send = out_grads
    gate, grad_branch_low, out_keep, out_send = tie(gate, grad_branch_low, out_keep, out_send)
    out_got = grid.swap_cores(out_send)
    grad_hidden, vec_hidden, in_keep, in_send = hidden_back(
        grid, info, grad_branch_low, slope, second_low, out_w
    )
    out_got, grad_hidden, in_keep, in_send = tie(out_got, grad_hidden, in_keep, in_send)
    in_keep, in_send = by_piece(in_keep), by_piece(in_send)
    in_got = grid.swap_cores(in_send)
    outs = first_returns(grid, info, out_keep, out_got)
    grad_second_sum, vec_second = second_back(
        grid, info, table, second_sum, grad_third_sum, grad_hidden, in_w
    )
    in_got, grad_second_sum = tie(in_got, grad_second_sum)
    ins = first_returns(grid, info, in_keep, in_got)
    *self_parts, vec_self, self_keep, self_send = scores_back(
        grid, False, slots, info, counts, grad_second_sum, [sq, sk, sv, so], [first_low], self_w
    )
    outs, self_parts, self_keep, self_send = tie(outs, self_parts, self_keep, self_send)
    self_keep, self_send = by_piece(self_keep), by_piece(self_send)
    self_got = grid.swap_cores(self_send)
    outs = second_returns(grid, info, gate, outs)
    grad_first_sum, vec_first = project_back(
        grid, False, info, table, grad_second_sum, self_parts, [first_sum], self_w
    )
    ins, outs, self_got, grad_first_sum = tie(ins, outs, self_got, grad_first_sum)
    ins = second_returns(grid, info, ins)
    selfs = first_returns(grid, info, self_keep, self_got)
    outs = third_returns(grid, info, outs)
    *cross_parts, vec_cross, cross_keep, cross_send = scores_back(
        grid, True, slots, info, other_counts, grad_first_sum, [cq, ck, cv, co], inputs, cross_w
    )
    selfs, ins, outs, cross_parts, cross_keep, cross_send = tie(
        selfs, ins, outs, cross_parts, cross_keep, cross_send
    )
    cross_keep, cross_send = by_piece(cross_keep), by_piece(cross_send)
    cross_got = grid.swap_cores(cross_send)
    selfs = second_returns(grid, info, selfs)
    ins = third_returns(grid, info, ins)
    tables = [vec_cross, vec_self, vec_first, vec_second, vec_third, grad_gate_shift, vec_hidden]
    where = [(0, 0), (0, 1), (0, 2), (1, 0), (1, 1), (1, 2)]
    where += [(2, 0), (3, 0), (4, 0), (2, 1), (3, 1), (4, 1), (4, 2), (5, 0), (6, 0)]
    grad_vec = relay_vectors(grid, tables, where)
    grad_mine, grad_theirs, outgoing = project_back(
        grid, True, info, table, grad_first_sum, cross_parts, [], cross_w
    )
    cross_got, outgoing, selfs, ins, grad_vec = tie(cross_got, outgoing, selfs, ins, grad_vec)
    crosses = first_returns(grid, info, cross_keep, cross_got, grad_vec)
    incoming = grid.across(outgoing, grid.partner)
    selfs = third_returns(grid, info, selfs)
    crosses, selfs = tie(crosses, selfs)
    crosses = second_returns(grid, info, crosses)
    crosses[0], outs, ins = tie(crosses[0], outs, ins)
    out_done = last_swap(grid, outs)
    in_done = last_swap(grid, ins)

    def sides(near, far):
        return jnp.where(first, jnp.stack([near, far]), jnp.stack([far, near]))

    def finished(done, count, start=0):
        mine, far = [part[:, start * rows : (start + count) * rows] for part in done]
        mine, far = [part.reshape(2, count, rows, width) for part in (mine, far)]
        both = jnp.where(core == 0, jnp.concatenate([mine, far], 1), jnp.concatenate([far, mine], 1))
        return both.astype(f32)

    def by_side(both):
        return jnp.where(first, both, both[::-1])

    def attention_grads(done):
        if rows % 16:
            both = by_side(finished(done, 2))
            return [both[:, 0:3], both[:, 3]]
        layout = (((0, (0,)), (0, (1,))), ((0, (2,)), (1, ())))
        return finish(info, done, layout, rows, [(2, 3, rows, width), (2, rows, width)])

    if rows % 16:
        in_all = by_side(finished(in_done, 2)).transpose(0, 2, 1, 3).reshape(2, rows, 4 * width)
        gate_all = finished(out_done, 1)
        gate_both = sides(gate_all[0, 0] + gate_all[1, 1], gate_all[0, 1] + gate_all[1, 0])
        out_all = by_side(finished(out_done, 2, 1)).reshape(2, 4 * rows, width)
    else:
        every = slice(None)
        cuts = [(0, (every, slice(i * width, (i + 1) * width))) for i in range(4)]
        in_all = finish(info, in_done, (cuts[:2], cuts[2:]), rows, [(2, rows, 4 * width)])[0]
        gate_both = call(
            finish_gate_kernel,
            [((2, rows, width), f32)],
            [info] + list(out_done),
            [SMEM, VMEM, VMEM],
            [VMEM],
            room=GLUE_LIMIT,
        )[0]
        places = [(1, ())] + [(0, (slice(i * rows, (i + 1) * rows),)) for i in range(4)]
        layout = ((places[0], places[1], places[2]), (places[0], places[3], places[4]))
        shapes = [(2, 4 * rows, width), (2, rows, width)]
        out_all = finish(info, out_done, layout, rows, shapes)[0]
    crosses, in_all, out_all, gate_both = tie(crosses, in_all, out_all, gate_both)
    crosses = third_returns(grid, info, crosses)
    selfs, crosses[0], incoming = tie(selfs, crosses[0], incoming)
    self_done = last_swap(grid, selfs)
    page_shape = language_in.shape
    got = incoming.astype(f32)
    grad_mine = grad_mine + got[: pages * slots]
    grad_theirs = grad_theirs + got[pages * slots :]
    grad_language = jnp.where(first, grad_mine, grad_theirs).astype(bf16).reshape(page_shape)
    grad_vision = jnp.where(first, grad_theirs, grad_mine).astype(bf16).reshape(page_shape)

    self_qkv_grad, self_proj_grad = attention_grads(self_done)
    crosses, self_qkv_grad, self_proj_grad, grad_language, grad_vision = tie(
        crosses, self_qkv_grad, self_proj_grad, grad_language, grad_vision
    )
    cross_done = last_swap(grid, crosses)
    cross_qkv_grad, cross_proj_grad = attention_grads(cross_done)
    vec_sum = (cross_done[0].astype(f32) + cross_done[1].astype(f32))[:, 2 * rows :]
    vec_both = by_side(vec_sum)
    gate_vec = vec_sum[0, 4, 128 : 128 + rows] + vec_sum[1, 4, 128 : 128 + rows]
    return (
        united.reshape(page_shape),
        grad_language,
        grad_vision,
        cross_qkv_grad,
        cross_proj_grad,
        vec_both[:, 0:3, :rows],
        vec_both[:, 0:3, 256 : 256 + rows],
        vec_both[:, 0:3, 384 : 384 + rows],
        self_qkv_grad,
        self_proj_grad,
        vec_both[:, 0:3, 128 : 128 + rows],
        in_all,
        vec_both[:, 3, : 4 * rows],
        out_all,
        vec_both[:, 4, :rows],
        gate_both,
        gate_vec,
    )


def solution(mesh):
    whole = P(("dp", "rep"), None, None)
    weights = (
        P(None, None, "dp", None),
        P(None, "dp", None),
        P(None, None, "dp"),
        P(None, None, "dp"),
        P(None, None, "dp"),
        P(None, None, "dp", None),
        P(None, "dp", None),
        P(None, None, "dp"),
        P(None, "dp", None),
        P(None, "dp"),
        P(None, "dp", None),
        P(None, "dp"),
        P(None, "dp", None),
        P("dp"),
    )
    return jax.shard_map(
        functools.partial(on_device, Grid(mesh)),
        mesh=mesh,
        in_specs=(whole, whole, P(("dp", "rep")), P(("dp", "rep"))) + weights + (whole,),
        out_specs=(whole, whole, whole) + weights,
        check_vma=False,
    )
```
